32 devices in a mesh: dp: 8 (over z, x), mp: 4 (over y, core).
Axes of the slice: x: 2, y: 2, z: 4, core: 2. Of those that a mesh axis runs over, the one named last changes fastest.
Arguments:
- tokens: bfloat16 [16, 1024, 1024], P('dp', 'mp'), may hold values from -6 to 6
- out_cot: float32 [16, 1024, 1024], P('dp', 'mp'), may hold values from -6 to 6
- cls_offset: int32 [16, 4], P('dp'), may hold values from 0 to 255
- w_qkv: float32 [1024, 3, 1024], P('dp', None, 'mp'), may hold values from -0.1875 to 0.1875
- w_out: float32 [1024, 1024], P('dp', 'mp'), may hold values from -3.5 to 3.5
- w_one: float32 [1024, 4096], P('dp', 'mp'), may hold values from -0.1875 to 0.1875
- w_two: float32 [1024, 4096], P('dp', 'mp'), may hold values from -0.16875 to 0.16875
- vectors: float32 [12, 1024], replicated, may hold values from -1 to 4
- m_qkv: float32 [1024, 3, 1024], P('dp', None, 'mp'), may hold values from -1.25 to 1.25
- v_qkv: float32 [1024, 3, 1024], P('dp', None, 'mp'), may hold values from 0.000589824 to 0.002359296
- m_out: float32 [1024, 1024], P('dp', 'mp'), may hold values from -0.5 to 0.5
- v_out: float32 [1024, 1024], P('dp', 'mp'), may hold values from 7.3728e-05 to 0.000294912
- m_one: float32 [1024, 4096], P('dp', 'mp'), may hold values from -1.25 to 1.25
- v_one: float32 [1024, 4096], P('dp', 'mp'), may hold values from 0.000589824 to 0.002359296
- m_two: float32 [1024, 4096], P('dp', 'mp'), may hold values from -1.25 to 1.25
- v_two: float32 [1024, 4096], P('dp', 'mp'), may hold values from 0.000589824 to 0.002359296
- m_vec: float32 [12, 1024], replicated, may hold values from -5 to 5
- v_vec: float32 [12, 1024], replicated, may hold values from 0.0098304 to 0.0393216
Outputs:
- pooled: float32 [16, 1024], P('dp', 'mp')
- input_grad: float32 [16, 1024, 1024], P('dp', 'mp')
- grad_norm: float32 [], replicated
- qkv_new: float32 [1024, 3, 1024], P('dp', None, 'mp')
- qkv_first: float32 [1024, 3, 1024], P('dp', None, 'mp')
- qkv_second: float32 [1024, 3, 1024], P('dp', None, 'mp')
- out_new: float32 [1024, 1024], P('dp', 'mp')
- out_first: float32 [1024, 1024], P('dp', 'mp')
- out_second: float32 [1024, 1024], P('dp', 'mp')
- one_new: float32 [1024, 4096], P('dp', 'mp')
- one_first: float32 [1024, 4096], P('dp', 'mp')
- one_second: float32 [1024, 4096], P('dp', 'mp')
- two_new: float32 [1024, 4096], P('dp', 'mp')
- two_first: float32 [1024, 4096], P('dp', 'mp')
- two_second: float32 [1024, 4096], P('dp', 'mp')
- vec_new: float32 [12, 1024], replicated
- vec_first: float32 [12, 1024], replicated
- vec_second: float32 [12, 1024], replicated
The draws below stay inside these ranges and needn't reach their ends.
All inputs are finite; a program needn't handle non-finite values.
Results may differ from the reference program's by a relative error of at most 0.015.
The reference program's roundings to bfloat16 on the way count: a program that leaves them out, or rounds other values in their place, can miss the bound.
Values may be sent and summed in bfloat16 or wider, within the bound.
A program may use at most 128 MiB of HBM per device.

```python
import math
from functools import partial
import jax
import jax.numpy as jnp
from jax import lax

D = 1024
H = 16
HD = 64
FF = 4096
DOC_LEN = 1024
CLS_GAP = 256
STEP = 10
NCLS = 4
VROWS = 12
DOCS = 16
TOKENS = 16384


def draw_vectors(key, part):
    key = jax.random.fold_in(key, 5)
    bias_key, jitter_key = jax.random.split(key, 2)
    position_ramp = jnp.arange(D, dtype=jnp.float32) / (D - 1)
    row_ids = jnp.arange(VROWS)[:, None]
    biases = jnp.clip(0.2 * jax.random.normal(bias_key, (VROWS, D)), -1.0, 1.0)
    rising = 0.6 * jnp.power(3.0, position_ramp)
    jitter = jnp.exp(jax.random.uniform(jitter_key, (VROWS, D), minval=-0.22, maxval=0.22))
    gains = rising[None, :] * jitter
    is_gain = (row_ids == 3) | (row_ids == 6)
    return jnp.where(is_gain, gains, biases).astype(jnp.float32)


def draw_w_two(key, part):
    key = jax.random.fold_in(key, 17)
    unit_ramp = jnp.arange(FF, dtype=jnp.float32) / (FF - 1)
    base_draw = jnp.clip(jax.random.normal(key, (D, FF)), -6.0, 6.0)
    rising = 0.6 * jnp.power(3.0, unit_ramp)
    return (base_draw * rising[None, :] * FF ** (-0.5)).astype(jnp.float32)


def with_ends(array, rng, low, largest):
    longest = array.shape.index(max(array.shape))
    spots = []
    for shift in (0, 1):
        where = [jax.random.randint(jax.random.fold_in(rng, axis), (), 0, length) for axis, length in enumerate(array.shape)]
        where[longest] = (where[longest] + shift) % array.shape[longest]
        spots.append(tuple(where))
    return array.at[spots[0]].set(low).at[spots[1]].set(largest)


def block_scale(rng, dims, pieces, low, high):
    def one(position, blocks):
        steps = jax.random.uniform(jax.random.fold_in(jax.random.fold_in(rng, 6), position), (blocks,), jnp.float32, low / len(pieces), high / len(pieces))
        return jnp.repeat(jnp.exp(steps), dims[position] // blocks).reshape((-1,) + (1,) * (len(dims) - position - 1))

    level = one(*pieces[0])
    for cut in pieces[1:]:
        level = level * one(*cut)
    return level


def scatter_about(stream_key, dims, spread, bound, shards=(), kind=jnp.bfloat16):
    gain = block_scale(stream_key, dims, shards, -0.22, 0.18) if shards else 1.0
    result = jax.random.normal(stream_key, dims, jnp.float32) * spread * gain
    return jnp.minimum(jnp.maximum(result, -bound), bound).astype(kind)


def setup_inputs(seed: int = 0) -> dict:
    splits = jax.random.split(jax.random.key(seed), 19)
    tokens = scatter_about(splits[0], (DOCS, DOC_LEN, D), 1.0, 6.0, ((0, 8), (1, 4)))
    out_cot = scatter_about(splits[1], (DOCS, DOC_LEN, D), 1.0, 6.0, ((0, 8), (1, 4)), jnp.float32)
    cls_offset = with_ends(jax.random.randint(splits[2], (DOCS, NCLS), 0, CLS_GAP), jax.random.fold_in(splits[2], 1), 0, CLS_GAP - 1).astype(jnp.int32)
    w_qkv = scatter_about(splits[3], (D, 3, D), D ** -0.5, 0.1875, ((0, 8), (2, 4)), jnp.float32)
    w_out = scatter_about(splits[4], (D, D), (max(1, 3 * D // DOC_LEN)) ** -0.5, 3.5, ((0, 8), (1, 4)), jnp.float32)
    w_one = scatter_about(splits[5], (D, FF), D ** -0.5, 0.1875, ((0, 8), (1, 4)), jnp.float32)
    w_two = draw_w_two(jax.random.fold_in(splits[18], 71), 0)
    vectors = draw_vectors(jax.random.fold_in(splits[18], 71), 0)
    m_qkv = scatter_about(splits[8], (D, 3, D), (0.0007 * TOKENS ** 0.5), 1.25, ((0, 8), (2, 4)), jnp.float32)
    v_qkv = jnp.clip(jnp.exp(math.log(0.002359296) - 1.3862944 * jax.random.uniform(splits[9], (D, 3, D), jnp.float32) ** block_scale(splits[9], (D, 3, D), ((0, 8), (2, 4)), -0.2, 0.2)), 0.000589824, 0.002359296)
    m_out = scatter_about(splits[10], (D, D), (0.00028 * TOKENS ** 0.5), 0.5, ((0, 8), (1, 4)), jnp.float32)
    v_out = jnp.clip(jnp.exp(math.log(0.000294912) - 1.3862944 * jax.random.uniform(splits[11], (D, D), jnp.float32) ** block_scale(splits[11], (D, D), ((0, 8), (1, 4)), -0.2, 0.2)), 7.372799882432446e-05, 0.000294912)
    m_one = scatter_about(splits[12], (D, FF), (0.0007 * TOKENS ** 0.5), 1.25, ((0, 8), (1, 4)), jnp.float32)
    v_one = jnp.clip(jnp.exp(math.log(0.002359296) - 1.3862944 * jax.random.uniform(splits[13], (D, FF), jnp.float32) ** block_scale(splits[13], (D, FF), ((0, 8), (1, 4)), -0.2, 0.2)), 0.000589824, 0.002359296)
    m_two = scatter_about(splits[14], (D, FF), (0.0007 * TOKENS ** 0.5), 1.25, ((0, 8), (1, 4)), jnp.float32)
    v_two = jnp.clip(jnp.exp(math.log(0.002359296) - 1.3862944 * jax.random.uniform(splits[15], (D, FF), jnp.float32) ** block_scale(splits[15], (D, FF), ((0, 8), (1, 4)), -0.2, 0.2)), 0.000589824, 0.002359296)
    m_vec = scatter_about(splits[16], (VROWS, D), (0.0028 * TOKENS ** 0.5), 5.0, (), jnp.float32)
    v_vec = jnp.clip(jnp.exp(jax.random.uniform(splits[17], (VROWS, D), jnp.float32, math.log(0.0098304), math.log(0.0393216))), 0.0098304, 0.0393216)
    return dict(tokens=tokens, out_cot=out_cot, cls_offset=cls_offset, w_qkv=w_qkv, w_out=w_out, w_one=w_one, w_two=w_two, vectors=vectors, m_qkv=m_qkv, v_qkv=v_qkv, m_out=m_out, v_out=v_out, m_one=m_one, v_one=v_one, m_two=m_two, v_two=v_two, m_vec=m_vec, v_vec=v_vec)


@jax.custom_vjp
def low(v):
    return lax.optimization_barrier(v.astype(jnp.bfloat16)).astype(jnp.float32)

@jax.custom_vjp
def low_back(v):
    return v

def low_keep(v):
    return (low(v), None)

def low_pass(kept, grad):
    return (grad,)

def back_keep(v):
    return (v, None)

def back_low(kept, grad):
    return (low(grad),)
low.defvjp(low_keep, low_pass)
low_back.defvjp(back_keep, back_low)
norm_eps = 1e-05
beta_one = 0.9
beta_two = 0.999
adam_eps = 1e-08
weight_decay = 0.01
vector_rate = 0.4
highest = lax.Precision.HIGHEST

def layer_norm(values_in, scale_vec, shift_vec):
    row_mean = lax.optimization_barrier(jnp.mean(values_in, axis=-1, keepdims=True))
    centered = values_in - row_mean
    row_var = lax.optimization_barrier(jnp.mean(centered * centered, axis=-1, keepdims=True))
    return centered * lax.rsqrt(row_var + norm_eps) * scale_vec + shift_vec

def clip_limit(params_all, tokens_all):
    return 0.005 * math.sqrt(params_all * tokens_all)

def matrix_rates(model_width, hidden, length):
    out_fan = max(1, 3 * model_width // length)
    return (1.5 / math.sqrt(model_width), 1.5 / math.sqrt(out_fan), 1.5 / math.sqrt(model_width), 1.5 / math.sqrt(hidden))

def adam_update(parameter, gradient, first_old, second_old, step_rate, decay_rate):
    first_new = beta_one * first_old + (1.0 - beta_one) * gradient
    second_new = beta_two * second_old + (1.0 - beta_two) * gradient * gradient
    first_hat = first_new / (1.0 - beta_one ** STEP)
    second_hat = second_new / (1.0 - beta_two ** STEP)
    updated = parameter - step_rate * (first_hat / (jnp.sqrt(second_hat) + adam_eps) + decay_rate * parameter)
    return (updated, first_new, second_new)

def attend_block(key_heads, value_heads, query_block):
    scores = jnp.einsum('qhd,khd->hqk', query_block, key_heads, precision=highest) * HD ** (-0.5)
    scores = low_back(scores)
    shares = low(jax.nn.softmax(scores, axis=-1))
    return jnp.einsum('hqk,khd->qhd', shares, value_heads, precision=highest)

def one_document(weights, vectors, doc_rows):
    full_qkv, full_out, full_one, full_two = weights
    doc_length = doc_rows.shape[0]
    block_rows = min(512, doc_length)
    projected = jnp.einsum('te,ecf->tcf', doc_rows, full_qkv, precision=highest)
    queries = low_back(low(projected[:, 0] + vectors[0]))
    keys_all = low_back(low(projected[:, 1]))
    values_all = low_back(low(projected[:, 2] + vectors[1]))
    key_heads = keys_all.reshape(doc_length, H, HD)
    value_heads = values_all.reshape(doc_length, H, HD)
    query_blocks = queries.reshape(doc_length // block_rows, block_rows, H, HD)
    attended = lax.map(jax.checkpoint(partial(attend_block, key_heads, value_heads)), query_blocks)
    attended = low_back(low(attended.reshape(doc_length, D)))
    branch = low_back(jnp.dot(attended, full_out.T, precision=highest, preferred_element_type=jnp.float32))
    y_one = layer_norm(doc_rows + branch + vectors[2], vectors[3], vectors[4])
    bias_ff = vectors[8:].reshape(FF)
    pre_act = low_back(jnp.dot(low(y_one), full_one, precision=highest, preferred_element_type=jnp.float32) + bias_ff)
    hidden = low(jax.nn.gelu(pre_act, approximate=False))
    ffn_out = low_back(jnp.dot(hidden, full_two.T, precision=highest, preferred_element_type=jnp.float32))
    return layer_norm(y_one + ffn_out + vectors[5], vectors[6], vectors[7])

def forward(w_qkv, w_out, w_one, w_two, vectors, inputs):
    weights = (low(w_qkv), low(w_out), low(w_one), low(w_two))
    return lax.map(partial(one_document, weights, vectors), inputs)

def reference(tokens, out_cot, cls_offset, w_qkv, w_out, w_one, w_two, vectors, m_qkv, v_qkv, m_out, v_out, m_one, v_one, m_two, v_two, m_vec, v_vec):
    inputs = tokens.astype(jnp.float32)
    layer_out, pullback = jax.vjp(forward, w_qkv, w_out, w_one, w_two, vectors, inputs)
    g_qkv, g_out, g_one, g_two, g_vec, input_grad = pullback(out_cot.astype(jnp.float32))
    positions = cls_offset + (jnp.arange(NCLS, dtype=jnp.int32) * CLS_GAP)[None, :]
    picked = jax.vmap(lambda doc_out, doc_pos: doc_out[doc_pos])(layer_out, positions)
    pooled = lax.optimization_barrier(jnp.mean(picked, axis=1))
    squares = jnp.sum(g_qkv * g_qkv) + jnp.sum(g_out * g_out) + jnp.sum(g_one * g_one) + jnp.sum(g_two * g_two) + jnp.sum(g_vec * g_vec)
    grad_norm = jnp.sqrt(squares)
    factor = jnp.minimum(1.0, clip_limit(4 * D * D + 2 * D * FF, TOKENS) / (grad_norm + 1e-06))
    rates = matrix_rates(D, FF, DOC_LEN)
    qkv_new, qkv_first, qkv_second = adam_update(w_qkv, g_qkv * factor, m_qkv, v_qkv, rates[0], weight_decay)
    out_new, out_first, out_second = adam_update(w_out, g_out * factor, m_out, v_out, rates[1], weight_decay)
    one_new, one_first, one_second = adam_update(w_one, g_one * factor, m_one, v_one, rates[2], weight_decay)
    two_new, two_first, two_second = adam_update(w_two, g_two * factor, m_two, v_two, rates[3], weight_decay)
    vec_new, vec_first, vec_second = adam_update(vectors, g_vec * factor, m_vec, v_vec, vector_rate, 0.0)
    return (pooled, input_grad, grad_norm, qkv_new, qkv_first, qkv_second, out_new, out_first, out_second, one_new, one_first, one_second, two_new, two_first, two_second, vec_new, vec_first, vec_second)
```

```python
from functools import partial
import math

import jax
import jax.numpy as jnp
from jax import lax
from jax.experimental import pallas as pl
from jax.experimental.pallas import tpu as pltpu
from jax.sharding import PartitionSpec as P

D = 1024
HD = 64
FF = 4096
DOC_LEN = 1024
CLS_GAP = 256
STEP = 10

MESH = pl.DeviceIdType.MESH
ANY = pl.BlockSpec(memory_space=pl.ANY)
VMEM = pl.BlockSpec(memory_space=pltpu.VMEM)
DMA = pltpu.SemaphoreType.DMA
f32 = jnp.float32
bf16 = jnp.bfloat16

norm_eps = 1e-05
beta_one = 0.9
beta_two = 0.999
adam_eps = 1e-08
weight_decay = 0.01
vector_rate = 0.4
highest = lax.Precision.HIGHEST
contract_last = (((1,), (1,)), ((), ()))
contract_first = (((0,), (0,)), ((), ()))


def layer_norm(values_in, scale_vec, shift_vec):
    row_mean = jnp.mean(values_in, axis=-1, keepdims=True)
    centered = values_in - row_mean
    row_var = jnp.mean(centered * centered, axis=-1, keepdims=True)
    return centered * lax.rsqrt(row_var + norm_eps) * scale_vec + shift_vec


def clip_limit(params_all, tokens_all):
    return 0.005 * math.sqrt(params_all * tokens_all)


def matrix_rates(model_width, hidden, length):
    out_fan = max(1, 3 * model_width // length)
    return (
        1.5 / math.sqrt(model_width),
        1.5 / math.sqrt(out_fan),
        1.5 / math.sqrt(model_width),
        1.5 / math.sqrt(hidden),
    )


def adam_update(parameter, gradient, first_old, second_old, step_rate, decay_rate):
    first_new = beta_one * first_old + (1.0 - beta_one) * gradient
    second_new = beta_two * second_old + (1.0 - beta_two) * gradient * gradient
    first_hat = first_new / (1.0 - beta_one**STEP)
    second_hat = second_new / (1.0 - beta_two**STEP)
    updated = parameter - step_rate * (
        first_hat / (jnp.sqrt(second_hat) + adam_eps) + decay_rate * parameter
    )
    return (updated, first_new, second_new)


class Place:
    def __init__(self):
        dp, mp = lax.axis_index("dp"), lax.axis_index("mp")
        self.z, self.x = dp // 2, dp % 2
        self.y, self.k = mp // 2, mp % 2

    def near(self, axis):
        z, x, y, k = self.z, self.x, self.y, self.k
        if axis == "x":
            x = 1 - x
        elif axis == "y":
            y = 1 - y
        else:
            k = 1 - k
        return (z * 2 + x, y * 2 + k)

    def along(self, j, nz):
        return ((self.z + j) % nz * 2 + self.x, self.y * 2 + self.k)


def greet(place, nz, axes="xyk"):
    barrier = pltpu.get_barrier_semaphore()
    for axis in axes:
        pl.semaphore_signal(barrier, inc=1, device_id=place.near(axis), device_id_type=MESH)
    if nz > 1:

        def one(j, carry):
            pl.semaphore_signal(barrier, inc=1, device_id=place.along(j, nz), device_id_type=MESH)
            return carry

        lax.fori_loop(1, nz, one, 0)
    pl.semaphore_wait(barrier, len(axes) + nz - 1)


def remote(src, dst, send, recv, where):
    return pltpu.make_async_remote_copy(
        src_ref=src, dst_ref=dst, send_sem=send, recv_sem=recv, device_id=where, device_id_type=MESH
    )


def each(start, stop, body):
    def one(j, carry):
        body(j)
        return carry

    lax.fori_loop(start, stop, one, 0)


class Gather:
    def __init__(self, place, own, full, c0, cols, sems, c):
        self.p, self.own, self.full = place, own, full
        self.nz = full.shape[1]
        half = cols // 2
        self.all, self.a, self.b = pl.ds(c0, cols), pl.ds(c0, half), pl.ds(c0 + half, half)
        self.sems, self.c = sems, c

    def piece(self, y, z, x, cols):
        return self.full.at[y, z, x, :, cols]

    def sem(self, kind, j):
        return self.sems.at[0, kind, self.c, j], self.sems.at[1, kind, self.c, j]

    def to(self, kind, j, src, dst, where):
        return remote(src, dst, *self.sem(kind, j), where)

    def along_z(self, j):
        p = self.p
        return self.to(
            0, j, self.own.at[:, self.all], self.piece(p.y, p.z, p.x, self.all), p.along(j, self.nz)
        )

    def own_xy(self, kind):
        p = self.p
        return self.to(
            kind,
            0,
            self.own.at[:, self.all],
            self.piece(p.y, p.z, p.x, self.all),
            p.near("x" if kind == 1 else "y"),
        )

    def pass_xy(self, kind, j):
        p = self.p
        ref = self.piece(p.y, (p.z + self.nz - j) % self.nz, p.x, self.all)
        return self.to(kind, j, ref, ref, p.near("x" if kind == 1 else "y"))

    def pass_half(self, kind, j):
        p = self.p
        z = (p.z + self.nz - j) % self.nz
        if kind == 3:
            ref = self.piece(p.y, z, 1 - p.x, self.a)
            return self.to(3, j, ref, ref, p.near("y"))
        ref = self.piece(1 - p.y, z, p.x, self.b)
        return self.to(4, j, ref, ref, p.near("x"))

    def stage(self, s):
        nz = self.nz
        if s == 0:
            each(1, nz, lambda j: self.along_z(j).start())
            self.own_xy(1).start()
            self.own_xy(2).start()
        elif s == 1:

            def one(j):
                self.along_z(j).wait()
                self.pass_xy(1, j).start()
                self.pass_xy(2, j).start()

            each(1, nz, one)
        elif s == 2:

            def first(kind):
                self.own_xy(kind).wait()
                self.pass_half(kind + 2, 0).start()

            first(1)
            first(2)

            def two(j):
                for kind in (1, 2):
                    self.pass_xy(kind, j).wait()
                    self.pass_half(kind + 2, j).start()

            each(1, nz, two)
        else:

            def three(j):
                self.pass_half(3, j).wait()
                self.pass_half(4, j).wait()

            each(0, nz, three)


def pump(chunks, stages, t):
    for s in reversed(range(stages)):
        if 0 <= t - s < len(chunks):
            chunks[t - s].stage(s)


def gather_kernel(
    x_ref, cot_ref, wq, wo, w1, w2, x_all, cot_half, gq, go, g1, g2, sems, side, local_sem
):
    p = Place()
    nz = gq.shape[1]
    greet(p, nz)
    swap_x = remote(x_ref.at[1 - p.y], x_all.at[p.y, p.k], side.at[0, 0], side.at[1, 0], p.near("y"))
    swap_x.start()
    keep_x = pltpu.make_async_copy(x_ref.at[p.y], x_all.at[p.y, p.k], local_sem.at[0])
    keep_x.start()
    give_x = remote(x_ref.at[p.y], x_all.at[p.y, p.k], side.at[0, 1], side.at[1, 1], p.near("k"))
    give_x.start()
    keeps = []
    for i, (own, full) in enumerate(((wq, gq), (wo, go), (w1, g1), (w2, g2))):
        keeps.append(
            pltpu.make_async_copy(own, full.at[p.y, p.z, p.x], local_sem.at[1 + i])
        )
        keeps[-1].start()
    chunks = []
    for own, full, width in ((wq, gq, 768), (wo, go, 256), (w1, g1, 512), (w2, g2, 512)):
        for c0 in range(0, own.shape[1], width):
            chunks.append(Gather(p, own, full, c0, width, sems, len(chunks)))
    swap_cot = remote(cot_ref, cot_half, side.at[0, 2], side.at[1, 2], p.near("y"))
    for t in range(len(chunks) + 3):
        pump(chunks, 4, t)
        if t == 1:
            swap_x.wait()
            ref = x_all.at[1 - p.y, p.k]
            pass_x = remote(ref, ref, side.at[0, 3], side.at[1, 3], p.near("k"))
            pass_x.start()
            swap_cot.start()
    keep_x.wait()
    give_x.wait()
    pass_x.wait()
    swap_cot.wait()
    for keep in keeps:
        keep.wait()


def gather_all(x_loc, cot_send, shards):
    nz = lax.axis_size("dp") // 2
    rows = shards[0].shape[0]
    shapes = [
        jax.ShapeDtypeStruct((2, 2) + x_loc.shape[1:], bf16),
        jax.ShapeDtypeStruct(cot_send.shape, bf16),
    ] + [jax.ShapeDtypeStruct((2, nz, 2, rows, s.shape[1]), bf16) for s in shards]
    n_chunks = 6
    return pl.pallas_call(
        gather_kernel,
        out_shape=shapes,
        in_specs=[ANY] * 6,
        out_specs=[ANY] * 6,
        scratch_shapes=[
            DMA((2, 5, n_chunks, nz)),
            DMA((2, 4)),
            DMA((5,)),
        ],
        compiler_params=pltpu.CompilerParams(collective_id=0, has_side_effects=True),
        name="gather_weights",
    )(x_loc, cot_send, *shards)


class Reduce:
    def __init__(self, place, part, total, buffers, c0, cols, sems, c):
        self.p, self.part, self.total = place, part, total
        self.ra, self.rb, self.rx, self.ry, self.rz = buffers
        self.nz = part.shape[1]
        self.half = cols // 2
        self.all, self.a, self.b = pl.ds(c0, cols), pl.ds(c0, self.half), pl.ds(c0 + self.half, self.half)
        self.in_a = pl.ds(c0 // 2, self.half)
        self.sems, self.c = sems, c

    def to(self, kind, j, src, dst, where):
        return remote(src, dst, self.sems.at[0, kind, self.c, j], self.sems.at[1, kind, self.c, j], where)

    def send_half(self, kind, z):
        p = self.p
        if kind == 0:
            return self.to(
                0, z, self.part.at[1 - p.y, z, 1 - p.x, :, self.a], self.ra.at[z, :, self.in_a], p.near("y")
            )
        return self.to(
            1, z, self.part.at[1 - p.y, z, 1 - p.x, :, self.b], self.rb.at[z, :, self.in_a], p.near("x")
        )

    def send_sum(self, kind, z):
        p = self.p
        if kind == 2:
            return self.to(2, z, self.ra.at[z, :, self.in_a], self.rx.at[z, :, self.a], p.near("x"))
        return self.to(3, z, self.rb.at[z, :, self.in_a], self.ry.at[z, :, self.b], p.near("y"))

    def send_own(self, kind, z):
        p = self.p
        if kind == 5:
            return self.to(
                5, z, self.part.at[p.y, z, 1 - p.x, :, self.b], self.rx.at[z, :, self.b], p.near("x")
            )
        return self.to(
            6, z, self.part.at[1 - p.y, z, p.x, :, self.a], self.ry.at[z, :, self.a], p.near("y")
        )

    def send_z(self, j):
        p = self.p
        z = (p.z + j) % self.nz
        return self.to(4, j, self.rx.at[z, :, self.all], self.rz.at[j, :, self.all], p.along(j, self.nz))

    def stage(self, s):
        p, nz = self.p, self.nz
        if s == 0:

            def zero(z):
                self.send_half(0, z).start()
                self.send_half(1, z).start()

            each(0, nz, zero)
        elif s == 1:

            def one(z):
                self.send_half(0, z).wait()
                into = self.ra.at[z, :, self.in_a]
                into[...] = (
                    into[...].astype(f32) + self.part[p.y, z, 1 - p.x, :, self.a].astype(f32)
                ).astype(bf16)
                self.send_sum(2, z).start()
                self.send_own(5, z).start()
                self.send_half(1, z).wait()
                into = self.rb.at[z, :, self.in_a]
                into[...] = (
                    into[...].astype(f32) + self.part[1 - p.y, z, p.x, :, self.b].astype(f32)
                ).astype(bf16)
                self.send_sum(3, z).start()
                self.send_own(6, z).start()

            each(0, nz, one)
        elif s == 2:

            def add(z):
                self.send_sum(2, z).wait()
                self.send_own(5, z).wait()
                self.send_sum(3, z).wait()
                self.send_own(6, z).wait()
                return (
                    self.part[p.y, z, p.x, :, self.all].astype(f32)
                    + self.rx[z, :, self.all].astype(f32)
                    + self.ry[z, :, self.all].astype(f32)
                )

            def two(j):
                z = (p.z + j) % nz
                self.rx[z, :, self.all] = add(z).astype(bf16)
                self.send_z(j).start()

            each(1, nz, two)
            self.total[:, self.all] = add(p.z)
        else:

            def three(j):
                self.send_z(j).wait()
                self.total[:, self.all] += self.rz[j, :, self.all].astype(f32)

            each(1, nz, three)


def reduce_kernel(widths, *refs):
    n = len(widths)
    parts, totals = refs[:n], refs[n : 2 * n]
    buffers = [refs[2 * n + 5 * i : 2 * n + 5 * i + 5] for i in range(n)]
    (sems,) = refs[7 * n :]
    p = Place()
    greet(p, parts[0].shape[1], "xy")
    chunks = []
    for i, width in enumerate(widths):
        for c0 in range(0, parts[i].shape[-1], width):
            chunks.append(Reduce(p, parts[i], totals[i], buffers[i], c0, width, sems, len(chunks)))
    for t in range(len(chunks) + 3):
        pump(chunks, 4, t)


def reduce_all(parts, widths):
    nz, rows = parts[0].shape[1], parts[0].shape[3]
    scratch = []
    for part in parts:
        cols = part.shape[-1]
        scratch += [pltpu.VMEM((nz, rows, cols // 2), bf16)] * 2
        scratch += [pltpu.VMEM((nz, rows, cols), bf16)] * 3
    n_chunks = sum(part.shape[-1] // width for part, width in zip(parts, widths))
    return pl.pallas_call(
        partial(reduce_kernel, widths),
        out_shape=[jax.ShapeDtypeStruct((rows, part.shape[-1]), f32) for part in parts],
        in_specs=[VMEM] * len(parts),
        out_specs=[VMEM] * len(parts),
        scratch_shapes=scratch + [DMA((2, 7, n_chunks, nz))],
        compiler_params=pltpu.CompilerParams(
            collective_id=1, has_side_effects=True, vmem_limit_bytes=56 * 2**20
        ),
        name="reduce_gradients",
    )(*parts)


def swap_kernel(axis, src, dst, sems):
    p = Place()
    greet(p, 1, axis)
    copy = remote(src, dst, sems.at[0], sems.at[1], p.near(axis))
    copy.start()
    copy.wait()


def swap(array, axis, call):
    return pl.pallas_call(
        partial(swap_kernel, axis),
        out_shape=jax.ShapeDtypeStruct(array.shape, array.dtype),
        in_specs=[VMEM],
        out_specs=VMEM,
        scratch_shapes=[DMA((2,))],
        compiler_params=pltpu.CompilerParams(
            collective_id=call, has_side_effects=True, vmem_limit_bytes=32 * 2**20
        ),
        name="swap_" + axis,
    )(array)


def heads_of(columns):
    return columns.reshape(columns.shape[0], -1, HD)


def attend_forward(key_heads, value_heads, query_block):
    scores = jnp.einsum(
        "qhd,khd->hqk", query_block, key_heads, preferred_element_type=jnp.float32
    ) * HD ** (-0.5)
    row_top = jnp.max(scores, axis=-1, keepdims=True)
    raised = jnp.exp(scores - row_top)
    row_total = jnp.sum(raised, axis=-1, keepdims=True)
    shares = (raised / row_total).astype(jnp.bfloat16)
    mixed = jnp.einsum("hqk,khd->qhd", shares, value_heads, preferred_element_type=jnp.float32)
    return (mixed.astype(jnp.bfloat16), (row_top + jnp.log(row_total))[..., 0])


def attend_backward(key_heads, value_heads, carry, block):
    query_block, log_block, grad_block = block
    key_sum, value_sum = carry
    scores = jnp.einsum(
        "qhd,khd->hqk", query_block, key_heads, preferred_element_type=jnp.float32
    ) * HD ** (-0.5)
    shares = jnp.exp(scores - log_block[..., None])
    value_sum = value_sum + jnp.einsum(
        "hqk,qhd->khd", shares.astype(jnp.bfloat16), grad_block, preferred_element_type=jnp.float32
    )
    dshares = jnp.einsum(
        "qhd,khd->hqk", grad_block, value_heads, preferred_element_type=jnp.float32
    )
    dscores = (shares * (dshares - jnp.sum(shares * dshares, axis=-1, keepdims=True))).astype(
        jnp.bfloat16
    )
    query_grad = jnp.einsum(
        "hqk,khd->qhd", dscores, key_heads, preferred_element_type=jnp.float32
    ) * HD ** (-0.5)
    key_sum = key_sum + jnp.einsum(
        "hqk,qhd->khd", dscores, query_block, preferred_element_type=jnp.float32
    ) * HD ** (-0.5)
    return ((key_sum, value_sum), query_grad)


def dot(a, b, dims=(((1,), (0,)), ((), ()))):
    return lax.dot_general(a, b, dims, preferred_element_type=f32)


def local(
    tokens, out_cot, cls_offset, w_qkv, w_out, w_one, w_two, vectors,
    m_qkv, v_qkv, m_out, v_out, m_one, v_one, m_two, v_two, m_vec, v_vec,
):
    rows_dev = tokens.shape[1]
    mp_rank = lax.axis_index("mp")
    y, k = mp_rank // 2, mp_rank % 2
    length = rows_dev * lax.axis_size("mp")
    rows_w = w_qkv.shape[0]
    head_cols = w_qkv.shape[2]
    ff_cols = w_one.shape[1]

    def mine(row, width):
        return [
            lax.dynamic_slice_in_dim(row, (2 * b + k) * width, width) for b in range(2)
        ]

    query_bias = mine(vectors[0], head_cols)
    value_bias = mine(vectors[1], head_cols)
    ff_bias = mine(vectors[8:].reshape(-1), ff_cols)
    shards = (
        w_qkv.astype(bf16).reshape(rows_w, 3 * head_cols),
        w_out.astype(bf16),
        w_one.astype(bf16),
        w_two.astype(bf16),
    )
    cot_own = lax.dynamic_index_in_dim(out_cot, y, 0, keepdims=False)
    cot_send = lax.dynamic_index_in_dim(out_cot, 1 - y, 0, keepdims=False).astype(bf16)
    x_all, cot_other, *full = gather_all(tokens, cot_send, shards)
    full_qkv, full_out, full_one, full_two = [g.reshape(2, D, g.shape[-1]) for g in full]
    x_doc = x_all.reshape(length, D)

    def own_rows(a):
        return lax.dynamic_index_in_dim(a.reshape(2, 2, rows_dev, D), k, 1, keepdims=False)

    def other_rows(a):
        return lax.dynamic_index_in_dim(a.reshape(2, 2, rows_dev, D), 1 - k, 1, keepdims=False)

    def by_y(own, other):
        return jnp.where(y == 0, jnp.stack([own, other]), jnp.stack([other, own]))

    def core_sum(partial_sum, call):
        got = swap(other_rows(partial_sum).astype(bf16), "k", call)
        return own_rows(partial_sum) + got.astype(f32)

    def core_gather(rows, call):
        got = swap(rows, "k", call)
        pair = jnp.where(k == 0, jnp.stack([rows, got], 1), jnp.stack([got, rows], 1))
        return pair.reshape(length, D)

    cot = by_y(cot_own, cot_other.astype(f32))
    x_rows = own_rows(x_doc).astype(f32)

    queries, keys_all, values_all = [], [], []
    for b in range(2):
        projected = dot(x_doc, full_qkv[b])
        queries.append((projected[:, :head_cols] + query_bias[b]).astype(bf16))
        keys_all.append(projected[:, head_cols : 2 * head_cols].astype(bf16))
        values_all.append((projected[:, 2 * head_cols :] + value_bias[b]).astype(bf16))
    queries, keys_all, values_all = [jnp.concatenate(a, 1) for a in (queries, keys_all, values_all)]
    key_heads, value_heads = heads_of(keys_all), heads_of(values_all)
    query_blocks = heads_of(queries).reshape(2, length // 2, -1, HD)
    attended, log_sums = lax.map(partial(attend_forward, key_heads, value_heads), query_blocks)
    attended = attended.reshape(length, 2 * head_cols)
    part_out = sum(
        dot(attended[:, b * head_cols : (b + 1) * head_cols], full_out[b], contract_last)
        for b in range(2)
    )
    z_one = x_rows + core_sum(part_out, 2) + vectors[2]
    y_one, first_back = jax.vjp(layer_norm, z_one, vectors[3], vectors[4])
    normed_all = core_gather(y_one.astype(bf16), 3)
    pre_act = [dot(normed_all, full_one[b]) + ff_bias[b] for b in range(2)]
    hidden = [jax.nn.gelu(u, approximate=False).astype(bf16) for u in pre_act]
    part_two = sum(dot(hidden[b], full_two[b], contract_last) for b in range(2))
    z_two = y_one + core_sum(part_two, 4) + vectors[5]
    layer_out, second_back = jax.vjp(layer_norm, z_two, vectors[6], vectors[7])
    offsets = lax.dynamic_index_in_dim(cls_offset, y, 0, keepdims=False)
    positions = offsets + jnp.arange(offsets.shape[0], dtype=jnp.int32) * CLS_GAP
    row_ids = (
        (2 * jnp.arange(2, dtype=jnp.int32)[:, None] + k) * rows_dev
        + jnp.arange(rows_dev, dtype=jnp.int32)[None, :]
    )
    picks = (
        jnp.sum((positions[:, None, None] == row_ids[None]).astype(f32), axis=0)
        / offsets.shape[0]
    )
    pool_part = jnp.einsum("br,brd->d", picks, layer_out, precision=highest)
    pool_parts = jnp.where(jnp.arange(2)[:, None] == y, pool_part[None], 0.0)
    dz_two, dscale_two, dshift_two = second_back(cot)
    dffn_all = core_gather(dz_two.astype(bf16), 5)
    grad_two = [dot(dffn_all, hidden[b], contract_first) for b in range(2)]
    dpre = []
    for b in range(2):
        dhidden = dot(dffn_all, full_two[b])
        gelu_back = jax.vjp(partial(jax.nn.gelu, approximate=False), pre_act[b])[1]
        dpre.append(gelu_back(dhidden)[0].astype(bf16))
    grad_one = [dot(normed_all, dpre[b], contract_first) for b in range(2)]
    dff_bias = [jnp.sum(d, axis=0, dtype=f32) for d in dpre]
    part_one = sum(dot(dpre[b], full_one[b], contract_last) for b in range(2))
    dz_one, dscale_one, dshift_one = first_back(dz_two + core_sum(part_one, 6))
    dbranch_all = core_gather(dz_one.astype(bf16), 7)
    grad_out = [
        dot(dbranch_all, attended[:, b * head_cols : (b + 1) * head_cols], contract_first)
        for b in range(2)
    ]
    dattended = jnp.concatenate([dot(dbranch_all, full_out[b]).astype(bf16) for b in range(2)], 1)
    grad_blocks = heads_of(dattended).reshape(2, length // 2, -1, HD)
    zero_heads = jnp.zeros(key_heads.shape, f32)
    (key_sum, value_sum), query_grad = lax.scan(
        partial(attend_backward, key_heads, value_heads),
        (zero_heads, zero_heads),
        (query_blocks, log_sums, grad_blocks),
    )
    dparts = [
        a.reshape(length, 2, head_cols).astype(bf16) for a in (query_grad, key_sum, value_sum)
    ]
    dprojected = [jnp.concatenate([a[:, b] for a in dparts], 1) for b in range(2)]
    grad_qkv = [dot(x_doc, dprojected[b], contract_first) for b in range(2)]
    part_x = sum(dot(dprojected[b], full_qkv[b], contract_last) for b in range(2))
    input_rows = dz_one + core_sum(part_x, 8)
    back = swap(
        lax.dynamic_index_in_dim(input_rows, 1 - y, 0, keepdims=False).astype(bf16), "y", 9
    )
    input_grad = by_y(
        lax.dynamic_index_in_dim(input_rows, y, 0, keepdims=False), back.astype(f32)
    )

    def spread(width, blocks):
        row = jnp.zeros((4 * width,), f32)
        for b in range(2):
            row = lax.dynamic_update_slice(row, blocks[b], ((2 * b + k) * width,))
        return row

    head_sums = [jnp.sum(d, axis=0, dtype=f32) for d in dprojected]
    vec_local = jnp.concatenate(
        [
            jnp.stack(
                [
                    spread(head_cols, [h[:head_cols] for h in head_sums]),
                    spread(head_cols, [h[2 * head_cols :] for h in head_sums]),
                    jnp.sum(dz_one, axis=(0, 1)),
                    dscale_one,
                    dshift_one,
                    jnp.sum(dz_two, axis=(0, 1)),
                    dscale_two,
                    dshift_two,
                ]
            ),
            spread(ff_cols, dff_bias).reshape(-1, D),
        ]
    )
    pooled = lax.psum_scatter(pool_parts, "mp", scatter_dimension=1, tiled=True)

    def as_parts(blocks):
        return jnp.stack([b.astype(bf16) for b in blocks]).reshape(
            2, D // rows_w // 2, 2, rows_w, -1
        )

    g_two, g_one, g_out, g_qkv = reduce_all(
        [as_parts(grad_two), as_parts(grad_one), as_parts(grad_out), as_parts(grad_qkv)],
        (512, 512, 256, 768),
    )
    g_qkv = g_qkv.reshape(w_qkv.shape)
    own_squares = (
        jnp.sum(g_qkv * g_qkv)
        + jnp.sum(g_out * g_out)
        + jnp.sum(g_one * g_one)
        + jnp.sum(g_two * g_two)
    )
    g_vec, squares_all = lax.psum((vec_local, own_squares), ("dp", "mp"))
    grad_norm = jnp.sqrt(squares_all + jnp.sum(g_vec * g_vec))
    tokens_all = tokens.shape[0] * length * lax.axis_size("dp")
    factor = jnp.minimum(1.0, clip_limit(4 * D * D + 2 * D * FF, tokens_all) / (grad_norm + 1e-06))
    rates = matrix_rates(D, FF, DOC_LEN)
    return (
        pooled,
        input_grad,
        grad_norm,
        *adam_update(w_qkv, g_qkv * factor, m_qkv, v_qkv, rates[0], weight_decay),
        *adam_update(w_out, g_out * factor, m_out, v_out, rates[1], weight_decay),
        *adam_update(w_one, g_one * factor, m_one, v_one, rates[2], weight_decay),
        *adam_update(w_two, g_two * factor, m_two, v_two, rates[3], weight_decay),
        *adam_update(vectors, g_vec * factor, m_vec, v_vec, vector_rate, 0.0),
    )


def solution(mesh):
    rows, wide, flat, whole = P("dp", "mp", None), P("dp", None, "mp"), P("dp", "mp"), P()
    return jax.shard_map(
        local,
        mesh=mesh,
        in_specs=(rows, rows, P("dp", None), wide, flat, flat, flat, whole)
        + (wide, wide)
        + (flat,) * 6
        + (whole, whole),
        out_specs=(flat, rows, whole) + (wide,) * 3 + (flat,) * 9 + (whole,) * 3,
        check_vma=False,
    )
```

```python
from functools import partial
import math

import jax
import jax.numpy as jnp
from jax import lax
from jax.experimental import pallas as pl
from jax.experimental.pallas import tpu as pltpu
from jax.sharding import PartitionSpec as P

D = 1024
HD = 64
FF = 4096
DOC_LEN = 1024
CLS_GAP = 256
STEP = 10

MESH = pl.DeviceIdType.MESH
ANY = pl.BlockSpec(memory_space=pl.ANY)
VMEM = pl.BlockSpec(memory_space=pltpu.VMEM)
DMA = pltpu.SemaphoreType.DMA
f32 = jnp.float32
bf16 = jnp.bfloat16

norm_eps = 1e-05
beta_one = 0.9
beta_two = 0.999
adam_eps = 1e-08
weight_decay = 0.01
vector_rate = 0.4
contract_last = (((1,), (1,)), ((), ()))


def clip_limit(params_all, tokens_all):
    return 0.005 * math.sqrt(params_all * tokens_all)


def matrix_rates(model_width, hidden, length):
    out_fan = max(1, 3 * model_width // length)
    return (
        1.5 / math.sqrt(model_width),
        1.5 / math.sqrt(out_fan),
        1.5 / math.sqrt(model_width),
        1.5 / math.sqrt(hidden),
    )


def adam_update(parameter, gradient, first_old, second_old, step_rate, decay_rate):
    first_new = beta_one * first_old + (1.0 - beta_one) * gradient
    second_new = beta_two * second_old + (1.0 - beta_two) * gradient * gradient
    first_hat = first_new / (1.0 - beta_one**STEP)
    second_hat = second_new / (1.0 - beta_two**STEP)
    updated = parameter - step_rate * (
        first_hat / (jnp.sqrt(second_hat) + adam_eps) + decay_rate * parameter
    )
    return (updated, first_new, second_new)


class Place:
    def __init__(self):
        dp, mp = lax.axis_index("dp"), lax.axis_index("mp")
        self.z, self.x = dp // 2, dp % 2
        self.y, self.k = mp // 2, mp % 2

    def near(self, axis):
        z, x, y, k = self.z, self.x, self.y, self.k
        if axis == "x":
            x = 1 - x
        elif axis == "y":
            y = 1 - y
        else:
            k = 1 - k
        return (z * 2 + x, y * 2 + k)

    def along(self, j, nz):
        return ((self.z + j) % nz * 2 + self.x, self.y * 2 + self.k)


def greet(place, nz, axes="xyk"):
    barrier = pltpu.get_barrier_semaphore()
    for axis in axes:
        pl.semaphore_signal(barrier, inc=1, device_id=place.near(axis), device_id_type=MESH)
    if nz > 1:

        def one(j, carry):
            pl.semaphore_signal(barrier, inc=1, device_id=place.along(j, nz), device_id_type=MESH)
            return carry

        lax.fori_loop(1, nz, one, 0)
    pl.semaphore_wait(barrier, len(axes) + nz - 1)


def remote(src, dst, send, recv, where):
    return pltpu.make_async_remote_copy(
        src_ref=src, dst_ref=dst, send_sem=send, recv_sem=recv, device_id=where, device_id_type=MESH
    )


def each(start, stop, body):
    def one(j, carry):
        body(j)
        return carry

    lax.fori_loop(start, stop, one, 0)


def dot(a, b, dims=(((1,), (0,)), ((), ()))):
    return lax.dot_general(a, b, dims, preferred_element_type=f32)


class Gather:
    def __init__(self, place, own, full, send, recv):
        self.p, self.own, self.full, self.send, self.recv = place, own, full, send, recv
        self.nz = full.shape[2]

    def to(self, kind, c, j, src, dst, where):
        return remote(src, dst, self.send.at[kind, c % 4, j], self.recv.at[kind, c, j], where)

    def along_z(self, c, j):
        p = self.p
        return self.to(
            0, c, j, self.own.at[c], self.full.at[c, p.y, p.z, p.x], p.along(j, self.nz)
        )

    def pass_xy(self, kind, c, j):
        p = self.p
        there = self.full.at[c, p.y, (p.z + self.nz - j) % self.nz, p.x]
        src = self.own.at[c] if isinstance(j, int) and j == 0 else there
        return self.to(kind, c, j, src, there, p.near("x" if kind == 1 else "y"))

    def pass_half(self, kind, c, j):
        p = self.p
        z = (p.z + self.nz - j) % self.nz
        if kind == 3:
            ref = self.full.at[c, p.y, z, 1 - p.x, :, pl.ds(0, 128)]
            return self.to(3, c, j, ref, ref, p.near("y"))
        ref = self.full.at[c, 1 - p.y, z, p.x, :, pl.ds(128, 128)]
        return self.to(4, c, j, ref, ref, p.near("x"))

    def stage(self, s, c):
        nz = self.nz
        if s == 0:
            self.pass_xy(1, c, 0).start()
            self.pass_xy(2, c, 0).start()
            each(1, nz, lambda j: self.along_z(c, j).start())
        elif s == 1:

            def one(j):
                self.along_z(c, j).wait()
                self.pass_xy(1, c, j).start()
                self.pass_xy(2, c, j).start()

            each(1, nz, one)
        elif s == 2:
            for kind in (1, 2):
                self.pass_xy(kind, c, 0).wait()
                self.pass_half(kind + 2, c, 0).start()

            def two(j):
                for kind in (1, 2):
                    self.pass_xy(kind, c, j).wait()
                    self.pass_half(kind + 2, c, j).start()

            each(1, nz, two)
        else:

            def three(j):
                self.pass_half(3, c, j).wait()
                self.pass_half(4, c, j).wait()

            each(0, nz, three)


class Pump:
    def __init__(self, mover, chunks):
        self.mover, self.chunks, self.t = mover, chunks, 0

    def step(self):
        for s in (3, 2, 1, 0):
            if 0 <= self.t - s < self.chunks:
                self.mover.stage(s, self.t - s)
        self.t += 1


class Saver:
    def __init__(self, sems):
        self.sems, self.list = sems, []

    def start(self, src, dst):
        copy = pltpu.make_async_copy(src, dst, self.sems.at[len(self.list)])
        copy.start()
        self.list.append(copy)
        return copy

    def wait(self, *done):
        for copy in self.list:
            if all(copy is not other for other in done):
                copy.wait()


def turn(block):
    return block.astype(f32).T.astype(bf16)


def normalize(z):
    centered = z - jnp.mean(z, axis=-1, keepdims=True)
    r = lax.rsqrt(jnp.mean(centered * centered, axis=-1, keepdims=True) + norm_eps)
    return centered * r, r


def norm_backward(cot, xh, r, gain):
    e = cot * gain
    return r * (
        e - jnp.mean(e, axis=-1, keepdims=True) - xh * jnp.mean(e * xh, axis=-1, keepdims=True)
    )


def head_mask(h, dim, shape):
    lane = lax.broadcasted_iota(jnp.int32, shape, dim)
    return (lane // HD) == h


def keep_head(block, h, dim):
    return jnp.where(head_mask(h, dim, block.shape), block, jnp.zeros_like(block))


def col_sum(a):
    return jnp.sum(a, axis=0, keepdims=True)


FWD_SAVES = 40


def forward_kernel(
    x_ref, cot_ref, cot_send, shard, vec, qb, vb, b1, picks,
    w_all, q_o, k_o, v_o, kt_o, xt_o, o_o, l_o, yt_o, g_o, gp_o, xh_o, df_o, dft_o, dz_o,
    r_o, small,
    x_v, w_v, q_s, k_s, v_s, kt_s, vt_s, o_s, l_s, xt_s, y_s, yt_s, g_s, gp_s, acc, y1_s, xh_s,
    sb, rb, cot_v, cot_r,
    send, recv, side, save_sems, load_sems,
):
    p = Place()
    nz = w_all.shape[2]
    length = xt_s.shape[1]
    blk_rows = x_v.shape[1]
    greet(p, nz)
    gather = Gather(p, shard, w_all, send, recv)
    pump = Pump(gather, w_all.shape[0])
    saver = Saver(save_sems)
    n_side = [0]

    def beside(src, dst, axis):
        i = n_side[0]
        n_side[0] += 1
        copy = remote(src, dst, side.at[0, i], side.at[1, i], p.near(axis))
        copy.start()
        return copy

    def own(s):
        return (p.y if s == 0 else 1 - p.y) * 2 + p.k

    def other(s):
        return (p.y if s == 0 else 1 - p.y) * 2 + 1 - p.k

    loads = {}

    def load(c):
        loads[c] = pltpu.make_async_copy(w_all.at[c], w_v.at[c], load_sems.at[c])
        loads[c].start()

    def weight(c, b):
        return w_v[c, b].reshape(-1, 256)

    def rows_of(i, n):
        return pl.ds(pl.multiple_of(i * n, n), n)

    mine = x_v.at[own(0)]
    swap_x = beside(x_ref.at[1 - p.y], mine, "y")
    keep_x = saver.start(x_ref.at[p.y], mine)
    give_x = beside(x_ref.at[p.y], mine, "k")
    keep_cot = saver.start(cot_ref.at[p.y], cot_v)
    keep_w = saver.start(shard, w_all.at[:, p.y, p.z, p.x])
    pump.step()
    pump.step()
    swap_x.wait()
    pass_x = beside(x_v.at[own(1)], x_v.at[own(1)], "k")
    pump.step()
    swap_cot = beside(cot_send, cot_r, "y")
    keep_x.wait()
    keep_w.wait()
    give_x.wait()
    pass_x.wait()
    half_rows = 2 * blk_rows

    def project(j):
        for b in range(2):
            w = weight(j, b)

            def tile(i):
                rows = rows_of(i, half_rows)
                x = x_v[pl.ds(2 * i, 2)].reshape(half_rows, -1)
                got = dot(x, w)
                if j == 0:
                    got = got + qb[b]
                elif j == 2:
                    got = got + vb[b]
                got = got.astype(bf16)
                if j == 0:
                    got = got * bf16(0.125)
                dst = (q_s, k_s, v_s)[j]
                dst[2 * b, rows, :] = got[:, :128]
                dst[2 * b + 1, rows, :] = got[:, 128:]
                if j > 0:
                    turned = turn(got)
                    dst = (None, kt_s, vt_s)[j]
                    dst[2 * b, :, rows] = turned[:128]
                    dst[2 * b + 1, :, rows] = turned[128:]

            each(0, 2, tile)

    def flip(i):
        for s in range(4):
            cols = pl.ds(s * 256, 256)
            xt_s[cols, rows_of(i, blk_rows)] = turn(x_v[i, :, cols])

    each(0, 4, flip)
    save_xt = saver.start(xt_s, xt_o)
    pump.step()
    load(0)
    pump.step()
    load(1)
    loads[0].wait()
    project(0)
    pump.step()
    load(2)
    loads[1].wait()
    project(1)
    pump.step()
    load(3)
    loads[2].wait()
    project(2)

    q_tile = 256

    def attend(pair):
        b, lanes = pair // 2, pl.ds(pair % 2 * 128, 128)

        def tile(i):
            rows = rows_of(i, q_tile)
            q2, k2, vt2 = q_s[pair, rows, :], k_s[pair], vt_s[pair]
            mixed = None
            for h in range(2):
                scores = dot(k2, keep_head(q2, h, 1), contract_last)
                top = jnp.max(scores, axis=0, keepdims=True)
                raised = jnp.exp(scores - top)
                total = col_sum(raised)
                shares = (raised * (1.0 / total)).astype(bf16)
                l_s[2 * pair + h, :, rows] = top + jnp.log(total)
                one = dot(keep_head(vt2, h, 0), shares)
                mixed = one if mixed is None else mixed + one
            o_s[b, rows, lanes] = mixed.T.astype(bf16)

        each(0, length // q_tile, tile)

    for pair in range(4):
        attend(pair)
        pump.step()
        load(4 + pair)
    for src, dst in ((q_s, q_o), (k_s, k_o), (v_s, v_o), (kt_s, kt_o), (o_s, o_o), (l_s, l_o)):
        saver.start(src, dst)

    loads[3].wait()

    def out_rows(blk):
        rows = rows_of(blk, blk_rows)
        acc[blk] = dot(o_s[0, rows, :], weight(3, 0), contract_last) + dot(
            o_s[1, rows, :], weight(3, 1), contract_last
        )

    def give_half(call, compute):
        sent = []
        for s in range(2):
            compute(other(s))
            sb[call, s] = acc[other(s)].astype(bf16)
            sent.append(beside(sb.at[call, s], rb.at[call, s], "k"))
        for s in range(2):
            compute(own(s))
        return sent

    sent = give_half(0, out_rows)
    shared = []
    for s in range(2):
        sent[s].wait()
        z = x_v[own(s)].astype(f32) + (acc[own(s)] + rb[0, s].astype(f32)) + vec[2:3, :]
        xh, r = normalize(z)
        xh_s[s] = xh
        r_o[s] = r
        y1 = xh * vec[3:4, :] + vec[4:5, :]
        y1_s[s] = y1
        y_s[own(s)] = y1.astype(bf16)
        shared.append(beside(y_s.at[own(s)], y_s.at[own(s)], "k"))
    saver.start(xh_s, xh_o)
    for copy in shared:
        copy.wait()

    def flip_y(i):
        for s in range(4):
            cols = pl.ds(s * 256, 256)
            yt_s[cols, rows_of(i, blk_rows)] = turn(y_s[i, :, cols])

    each(0, 4, flip_y)
    saver.start(yt_s, yt_o)

    def ffn_up(c):
        for b in range(2):
            w = weight(4 + c, b)

            def tile(i):
                rows = rows_of(i, half_rows)
                u = dot(y_s[pl.ds(2 * i, 2)].reshape(half_rows, -1), w) + b1[2 * c + b]
                share = 0.5 * (1.0 + lax.erf(u * 0.7071067811865476))
                g_s[2 * c + b, rows, :] = (u * share).astype(bf16)
                gp_s[2 * c + b, rows, :] = share + u * (
                    jnp.exp(-0.5 * (u * u)) * 0.3989422804014327
                )

            each(0, 2, tile)
        saver.start(g_s.at[2 * c : 2 * c + 2], g_o.at[2 * c : 2 * c + 2])
        saver.start(gp_s.at[2 * c : 2 * c + 2], gp_o.at[2 * c : 2 * c + 2])

    def down_rows(c, blk):
        rows = rows_of(blk, blk_rows)
        got = dot(g_s[2 * c, rows, :], weight(8 + c, 0), contract_last) + dot(
            g_s[2 * c + 1, rows, :], weight(8 + c, 1), contract_last
        )
        acc[blk] = got if c == 0 else acc[blk] + got

    for c in range(4):
        loads[4 + c].wait()
        ffn_up(c)
        pump.step()
        load(8 + c)
    for c in range(3):
        loads[8 + c].wait()
        each(0, 4, partial(down_rows, c))
    loads[11].wait()
    keep_cot.wait()
    swap_cot.wait()
    save_xt.wait()
    sent = give_half(1, partial(down_rows, 3))
    shared = []
    totals = [0.0, 0.0, 0.0, 0.0]
    for s in range(2):
        sent[s].wait()
        z = y1_s[s] + (acc[own(s)] + rb[1, s].astype(f32)) + vec[5:6, :]
        xh, r = normalize(z)
        cot = cot_v[...] if s == 0 else cot_r[...].astype(f32)
        dz = norm_backward(cot, xh, r, vec[6:7, :])
        df = dz.astype(bf16)
        x_v[own(s)] = df
        shared.append(beside(x_v.at[own(s)], x_v.at[own(s)], "k"))
        xt_s[:, rows_of(own(s), blk_rows)] = turn(df)
        cols = xt_s.at[:, rows_of(own(s), blk_rows)]
        shared.append(beside(cols, cols, "k"))
        y1_s[s] = dz
        out = xh * vec[6:7, :] + vec[7:8, :]
        for i, term in enumerate((dz, cot * xh, cot, picks[s] * out)):
            totals[i] = totals[i] + col_sum(term)
    for i in range(4):
        small[i : i + 1, :] = totals[i]
    saver.start(y1_s, dz_o)
    for copy in shared:
        copy.wait()
    saver.start(x_v, df_o)
    saver.start(xt_s, dft_o)
    saver.wait(keep_x, keep_w, keep_cot, save_xt)


def forward(x_loc, cot, cot_send, shard, vec, qb, vb, b1, picks):
    nz = lax.axis_size("dp") // 2
    n_chunks, rows = shard.shape[:2]
    blk = x_loc.shape[1]
    length = 4 * blk
    full = (n_chunks, 2, nz, 2, rows, 256)
    sd = jax.ShapeDtypeStruct
    outs = [
        sd(full, bf16),
        sd((4, length, 128), bf16),
        sd((4, length, 128), bf16),
        sd((4, length, 128), bf16),
        sd((4, 128, length), bf16),
        sd((D, length), bf16),
        sd((2, length, 256), bf16),
        sd((8, 1, length), f32),
        sd((D, length), bf16),
        sd((8, length, 256), bf16),
        sd((8, length, 256), f32),
        sd((2, blk, D), f32),
        sd((4, blk, D), bf16),
        sd((D, length), bf16),
        sd((2, blk, D), f32),
        sd((2, blk, 1), f32),
        sd((8, D), f32),
    ]
    V = pltpu.VMEM
    scratch = [
        V((4, blk, D), bf16), V(full, bf16),
        V((4, length, 128), bf16), V((4, length, 128), bf16), V((4, length, 128), bf16),
        V((4, 128, length), bf16), V((4, 128, length), bf16),
        V((2, length, 256), bf16), V((8, 1, length), f32),
        V((D, length), bf16), V((4, blk, D), bf16), V((D, length), bf16),
        V((8, length, 256), bf16), V((8, length, 256), f32),
        V((4, blk, D), f32), V((2, blk, D), f32), V((2, blk, D), f32),
        V((2, 2, blk, D), bf16), V((2, 2, blk, D), bf16),
        V((blk, D), f32), V((blk, D), bf16),
        DMA((5, 4, nz)), DMA((5, n_chunks, nz)), DMA((2, 16)), DMA((FWD_SAVES,)), DMA((n_chunks,)),
    ]
    return pl.pallas_call(
        forward_kernel,
        out_shape=outs,
        in_specs=[ANY] * 4 + [VMEM] * 5,
        out_specs=[ANY] * 15 + [VMEM] * 2,
        scratch_shapes=scratch,
        compiler_params=pltpu.CompilerParams(
            collective_id=0, has_side_effects=True, vmem_limit_bytes=62 * 2**20
        ),
        name="forward",
    )(x_loc, cot, cot_send, shard, vec, qb, vb, b1, picks)


class Reduce:
    def __init__(self, place, part, total, order, ra, rb, rx, ry, rz, send, recv):
        self.p, self.part, self.total, self.order = place, part, total, order
        self.ra, self.rb, self.rx, self.ry, self.rz = ra, rb, rx, ry, rz
        self.send, self.recv = send, recv
        self.nz = part.shape[2]

    def to(self, kind, r, j, src, dst, where):
        return remote(src, dst, self.send.at[kind, r % 4, j], self.recv.at[kind, r % 4, j], where)

    def copy(self, kind, r, z):
        p, a, b = self.p, pl.ds(0, 128), pl.ds(128, 128)
        part, slot = self.part.at[r % 3], r % 4
        if kind == 0:
            src, dst, axis = part.at[1 - p.y, z, 1 - p.x, :, a], self.ra.at[slot, z], "y"
        elif kind == 1:
            src, dst, axis = part.at[1 - p.y, z, 1 - p.x, :, b], self.rb.at[slot, z], "x"
        elif kind == 2:
            src, dst, axis = self.ra.at[slot, z], self.rx.at[slot, z, :, a], "x"
        elif kind == 3:
            src, dst, axis = self.rb.at[slot, z], self.ry.at[slot, z, :, b], "y"
        elif kind == 5:
            src, dst, axis = part.at[p.y, z, 1 - p.x, :, b], self.rx.at[slot, z, :, b], "x"
        else:
            src, dst, axis = part.at[1 - p.y, z, p.x, :, a], self.ry.at[slot, z, :, a], "y"
        return self.to(kind, r, z, src, dst, p.near(axis))

    def send_z(self, r, j):
        p = self.p
        z = (p.z + j) % self.nz
        return self.to(4, r, j, self.rx.at[r % 4, z], self.rz.at[r % 4, j], p.along(j, self.nz))

    def stage(self, s, r):
        p, nz, slot = self.p, self.nz, r % 4
        part, chunk = self.part.at[r % 3], self.order[r]
        if s == 0:

            def zero(z):
                self.copy(0, r, z).start()
                self.copy(1, r, z).start()

            each(0, nz, zero)
        elif s == 1:

            def one(z):
                self.copy(0, r, z).wait()
                self.copy(1, r, z).wait()
                self.ra[slot, z] = (
                    self.ra[slot, z].astype(f32) + part[p.y, z, 1 - p.x, :, 0:128].astype(f32)
                ).astype(bf16)
                self.rb[slot, z] = (
                    self.rb[slot, z].astype(f32) + part[1 - p.y, z, p.x, :, 128:256].astype(f32)
                ).astype(bf16)
                for kind in (2, 3, 5, 6):
                    self.copy(kind, r, z).start()

            each(0, nz, one)
        elif s == 2:

            def add(z):
                for kind in (2, 3, 5, 6):
                    self.copy(kind, r, z).wait()
                return (
                    part[p.y, z, p.x].astype(f32)
                    + self.rx[slot, z].astype(f32)
                    + self.ry[slot, z].astype(f32)
                )

            def two(j):
                z = (p.z + j) % nz
                self.rx[slot, z] = add(z).astype(bf16)
                self.send_z(r, j).start()

            each(1, nz, two)
            self.total[chunk] = add(p.z)
        else:

            def three(j):
                self.send_z(r, j).wait()
                self.total[chunk] += self.rz[slot, j].astype(f32)

            each(1, nz, three)


def backward_kernel(
    w_all, q_i, k_i, v_i, kt_i, xt_i, o_i, l_i, yt_i, g_i, gp_i, xh_i, df_i, dft_i, dz_i,
    r1, small, vec,
    in_own, in_other,
    total, vec_sum, pools, squares,
    w_v, g_s, gp_v, df_s, dft_s, du_s, dp_s, t_s, acc, xh_s, dz_s, o_s, kt_s, l_s,
    sb, rb, dk_s, dv_s, db_s, part, ra, rb_r, rx, ry, rz, vs, vr, vz, qs, qr, qz,
    send, recv, side, load_sems, w_sems, z_sems,
):
    p = Place()
    nz = w_all.shape[2]
    length = dft_s.shape[1]
    blk_rows = df_s.shape[1]
    half_rows = 2 * blk_rows

    loader = Saver(load_sems)
    n_side = [0]

    def beside(src, dst, axis):
        i = n_side[0]
        n_side[0] += 1
        copy = remote(src, dst, side.at[0, i], side.at[1, i], p.near(axis))
        copy.start()
        return copy

    def own(s):
        return (p.y if s == 0 else 1 - p.y) * 2 + p.k

    def other(s):
        return (p.y if s == 0 else 1 - p.y) * 2 + 1 - p.k

    def rows_of(i, n):
        return pl.ds(pl.multiple_of(i * n, n), n)

    n_w = [0]

    def load_w(c, slot):
        copy = pltpu.make_async_copy(w_all.at[c], w_v.at[slot], w_sems.at[n_w[0]])
        n_w[0] += 1
        copy.start()
        return copy

    def weight(slot, b):
        return w_v[slot, b].reshape(-1, 256)

    got_dft = loader.start(dft_i, dft_s)
    got_g = [loader.start(g_i.at[2 * c : 2 * c + 2], g_s.at[2 * c : 2 * c + 2]) for c in range(4)]
    got_df = loader.start(df_i, df_s)
    got_w2 = [load_w(8 + c, c) for c in range(4)]
    got_gp = [loader.start(gp_i.at[i], gp_v.at[i]) for i in range(2)]
    got_w1 = [load_w(4 + c, 4 + c) for c in range(4)]
    got_yt = loader.start(yt_i, t_s)
    got_xh = loader.start(xh_i, xh_s)
    got_dz = loader.start(dz_i, dz_s)
    got_o = loader.start(o_i, o_s)
    got_kt = loader.start(kt_i, kt_s)
    got_l = loader.start(l_i, l_s)
    greet(p, nz)
    order = (8, 9, 10, 11, 4, 5, 6, 7, 3, 0, 1, 2)
    reduce = Reduce(p, part, total, order, ra, rb_r, rx, ry, rz, send, recv)
    pump = Pump(reduce, len(order))

    def into_part(r, left, right):
        for b in range(2):

            def tile(i):
                got = dot(left[rows_of(i, half_rows), :], right(b)).astype(bf16)
                part[r % 3, b, pl.ds(i * (nz // 2), nz // 2)] = got.reshape(
                    (nz // 2,) + part.shape[3:]
                )

            each(0, 2, tile)

    def grad_two(c):
        got_g[c].wait()
        into_part(c, dft_s, lambda b: g_s[2 * c + b])

    def grad_pre(c):
        got_w2[c].wait()
        for b in range(2):
            i = 2 * c + b
            got_gp[i].wait()
            w = weight(c, b)
            db_s[i] = jnp.zeros_like(db_s[i])

            def tile(t):
                rows = rows_of(t, half_rows)
                hidden = dot(df_s[pl.ds(2 * t, 2)].reshape(half_rows, -1), w)
                pre = (hidden * gp_v[i % 2, rows, :]).astype(bf16)
                du_s[i, rows, :] = pre
                db_s[i] += col_sum(pre.astype(f32))

            each(0, 2, tile)
            if i + 2 < 8:
                got_gp.append(loader.start(gp_i.at[i + 2], gp_v.at[i % 2]))

    def one_rows(blk):
        rows = rows_of(blk, blk_rows)
        got = None
        for c in range(4):
            for b in range(2):
                term = dot(du_s[2 * c + b, rows, :], weight(4 + c, b), contract_last)
                got = term if got is None else got + term
        acc[blk] = got

    def x_rows(blk):
        rows = rows_of(blk, blk_rows)
        got = None
        for j in range(3):
            for b in range(2):
                term = dot(dp_s[2 * j + b, rows, :], weight(j, b), contract_last)
                got = term if got is None else got + term
        acc[blk] = got

    def give_half(call, compute):
        sent = []
        for s in range(2):
            compute(other(s))
            sb[call, s] = acc[other(s)].astype(bf16)
            sent.append(beside(sb.at[call, s], rb.at[call, s], "k"))
        for s in range(2):
            compute(own(s))
        return sent

    got_dft.wait()
    grad_two(0)
    pump.step()
    grad_two(1)
    got_df.wait()
    grad_pre(0)
    grad_pre(1)
    grad_pre(2)
    pump.step()
    grad_two(2)
    grad_pre(3)
    got_w = [load_w(c, c) for c in range(4)]
    for copy in got_w1:
        copy.wait()
    pump.step()
    grad_two(3)
    lo, hi = pl.ds(0, 128), pl.ds(128, 128)
    got_q = loader.start(q_i, g_s.at[0:4, :, lo])
    got_k = loader.start(k_i, g_s.at[0:4, :, hi])
    got_v = loader.start(v_i, g_s.at[4:8, :, lo])
    sent = give_half(0, one_rows)
    got_xh.wait()
    got_dz.wait()
    shared = []
    sums = [0.0, 0.0, 0.0]
    for s in range(2):
        sent[s].wait()
        dy = dz_s[s] + (acc[own(s)] + rb[0, s].astype(f32))
        xh = xh_s[s]
        dz = norm_backward(dy, xh, r1[s], vec[3:4, :])
        da = dz.astype(bf16)
        df_s[own(s)] = da
        shared.append(beside(df_s.at[own(s)], df_s.at[own(s)], "k"))
        cols = dft_s.at[:, rows_of(own(s), blk_rows)]
        cols[...] = turn(da)
        shared.append(beside(cols, cols, "k"))
        dz_s[s] = dz
        for i, term in enumerate((dz, dy * xh, dy)):
            sums[i] = sums[i] + col_sum(term)
    pump.step()
    got_yt.wait()

    def grad_one(c):
        into_part(4 + c, t_s, lambda b: du_s[2 * c + b])

    grad_one(0)
    pump.step()
    for copy in shared:
        copy.wait()
    got_w[3].wait()
    for b in range(2):
        w = weight(3, b)

        def tile(t):
            rows = rows_of(t, half_rows)
            got = dot(df_s[pl.ds(2 * t, 2)].reshape(half_rows, -1), w).astype(bf16)
            g_s[4 + 2 * b, rows, 128:256] = got[:, :128]
            g_s[5 + 2 * b, rows, 128:256] = got[:, 128:]

        each(0, 2, tile)
    got_q.wait()
    got_k.wait()
    got_v.wait()
    got_kt.wait()
    got_l.wait()

    q_tile = 256
    vs[...] = jnp.zeros_like(vs)
    vs[0, 12:13, :] = small[3:4, :]
    for i in range(3):
        vs[0, 2 + i : 3 + i, :] = sums[i]
        vs[0, 5 + i : 6 + i, :] = small[i : i + 1, :]

    def attend(pair):
        b, lanes = pair // 2, slice(pair % 2 * 128, pair % 2 * 128 + 128)
        dk_s[...] = jnp.zeros_like(dk_s)
        dv_s[...] = jnp.zeros_like(dv_s)

        def tile(i):
            rows = rows_of(i, q_tile)
            q2, do2 = g_s[pair, rows, 0:128], g_s[4 + pair, rows, 128:256]
            k2, v2, kt2 = g_s[pair, :, 128:256], g_s[4 + pair, :, 0:128], kt_s[pair]
            dqt = None
            for h in range(2):
                qh, doh = keep_head(q2, h, 1), keep_head(do2, h, 1)
                scores = dot(k2, qh, contract_last)
                shares = jnp.exp(scores - l_s[2 * pair + h, :, rows])
                dshares = dot(v2, doh, contract_last)
                mean = col_sum(shares * dshares)
                dscores = (shares * (dshares - mean)).astype(bf16)
                dv_s[...] += dot(shares.astype(bf16), doh)
                dk_s[...] += dot(dscores, qh)
                one = dot(keep_head(kt2, h, 0), dscores)
                dqt = one if dqt is None else dqt + one
            dq = (dqt * 0.125).T.astype(bf16)
            dp_s[b, rows, lanes] = dq

        each(0, length // q_tile, tile)
        dp_s[2 + b, :, lanes] = dk_s[...].astype(bf16)
        dp_s[4 + b, :, lanes] = dv_s[...].astype(bf16)
        place = pl.ds(pl.multiple_of((2 * b + p.k) * 256 + pair % 2 * 128, 128), 128)
        vs[0, 0:1, place] = col_sum(dp_s[b, :, lanes].astype(f32))
        vs[0, 1:2, place] = col_sum(dp_s[4 + b, :, lanes].astype(f32))

    for pair in range(4):
        attend(pair)
        if pair < 3:
            grad_one(1 + pair)
        else:
            got_xt = loader.start(xt_i, t_s)
            got_o.wait()
            into_part(8, dft_s, lambda b: o_s[b])
        pump.step()
    for c in range(4):
        for b in range(2):
            vs[0, pl.ds(8 + 2 * b + p.k, 1), c * 256 : c * 256 + 256] = db_s[2 * c + b]
    vec_copy = beside(vs.at[0], vr.at[0], "k")
    got_xt.wait()

    def grad_qkv(j):
        into_part(9 + j, t_s, lambda b: dp_s[2 * j + b])

    grad_qkv(0)
    for c in range(3):
        got_w[c].wait()
    pump.step()
    vec_copy.wait()
    vs[1] = vs[0] + vr[0]
    vec_copy = beside(vs.at[1], vr.at[1], "y")
    grad_qkv(1)
    pump.step()
    vec_copy.wait()
    pools[0:1, :] = vs[1, 12:13, :]
    pools[1:2, :] = vr[1, 12:13, :]
    vs[2] = vs[1] + vr[1]
    vec_copy = beside(vs.at[2], vr.at[2], "x")
    grad_qkv(2)
    pump.step()
    sent = give_half(1, x_rows)
    vec_copy.wait()
    vs[3] = vs[2] + vr[2]

    def along(src, into, base, j):
        return remote(
            src, into.at[p.z], z_sems.at[0, base, j], z_sems.at[1, base, j], p.along(j, nz)
        )

    def from_z(src, into, base, j):
        return remote(
            src,
            into.at[(p.z + nz - j) % nz],
            z_sems.at[0, base, j],
            z_sems.at[1, base, j],
            p.along(j, nz),
        )

    vz[p.z] = vs[3]
    each(1, nz, lambda j: along(vs.at[3], vz, 0, j).start())
    sent[1].wait()
    dz_s[1] += acc[own(1)] + rb[1, 1].astype(f32)
    sb[0, 0] = dz_s[1].astype(bf16)
    swap_in = beside(sb.at[0, 0], in_other, "y")
    sent[0].wait()
    dz_s[0] += acc[own(0)] + rb[1, 0].astype(f32)
    keep_in = loader.start(dz_s.at[0], in_own)
    pump.step()
    each(1, nz, lambda j: from_z(vs.at[3], vz, 0, j).wait())
    vec_sum[...] = vz[0]

    def add_vec(z):
        vec_sum[...] += vz[z]

    each(1, nz, add_vec)
    pump.step()
    swap_in.wait()
    pump.step()

    tile8 = jnp.zeros(qs.shape[1:], f32)
    for c in range(len(order)):
        t = total[c]
        t = jnp.sum((t * t).reshape(-1, 8, 256), axis=0)
        tile8 = tile8 + t[:, :128] + t[:, 128:]
    qs[0] = tile8
    for i, axis in enumerate("kyx"):
        beside(qs.at[i], qr.at[i], axis).wait()
        qs[i + 1] = qs[i] + qr[i]
    qz[p.z] = qs[3]
    each(1, nz, lambda j: along(qs.at[3], qz, 1, j).start())
    each(1, nz, lambda j: from_z(qs.at[3], qz, 1, j).wait())
    squares[...] = qz[0]

    def add_square(z):
        squares[...] += qz[z]

    each(1, nz, add_square)
    keep_in.wait()


def backward(saved, r1, small, vec):
    w_all = saved[0]
    n_chunks, _, nz, _, rows, _ = w_all.shape
    length = saved[5].shape[1]
    blk = length // 4
    sd = jax.ShapeDtypeStruct
    V = pltpu.VMEM
    scratch = [
        V((8,) + w_all.shape[1:], bf16), V((8, length, 256), bf16), V((2, length, 256), f32),
        V((4, blk, D), bf16), V((D, length), bf16), V((8, length, 256), bf16),
        V((6, length, 256), bf16), V((D, length), bf16), V((4, blk, D), f32),
        V((2, blk, D), f32), V((2, blk, D), f32), V((2, length, 256), bf16),
        V((4, 128, length), bf16), V((8, 1, length), f32),
        V((2, 2, blk, D), bf16), V((2, 2, blk, D), bf16),
        V((length, 128), f32), V((length, 128), f32), V((8, 1, 256), f32),
        V((3, 2, nz, 2, rows, 256), bf16),
        V((4, nz, rows, 128), bf16), V((4, nz, rows, 128), bf16),
        V((4, nz, rows, 256), bf16), V((4, nz, rows, 256), bf16), V((4, nz, rows, 256), bf16),
        V((4, 16, D), f32), V((3, 16, D), f32), V((nz, 16, D), f32),
        V((4, 8, 128), f32), V((3, 8, 128), f32), V((nz, 8, 128), f32),
        DMA((7, 4, nz)), DMA((7, 4, nz)), DMA((2, 20)), DMA((32,)), DMA((12,)), DMA((2, 2, nz)),
    ]
    return pl.pallas_call(
        backward_kernel,
        out_shape=[
            sd((blk, D), f32), sd((blk, D), bf16),
            sd((n_chunks, rows, 256), f32), sd((16, D), f32), sd((2, D), f32), sd((8, 128), f32),
        ],
        in_specs=[ANY] * 15 + [VMEM] * 3,
        out_specs=[ANY] * 2 + [VMEM] * 4,
        scratch_shapes=scratch,
        compiler_params=pltpu.CompilerParams(
            collective_id=1, has_side_effects=True, vmem_limit_bytes=63 * 2**20
        ),
        name="backward",
    )(*saved, r1, small, vec)


def local(
    tokens, out_cot, cls_offset, w_qkv, w_out, w_one, w_two, vectors,
    m_qkv, v_qkv, m_out, v_out, m_one, v_one, m_two, v_two, m_vec, v_vec,
):
    rows_dev = tokens.shape[1]
    mp_rank = lax.axis_index("mp")
    y, k = mp_rank // 2, mp_rank % 2
    length = rows_dev * lax.axis_size("mp")
    rows_w = w_qkv.shape[0]
    head_cols = w_qkv.shape[2]
    ff_cols = w_one.shape[1]

    def mine(row, width):
        return [lax.dynamic_slice_in_dim(row, (2 * b + k) * width, width) for b in range(2)]

    query_bias = jnp.stack(mine(vectors[0], head_cols))[:, None]
    value_bias = jnp.stack(mine(vectors[1], head_cols))[:, None]
    ff_bias = jnp.stack(mine(vectors[8:].reshape(-1), ff_cols)).reshape(2, 4, 1, 256)
    ff_bias = ff_bias.swapaxes(0, 1).reshape(8, 1, 256)

    def chunks(w):
        return w.astype(bf16).reshape(rows_w, -1, 256).swapaxes(0, 1)

    shard = jnp.concatenate([chunks(w) for w in (w_qkv, w_out, w_one, w_two)])
    cot_send = lax.dynamic_index_in_dim(out_cot, 1 - y, 0, keepdims=False).astype(bf16)
    offsets = lax.dynamic_index_in_dim(cls_offset, y, 0, keepdims=False)
    positions = offsets + jnp.arange(offsets.shape[0], dtype=jnp.int32) * CLS_GAP
    row_ids = (jnp.stack([y, 1 - y])[:, None] * 2 + k) * rows_dev + jnp.arange(
        rows_dev, dtype=jnp.int32
    )
    picks = (
        jnp.sum((positions[:, None, None] == row_ids[None]).astype(f32), axis=0)
        / offsets.shape[0]
    )[..., None]
    *saved, r1, small = forward(
        tokens, out_cot, cot_send, shard, vectors, query_bias, value_bias, ff_bias, picks
    )
    in_own, in_other, total, vec_sum, pools, squares = backward(saved, r1, small, vectors)

    def by_y(own, other):
        return jnp.where(y == 0, jnp.stack([own, other]), jnp.stack([other, own]))

    input_grad = by_y(in_own, in_other.astype(f32))
    pooled = lax.dynamic_slice_in_dim(by_y(pools[0], pools[1]), mp_rank * 256, 256, 1)

    def shard_of(c0, like):
        n = like.size // (rows_w * 256)
        return total[c0 : c0 + n].swapaxes(0, 1).reshape(like.shape)

    g_qkv, g_out = shard_of(0, w_qkv), shard_of(3, w_out)
    g_one, g_two = shard_of(4, w_one), shard_of(8, w_two)
    g_vec = vec_sum[: vectors.shape[0]]
    grad_norm = jnp.sqrt(jnp.sum(squares) + jnp.sum(g_vec * g_vec))
    tokens_all = tokens.shape[0] * length * lax.axis_size("dp")
    factor = jnp.minimum(1.0, clip_limit(4 * D * D + 2 * D * FF, tokens_all) / (grad_norm + 1e-06))
    rates = matrix_rates(D, FF, DOC_LEN)
    return (
        pooled,
        input_grad,
        grad_norm,
        *adam_update(w_qkv, g_qkv * factor, m_qkv, v_qkv, rates[0], weight_decay),
        *adam_update(w_out, g_out * factor, m_out, v_out, rates[1], weight_decay),
        *adam_update(w_one, g_one * factor, m_one, v_one, rates[2], weight_decay),
        *adam_update(w_two, g_two * factor, m_two, v_two, rates[3], weight_decay),
        *adam_update(vectors, g_vec * factor, m_vec, v_vec, vector_rate, 0.0),
    )


def solution(mesh):
    rows, wide, flat, whole = P("dp", "mp", None), P("dp", None, "mp"), P("dp", "mp"), P()
    return jax.shard_map(
        local,
        mesh=mesh,
        in_specs=(rows, rows, P("dp", None), wide, flat, flat, flat, whole)
        + (wide, wide)
        + (flat,) * 6
        + (whole, whole),
        out_specs=(flat, rows, whole) + (wide,) * 3 + (flat,) * 9 + (whole,) * 3,
        check_vma=False,
    )
```

```python
from functools import partial
import math

import jax
import jax.numpy as jnp
from jax import lax
from jax.experimental import pallas as pl
from jax.experimental.pallas import tpu as pltpu
from jax.sharding import PartitionSpec as P

D = 1024
HD = 64
FF = 4096
DOC_LEN = 1024
CLS_GAP = 256
STEP = 10

MESH = pl.DeviceIdType.MESH
ANY = pl.BlockSpec(memory_space=pl.ANY)
VMEM = pl.BlockSpec(memory_space=pltpu.VMEM)
DMA = pltpu.SemaphoreType.DMA
f32 = jnp.float32
bf16 = jnp.bfloat16

norm_eps = 1e-05
beta_one = 0.9
beta_two = 0.999
adam_eps = 1e-08
weight_decay = 0.01
vector_rate = 0.4
contract_last = (((1,), (1,)), ((), ()))


def clip_limit(params_all, tokens_all):
    return 0.005 * math.sqrt(params_all * tokens_all)


def matrix_rates(model_width, hidden, length):
    out_fan = max(1, 3 * model_width // length)
    return (
        1.5 / math.sqrt(model_width),
        1.5 / math.sqrt(out_fan),
        1.5 / math.sqrt(model_width),
        1.5 / math.sqrt(hidden),
    )


def adam_update(parameter, gradient, first_old, second_old, step_rate, decay_rate):
    first_new = beta_one * first_old + (1.0 - beta_one) * gradient
    second_new = beta_two * second_old + (1.0 - beta_two) * gradient * gradient
    first_hat = first_new / (1.0 - beta_one**STEP)
    second_hat = second_new / (1.0 - beta_two**STEP)
    updated = parameter - step_rate * (
        first_hat / (jnp.sqrt(second_hat) + adam_eps) + decay_rate * parameter
    )
    return (updated, first_new, second_new)


class Place:
    def __init__(self):
        dp, mp = lax.axis_index("dp"), lax.axis_index("mp")
        self.z, self.x = dp // 2, dp % 2
        self.y, self.k = mp // 2, mp % 2

    def near(self, axis):
        z, x, y, k = self.z, self.x, self.y, self.k
        if axis == "x":
            x = 1 - x
        elif axis == "y":
            y = 1 - y
        else:
            k = 1 - k
        return (z * 2 + x, y * 2 + k)

    def along(self, j, nz):
        return ((self.z + j) % nz * 2 + self.x, self.y * 2 + self.k)


def greet(place, nz, axes="xyk"):
    barrier = pltpu.get_barrier_semaphore()
    for axis in axes:
        pl.semaphore_signal(barrier, inc=1, device_id=place.near(axis), device_id_type=MESH)
    if nz > 1:

        def one(j, carry):
            pl.semaphore_signal(barrier, inc=1, device_id=place.along(j, nz), device_id_type=MESH)
            return carry

        lax.fori_loop(1, nz, one, 0)
    pl.semaphore_wait(barrier, len(axes) + nz - 1)


def remote(src, dst, send, recv, where):
    return pltpu.make_async_remote_copy(
        src_ref=src, dst_ref=dst, send_sem=send, recv_sem=recv, device_id=where, device_id_type=MESH
    )


def each(start, stop, body):
    def one(j, carry):
        body(j)
        return carry

    lax.fori_loop(start, stop, one, 0)


def dot(a, b, dims=(((1,), (0,)), ((), ()))):
    return lax.dot_general(a, b, dims, preferred_element_type=f32)


class Gather:
    def __init__(self, place, own, full, send, recv, by_x):
        self.p, self.own, self.full, self.send, self.recv = place, own, full, send, recv
        self.by_x = by_x
        self.nz = full.shape[2]

    def to(self, kind, c, j, src, dst, where):
        slot = c % 4 if c < 10 else c - 6
        return remote(src, dst, self.send.at[kind, slot, j], self.recv.at[kind, c, j], where)

    def along_z(self, c, j):
        p = self.p
        return self.to(
            0, c, j, self.own.at[c], self.full.at[c, p.y, p.z, p.x], p.along(j, self.nz)
        )

    def pass_xy(self, kind, c, j):
        p = self.p
        there = self.full.at[c, p.y, (p.z + self.nz - j) % self.nz, p.x]
        src = self.own.at[c] if isinstance(j, int) and j == 0 else there
        return self.to(kind, c, j, src, there, p.near("x" if kind == 1 else "y"))

    def pass_half(self, kind, c, j):
        p = self.p
        z = (p.z + self.nz - j) % self.nz
        if kind == 3:
            ref = self.full.at[c, p.y, z, 1 - p.x, :, pl.ds(0, 128)]
            return self.to(3, c, j, ref, ref, p.near("y"))
        ref = self.full.at[c, 1 - p.y, z, p.x]
        if c not in self.by_x:
            ref = ref.at[:, pl.ds(128, 128)]
        return self.to(4, c, j, ref, ref, p.near("x"))

    def halves(self, c):
        return (4,) if c in self.by_x else (3, 4)

    def stage(self, s, c):
        nz = self.nz
        if s == 0:
            self.pass_xy(1, c, 0).start()
            self.pass_xy(2, c, 0).start()
            each(1, nz, lambda j: self.along_z(c, j).start())
        elif s == 1:

            def one(j):
                self.along_z(c, j).wait()
                self.pass_xy(1, c, j).start()
                self.pass_xy(2, c, j).start()

            each(1, nz, one)
        elif s == 2:
            def two(j):
                for kind in (2, 1):
                    self.pass_xy(kind, c, j).wait()
                    if kind + 2 in self.halves(c):
                        self.pass_half(kind + 2, c, j).start()

            two(0)

            each(1, nz, two)
        else:

            def three(j):
                for kind in self.halves(c):
                    self.pass_half(kind, c, j).wait()

            each(0, nz, three)


class Far:
    def __init__(self, gather, c, sends, recvs):
        self.g, self.c, self.sends, self.recvs = gather, c, sends, recvs

    def piece(self, i):
        p = self.g.p
        x = 1 - p.x if i in (1, 3) else p.x
        y = 1 - p.y if i in (2, 3) else p.y
        return self.g.full.at[self.c, y, p.z, x]

    def copy(self, i, j):
        g = self.g
        ref = self.piece(i)
        src = g.own.at[self.c] if i == 0 else ref
        return remote(src, ref, self.sends.at[i, j], self.recvs.at[i, j], g.p.along(j, g.nz))

    def step(self, s):
        g, c = self.g, self.c
        if s == 0:
            g.pass_xy(1, c, 0).start()
            g.pass_xy(2, c, 0).start()
        elif s == 1:
            for kind in (1, 2):
                g.pass_xy(kind, c, 0).wait()
                g.pass_half(kind + 2, c, 0).start()
        elif s == 2:
            for kind in (3, 4):
                g.pass_half(kind, c, 0).wait()
        elif s < 7:
            each(1, g.nz, lambda j: self.copy(s - 3, j).start())
        else:

            def last(j):
                for i in range(4):
                    self.copy(i, j).wait()

            each(1, g.nz, last)


class Pump:
    def __init__(self, mover, times, order):
        self.mover, self.times, self.order, self.t = mover, times, order, 0

    def step(self):
        for s in self.order:
            for c, when in enumerate(self.times):
                if when[s] == self.t:
                    self.mover.stage(s, c)
        self.t += 1


class Saver:
    def __init__(self, sems):
        self.sems, self.list = sems, []

    def start(self, src, dst):
        copy = pltpu.make_async_copy(src, dst, self.sems.at[len(self.list)])
        copy.start()
        self.list.append(copy)
        return copy

    def wait(self, *done):
        for copy in self.list:
            if all(copy is not other for other in done):
                copy.wait()


def turn(block):
    return block.astype(f32).T.astype(bf16)


def normalize(z):
    centered = z - jnp.mean(z, axis=-1, keepdims=True)
    r = lax.rsqrt(jnp.mean(centered * centered, axis=-1, keepdims=True) + norm_eps)
    return centered * r, r


def norm_backward(cot, xh, r, gain):
    e = cot * gain
    return r * (
        e - jnp.mean(e, axis=-1, keepdims=True) - xh * jnp.mean(e * xh, axis=-1, keepdims=True)
    )


def head_mask(h, dim, shape):
    lane = lax.broadcasted_iota(jnp.int32, shape, dim)
    return (lane // HD) == h


def keep_head(block, h, dim):
    return jnp.where(head_mask(h, dim, block.shape), block, jnp.zeros_like(block))


def col_sum(a):
    return jnp.sum(a, axis=0, keepdims=True)


FWD_SAVES = 40


def forward_kernel(
    x_ref, cot_ref, cls, wq, wo, w1, w2, vec,
    w_all, q_o, k_o, v_o, kt_o, xt_o, o_o, l_o, yt_o, g_o, gp_o, xh_o, df_o, dft_o, dz_o,
    r_o, small,
    shard, x_v, w_v, q_s, k_s, v_s, kt_s, vt_s, o_s, l_s, xt_s, y_s, yt_s, g_s, gp_s, acc, y1_s,
    xh_s, sb, rb, cot_v, cot_r,
    send, recv, far_send, far_recv, side, save_sems, load_sems,
):
    p = Place()
    nz = w_all.shape[2]
    length = xt_s.shape[1]
    blk_rows = x_v.shape[1]
    saver = Saver(save_sems)
    keep_cot = saver.start(cot_ref.at[p.y], cot_v)
    load_cot = saver.start(cot_ref.at[1 - p.y], y1_s.at[0])
    for j in range(3):
        shard[j] = wq[j].astype(bf16)
    greet(p, nz)
    gather = Gather(p, shard, w_all, send, recv, (0, 1, 5, 6))
    early = [(max(0, c - 1), c + 1, c + 2, c + 3) for c in range(3)]
    later = [(c - 1, c + 1, c + 3, c + 5) for c in range(3, w_all.shape[0] - 2)]
    pump = Pump(gather, early + later, (2, 0, 1, 3))
    far = [Far(gather, 10 + i, far_send.at[i], far_recv.at[i]) for i in range(2)]
    n_side = [0]

    def beside(src, dst, axis):
        i = n_side[0]
        n_side[0] += 1
        copy = remote(src, dst, side.at[0, i], side.at[1, i], p.near(axis))
        copy.start()
        return copy

    def own(s):
        return (p.y if s == 0 else 1 - p.y) * 2 + p.k

    def other(s):
        return (p.y if s == 0 else 1 - p.y) * 2 + 1 - p.k

    loads = {}

    def load(c):
        loads[c] = pltpu.make_async_copy(w_all.at[c], w_v.at[c], load_sems.at[c])
        loads[c].start()

    def weight(c, b):
        return w_v[c, b].reshape(-1, 256)

    def rows_of(i, n):
        return pl.ds(pl.multiple_of(i * n, n), n)

    mine = x_v.at[own(0)]
    swap_x = beside(x_ref.at[1 - p.y], mine, "y")
    keep_x = saver.start(x_ref.at[p.y], mine)
    give_x = beside(x_ref.at[p.y], mine, "k")
    pump.step()
    shard[3] = wo[...].astype(bf16)
    for c in range(4):
        shard[4 + c] = w1[:, c * 256 : c * 256 + 256].astype(bf16)
        shard[8 + c] = w2[:, c * 256 : c * 256 + 256].astype(bf16)
    keep_w = saver.start(shard, w_all.at[:, p.y, p.z, p.x])
    load_cot.wait()
    sb[1, 0] = y1_s[0].astype(bf16)
    pump.step()
    swap_x.wait()
    pass_x = beside(x_v.at[own(1)], x_v.at[own(1)], "k")
    pump.step()
    far[0].step(0)
    far[1].step(0)
    keep_x.wait()
    keep_w.wait()
    give_x.wait()
    pass_x.wait()
    half_rows = 2 * blk_rows

    def project(j):
        for b in range(2):
            w = weight(j, b)

            def tile(i):
                rows = rows_of(i, half_rows)
                x = x_v[pl.ds(2 * i, 2)].reshape(half_rows, -1)
                got = dot(x, w)
                if j != 1:
                    bias = pl.ds(pl.multiple_of((2 * b + p.k) * 256, 256), 256)
                    got = got + vec[j // 2 : j // 2 + 1, bias]
                got = got.astype(bf16)
                if j == 0:
                    got = got * bf16(0.125)
                dst = (q_s, k_s, v_s)[j]
                dst[2 * b, rows, :] = got[:, :128]
                dst[2 * b + 1, rows, :] = got[:, 128:]
                if j > 0:
                    turned = turn(got)
                    dst = (None, kt_s, vt_s)[j]
                    dst[2 * b, :, rows] = turned[:128]
                    dst[2 * b + 1, :, rows] = turned[128:]

            each(0, 2, tile)

    def flip(i):
        for s in range(4):
            cols = pl.ds(s * 256, 256)
            xt_s[cols, rows_of(i, blk_rows)] = turn(x_v[i, :, cols])

    each(0, 4, flip)
    save_xt = saver.start(xt_s, xt_o)
    pump.step()
    load(0)
    far[0].step(1)
    far[1].step(1)
    pump.step()
    load(1)
    far[0].step(2)
    far[1].step(2)
    far[0].step(3)
    loads[0].wait()
    project(0)
    pump.step()
    load(2)
    far[1].step(3)
    loads[1].wait()
    project(1)
    swap_cot = beside(sb.at[1, 0], cot_r, "y")
    pump.step()
    far[0].step(4)
    loads[2].wait()
    project(2)

    q_tile = 256

    def attend(pair):
        b, lanes = pair // 2, pl.ds(pair % 2 * 128, 128)

        def tile(i):
            rows = rows_of(i, q_tile)
            q2, k2, vt2 = q_s[pair, rows, :], k_s[pair], vt_s[pair]
            mixed = None
            for h in range(2):
                scores = dot(k2, keep_head(q2, h, 1), contract_last)
                top = jnp.max(scores, axis=0, keepdims=True)
                raised = jnp.exp(scores - top)
                total = col_sum(raised)
                shares = (raised * (1.0 / total)).astype(bf16)
                l_s[2 * pair + h, :, rows] = top + jnp.log(total)
                one = dot(keep_head(vt2, h, 0), shares)
                mixed = one if mixed is None else mixed + one
            o_s[b, rows, lanes] = mixed.T.astype(bf16)

        each(0, length // q_tile, tile)

    for pair in range(4):
        attend(pair)
        pump.step()
        if pair > 0:
            load(2 + pair)
        far[1 - pair % 2].step(4 + (pair + 1) // 2)
    for src, dst in ((q_s, q_o), (k_s, k_o), (v_s, v_o), (kt_s, kt_o), (o_s, o_o), (l_s, l_o)):
        saver.start(src, dst)

    loads[3].wait()

    def out_rows(blk):
        rows = rows_of(blk, blk_rows)
        acc[blk] = dot(o_s[0, rows, :], weight(3, 0), contract_last) + dot(
            o_s[1, rows, :], weight(3, 1), contract_last
        )

    def give_half(call, compute):
        sent = []
        for s in range(2):
            compute(other(s))
            sb[call, s] = acc[other(s)].astype(bf16)
            sent.append(beside(sb.at[call, s], rb.at[call, s], "k"))
        for s in range(2):
            compute(own(s))
        return sent

    sent = give_half(0, out_rows)
    shared = []
    for s in range(2):
        sent[s].wait()
        z = x_v[own(s)].astype(f32) + (acc[own(s)] + rb[0, s].astype(f32)) + vec[2:3, :]
        xh, r = normalize(z)
        xh_s[s] = xh
        r_o[s] = r
        y1 = xh * vec[3:4, :] + vec[4:5, :]
        y1_s[s] = y1
        y_s[own(s)] = y1.astype(bf16)
        shared.append(beside(y_s.at[own(s)], y_s.at[own(s)], "k"))
    saver.start(xh_s, xh_o)
    for copy in shared:
        copy.wait()

    def flip_y(i):
        for s in range(4):
            cols = pl.ds(s * 256, 256)
            yt_s[cols, rows_of(i, blk_rows)] = turn(y_s[i, :, cols])

    each(0, 4, flip_y)
    saver.start(yt_s, yt_o)

    def ffn_up(c):
        for b in range(2):
            w = weight(4 + c, b)
            bias = vec[pl.ds(8 + 2 * b + p.k, 1), c * 256 : c * 256 + 256]

            def tile(i):
                rows = rows_of(i, half_rows)
                u = dot(y_s[pl.ds(2 * i, 2)].reshape(half_rows, -1), w) + bias
                share = 0.5 * (1.0 + lax.erf(u * 0.7071067811865476))
                g_s[2 * c + b, rows, :] = (u * share).astype(bf16)
                gp_s[2 * c + b, rows, :] = share + u * (
                    jnp.exp(-0.5 * (u * u)) * 0.3989422804014327
                )

            each(0, 2, tile)
        saver.start(g_s.at[2 * c : 2 * c + 2], g_o.at[2 * c : 2 * c + 2])
        saver.start(gp_s.at[2 * c : 2 * c + 2], gp_o.at[2 * c : 2 * c + 2])

    def down_rows(c, blk):
        rows = rows_of(blk, blk_rows)
        got = dot(g_s[2 * c, rows, :], weight(8 + c, 0), contract_last) + dot(
            g_s[2 * c + 1, rows, :], weight(8 + c, 1), contract_last
        )
        acc[blk] = got if c == 0 else acc[blk] + got

    pump.step()
    load(6)
    far[1].step(6)
    loads[4].wait()
    ffn_up(0)
    pump.step()
    load(7)
    loads[5].wait()
    ffn_up(1)
    pump.step()
    load(8)
    loads[6].wait()
    ffn_up(2)
    pump.step()
    load(9)
    far[0].step(7)
    load(10)
    loads[7].wait()
    ffn_up(3)
    far[1].step(7)
    load(11)
    for c in range(3):
        loads[8 + c].wait()
        each(0, 4, partial(down_rows, c))
    loads[11].wait()
    keep_cot.wait()
    swap_cot.wait()
    save_xt.wait()
    sent = give_half(1, partial(down_rows, 3))
    shared = []
    totals = [0.0, 0.0, 0.0, 0.0]
    for s in range(2):
        sent[s].wait()
        z = y1_s[s] + (acc[own(s)] + rb[1, s].astype(f32)) + vec[5:6, :]
        xh, r = normalize(z)
        cot = cot_v[...] if s == 0 else cot_r[...].astype(f32)
        dz = norm_backward(cot, xh, r, vec[6:7, :])
        df = dz.astype(bf16)
        x_v[own(s)] = df
        shared.append(beside(x_v.at[own(s)], x_v.at[own(s)], "k"))
        xt_s[:, rows_of(own(s), blk_rows)] = turn(df)
        cols = xt_s.at[:, rows_of(own(s), blk_rows)]
        shared.append(beside(cols, cols, "k"))
        y1_s[s] = dz
        out = xh * vec[6:7, :] + vec[7:8, :]
        row = lax.broadcasted_iota(jnp.int32, (blk_rows, 1), 0) + own(s) * blk_rows
        hits = [row == cls[p.y, j] + j * CLS_GAP for j in range(cls.shape[1])]
        picks = sum(hit.astype(f32) for hit in hits) / len(hits)
        for i, term in enumerate((dz, cot * xh, cot, picks * out)):
            totals[i] = totals[i] + col_sum(term)
    for i in range(4):
        small[i : i + 1, :] = totals[i]
    saver.start(y1_s, dz_o)
    for copy in shared:
        copy.wait()
    saver.start(x_v, df_o)
    saver.start(xt_s, dft_o)
    saver.wait(keep_x, keep_w, keep_cot, load_cot, save_xt)


def forward(x_loc, cot, cls, w_qkv, w_out, w_one, w_two, vec):
    nz = lax.axis_size("dp") // 2
    n_chunks, rows = 12, w_out.shape[0]
    blk = x_loc.shape[1]
    length = 4 * blk
    full = (n_chunks, 2, nz, 2, rows, 256)
    sd = jax.ShapeDtypeStruct
    outs = [
        sd(full, bf16),
        sd((4, length, 128), bf16),
        sd((4, length, 128), bf16),
        sd((4, length, 128), bf16),
        sd((4, 128, length), bf16),
        sd((D, length), bf16),
        sd((2, length, 256), bf16),
        sd((8, 1, length), f32),
        sd((D, length), bf16),
        sd((8, length, 256), bf16),
        sd((8, length, 256), f32),
        sd((2, blk, D), f32),
        sd((4, blk, D), bf16),
        sd((D, length), bf16),
        sd((2, blk, D), f32),
        sd((2, blk, 1), f32),
        sd((8, D), f32),
    ]
    V = pltpu.VMEM
    scratch = [
        V((n_chunks, rows, 256), bf16), V((4, blk, D), bf16), V(full, bf16),
        V((4, length, 128), bf16), V((4, length, 128), bf16), V((4, length, 128), bf16),
        V((4, 128, length), bf16), V((4, 128, length), bf16),
        V((2, length, 256), bf16), V((8, 1, length), f32),
        V((D, length), bf16), V((4, blk, D), bf16), V((D, length), bf16),
        V((8, length, 256), bf16), V((8, length, 256), f32),
        V((4, blk, D), f32), V((2, blk, D), f32), V((2, blk, D), f32),
        V((2, 2, blk, D), bf16), V((2, 2, blk, D), bf16),
        V((blk, D), f32), V((blk, D), bf16),
        DMA((5, 6, nz)), DMA((5, n_chunks, nz)), DMA((2, 4, nz)), DMA((2, 4, nz)), DMA((2, 16)), DMA((FWD_SAVES,)), DMA((n_chunks,)),
    ]
    return pl.pallas_call(
        forward_kernel,
        out_shape=outs,
        in_specs=[ANY] * 2 + [pl.BlockSpec(memory_space=pltpu.SMEM)] + [VMEM] * 5,
        out_specs=[ANY] * 15 + [VMEM] * 2,
        scratch_shapes=scratch,
        compiler_params=pltpu.CompilerParams(
            collective_id=0, has_side_effects=True, vmem_limit_bytes=62 * 2**20
        ),
        name="forward",
    )(x_loc, cot, cls, w_qkv, w_out, w_one, w_two, vec)


class Reduce:
    def __init__(self, place, part, total, order, ra, rb, rx, ry, rz, send, recv):
        self.p, self.part, self.total, self.order = place, part, total, order
        self.ra, self.rb, self.rx, self.ry, self.rz = ra, rb, rx, ry, rz
        self.send, self.recv = send, recv
        self.nz = part.shape[2]

    def to(self, kind, r, j, src, dst, where):
        return remote(src, dst, self.send.at[kind, r % 4, j], self.recv.at[kind, r % 4, j], where)

    def copy(self, kind, r, z):
        p, a, b = self.p, pl.ds(0, 128), pl.ds(128, 128)
        part, slot = self.part.at[r % 3], r % 4
        if kind == 0:
            src, dst, axis = part.at[1 - p.y, z, 1 - p.x, :, a], self.ra.at[r % 5, z], "y"
        elif kind == 1:
            src, dst, axis = part.at[1 - p.y, z, 1 - p.x, :, b], self.rb.at[r % 5, z], "x"
        elif kind == 2:
            src, dst, axis = self.ra.at[r % 5, z], self.rx.at[slot, z, :, a], "x"
        elif kind == 3:
            src, dst, axis = self.rb.at[r % 5, z], self.ry.at[slot, z, :, b], "y"
        elif kind == 5:
            src, dst, axis = part.at[p.y, z, 1 - p.x, :, b], self.rx.at[slot, z, :, b], "x"
        else:
            src, dst, axis = part.at[1 - p.y, z, p.x, :, a], self.ry.at[slot, z, :, a], "y"
        return self.to(kind, r, z, src, dst, p.near(axis))

    def send_z(self, r, j):
        p = self.p
        z = (p.z + j) % self.nz
        return self.to(4, r, j, self.rx.at[r % 4, z], self.rz.at[r % 4, j], p.along(j, self.nz))

    def stage(self, s, r):
        p, nz, slot = self.p, self.nz, r % 4
        part, chunk = self.part.at[r % 3], self.order[r]
        if s == 0:

            def zero(z):
                self.copy(0, r, z).start()
                self.copy(1, r, z).start()

            each(0, nz, zero)
        elif s == 1:

            def one(z):
                self.copy(0, r, z).wait()
                self.copy(1, r, z).wait()
                self.ra[r % 5, z] = (
                    self.ra[r % 5, z].astype(f32) + part[p.y, z, 1 - p.x, :, 0:128].astype(f32)
                ).astype(bf16)
                self.rb[r % 5, z] = (
                    self.rb[r % 5, z].astype(f32) + part[1 - p.y, z, p.x, :, 128:256].astype(f32)
                ).astype(bf16)
                for kind in (2, 3, 5, 6):
                    self.copy(kind, r, z).start()

            each(0, nz, one)
        elif s == 2:

            def add(z):
                for kind in (2, 3, 5, 6):
                    self.copy(kind, r, z).wait()
                return (
                    part[p.y, z, p.x].astype(f32)
                    + self.rx[slot, z].astype(f32)
                    + self.ry[slot, z].astype(f32)
                )

            def two(j):
                z = (p.z + j) % nz
                self.rx[slot, z] = add(z).astype(bf16)
                self.send_z(r, j).start()

            each(1, nz, two)
            self.total[chunk] = add(p.z)
        else:

            def three(j):
                self.send_z(r, j).wait()
                self.total[chunk] += self.rz[slot, j].astype(f32)

            each(1, nz, three)


def backward_kernel(
    w_all, q_i, k_i, v_i, kt_i, xt_i, o_i, l_i, yt_i, g_i, gp_i, xh_i, df_i, dft_i, dz_i,
    r1, small, vec,
    in_own, in_other,
    total, vec_sum, pools, squares,
    w_v, g_s, gp_v, df_s, dft_s, du_s, dp_s, t_s, acc, xh_s, dz_s, o_s, kt_s, l_s,
    sb, rb, dk_s, dv_s, db_s, part, ra, rb_r, rx, ry, rz, vs, vr, vz, qs, qr, qz,
    send, recv, side, load_sems, w_sems, z_sems,
):
    p = Place()
    nz = w_all.shape[2]
    length = dft_s.shape[1]
    blk_rows = df_s.shape[1]
    half_rows = 2 * blk_rows

    loader = Saver(load_sems)
    n_side = [0]

    def beside(src, dst, axis):
        i = n_side[0]
        n_side[0] += 1
        copy = remote(src, dst, side.at[0, i], side.at[1, i], p.near(axis))
        copy.start()
        return copy

    def own(s):
        return (p.y if s == 0 else 1 - p.y) * 2 + p.k

    def other(s):
        return (p.y if s == 0 else 1 - p.y) * 2 + 1 - p.k

    def rows_of(i, n):
        return pl.ds(pl.multiple_of(i * n, n), n)

    n_w = [0]

    def load_w(c, slot):
        copy = pltpu.make_async_copy(w_all.at[c], w_v.at[slot], w_sems.at[n_w[0]])
        n_w[0] += 1
        copy.start()
        return copy

    def weight(slot, b):
        return w_v[slot, b].reshape(-1, 256)

    got_dft = loader.start(dft_i, dft_s)
    got_g = [loader.start(g_i.at[2 * c : 2 * c + 2], g_s.at[2 * c : 2 * c + 2]) for c in range(4)]
    got_df = loader.start(df_i, df_s)
    got_w2 = [load_w(8 + c, c) for c in range(4)]
    got_gp = [loader.start(gp_i.at[i], gp_v.at[i]) for i in range(2)]
    got_w1 = [load_w(4 + c, 4 + c) for c in range(4)]
    got_yt = loader.start(yt_i, t_s)
    got_xh = loader.start(xh_i, xh_s)
    got_dz = loader.start(dz_i, dz_s)
    got_o = loader.start(o_i, o_s)
    got_kt = loader.start(kt_i, kt_s)
    got_l = loader.start(l_i, l_s)
    greet(p, nz)
    order = (8, 9, 10, 11, 4, 5, 6, 7, 3, 0, 1, 2)
    reduce = Reduce(p, part, total, order, ra, rb_r, rx, ry, rz, send, recv)
    pump = Pump(reduce, [(c, c + 1, c + 2, c + 3) for c in range(len(order))], (0, 2, 1, 3))

    def into_part(r, left, right):
        for b in range(2):

            def tile(i):
                got = dot(left[rows_of(i, half_rows), :], right(b)).astype(bf16)
                part[r % 3, b, pl.ds(i * (nz // 2), nz // 2)] = got.reshape(
                    (nz // 2,) + part.shape[3:]
                )

            each(0, 2, tile)

    def grad_two(c):
        got_g[c].wait()
        into_part(c, dft_s, lambda b: g_s[2 * c + b])

    def grad_pre(c):
        got_w2[c].wait()
        for b in range(2):
            i = 2 * c + b
            got_gp[i].wait()
            w = weight(c, b)
            db_s[i] = jnp.zeros_like(db_s[i])

            def tile(t):
                rows = rows_of(t, half_rows)
                hidden = dot(df_s[pl.ds(2 * t, 2)].reshape(half_rows, -1), w)
                pre = (hidden * gp_v[i % 2, rows, :]).astype(bf16)
                du_s[i, rows, :] = pre
                db_s[i] += col_sum(pre.astype(f32))

            each(0, 2, tile)
            if i + 2 < 8:
                got_gp.append(loader.start(gp_i.at[i + 2], gp_v.at[i % 2]))

    def one_rows(blk):
        rows = rows_of(blk, blk_rows)
        got = None
        for c in range(4):
            for b in range(2):
                term = dot(du_s[2 * c + b, rows, :], weight(4 + c, b), contract_last)
                got = term if got is None else got + term
        acc[blk] = got

    def x_rows(blk):
        rows = rows_of(blk, blk_rows)
        got = None
        for j in range(3):
            for b in range(2):
                term = dot(dp_s[2 * j + b, rows, :], weight(j, b), contract_last)
                got = term if got is None else got + term
        acc[blk] = got

    def give_half(call, compute):
        sent = []
        for s in range(2):
            compute(other(s))
            sb[call, s] = acc[other(s)].astype(bf16)
            sent.append(beside(sb.at[call, s], rb.at[call, s], "k"))
        for s in range(2):
            compute(own(s))
        return sent

    got_dft.wait()
    grad_two(0)
    pump.step()
    grad_two(1)
    got_df.wait()
    grad_pre(0)
    grad_pre(1)
    grad_pre(2)
    pump.step()
    grad_two(2)
    grad_pre(3)
    got_w = [load_w(c, c) for c in range(4)]
    for copy in got_w1:
        copy.wait()
    pump.step()
    grad_two(3)
    lo, hi = pl.ds(0, 128), pl.ds(128, 128)
    got_q = loader.start(q_i, g_s.at[0:4, :, lo])
    got_k = loader.start(k_i, g_s.at[0:4, :, hi])
    got_v = loader.start(v_i, g_s.at[4:8, :, lo])
    sent = give_half(0, one_rows)
    got_xh.wait()
    got_dz.wait()
    shared = []
    sums = [0.0, 0.0, 0.0]
    for s in range(2):
        sent[s].wait()
        dy = dz_s[s] + (acc[own(s)] + rb[0, s].astype(f32))
        xh = xh_s[s]
        dz = norm_backward(dy, xh, r1[s], vec[3:4, :])
        da = dz.astype(bf16)
        df_s[own(s)] = da
        shared.append(beside(df_s.at[own(s)], df_s.at[own(s)], "k"))
        cols = dft_s.at[:, rows_of(own(s), blk_rows)]
        cols[...] = turn(da)
        shared.append(beside(cols, cols, "k"))
        dz_s[s] = dz
        for i, term in enumerate((dz, dy * xh, dy)):
            sums[i] = sums[i] + col_sum(term)
    pump.step()
    got_yt.wait()

    def grad_one(c):
        into_part(4 + c, t_s, lambda b: du_s[2 * c + b])

    grad_one(0)
    pump.step()
    for copy in shared:
        copy.wait()
    got_w[3].wait()
    for b in range(2):
        w = weight(3, b)

        def tile(t):
            rows = rows_of(t, half_rows)
            got = dot(df_s[pl.ds(2 * t, 2)].reshape(half_rows, -1), w).astype(bf16)
            g_s[4 + 2 * b, rows, 128:256] = got[:, :128]
            g_s[5 + 2 * b, rows, 128:256] = got[:, 128:]

        each(0, 2, tile)
    got_q.wait()
    got_k.wait()
    got_v.wait()
    got_kt.wait()
    got_l.wait()

    q_tile = 256
    vs[...] = jnp.zeros_like(vs)
    vs[0, 12:13, :] = small[3:4, :]
    for i in range(3):
        vs[0, 2 + i : 3 + i, :] = sums[i]
        vs[0, 5 + i : 6 + i, :] = small[i : i + 1, :]

    def attend(pair):
        b, lanes = pair // 2, slice(pair % 2 * 128, pair % 2 * 128 + 128)
        dk_s[...] = jnp.zeros_like(dk_s)
        dv_s[...] = jnp.zeros_like(dv_s)

        def tile(i):
            rows = rows_of(i, q_tile)
            q2, do2 = g_s[pair, rows, 0:128], g_s[4 + pair, rows, 128:256]
            k2, v2, kt2 = g_s[pair, :, 128:256], g_s[4 + pair, :, 0:128], kt_s[pair]
            dqt = None
            for h in range(2):
                qh, doh = keep_head(q2, h, 1), keep_head(do2, h, 1)
                scores = dot(k2, qh, contract_last)
                shares = jnp.exp(scores - l_s[2 * pair + h, :, rows])
                dshares = dot(v2, doh, contract_last)
                mean = col_sum(shares * dshares)
                dscores = (shares * (dshares - mean)).astype(bf16)
                dv_s[...] += dot(shares.astype(bf16), doh)
                dk_s[...] += dot(dscores, qh)
                one = dot(keep_head(kt2, h, 0), dscores)
                dqt = one if dqt is None else dqt + one
            dq = (dqt * 0.125).T.astype(bf16)
            dp_s[b, rows, lanes] = dq

        each(0, length // q_tile, tile)
        dp_s[2 + b, :, lanes] = dk_s[...].astype(bf16)
        dp_s[4 + b, :, lanes] = dv_s[...].astype(bf16)
        place = pl.ds(pl.multiple_of((2 * b + p.k) * 256 + pair % 2 * 128, 128), 128)
        vs[0, 0:1, place] = col_sum(dp_s[b, :, lanes].astype(f32))
        vs[0, 1:2, place] = col_sum(dp_s[4 + b, :, lanes].astype(f32))

    for pair in range(4):
        attend(pair)
        if pair < 3:
            grad_one(1 + pair)
        else:
            got_xt = loader.start(xt_i, t_s)
            got_o.wait()
            into_part(8, dft_s, lambda b: o_s[b])
        pump.step()
    for c in range(4):
        for b in range(2):
            vs[0, pl.ds(8 + 2 * b + p.k, 1), c * 256 : c * 256 + 256] = db_s[2 * c + b]
    vec_copy = beside(vs.at[0], vr.at[0], "k")
    got_xt.wait()

    def grad_qkv(j):
        into_part(9 + j, t_s, lambda b: dp_s[2 * j + b])

    for c in range(3):
        got_w[c].wait()
    sent = give_half(1, x_rows)
    grad_qkv(0)
    sent[1].wait()
    dz_s[1] += acc[own(1)] + rb[1, 1].astype(f32)
    sb[0, 0] = dz_s[1].astype(bf16)
    swap_in = beside(sb.at[0, 0], in_other, "y")
    pump.step()
    sent[0].wait()
    dz_s[0] += acc[own(0)] + rb[1, 0].astype(f32)
    keep_in = loader.start(dz_s.at[0], in_own)
    vec_copy.wait()
    vs[1] = vs[0] + vr[0]
    vec_copy = beside(vs.at[1], vr.at[1], "y")
    grad_qkv(1)
    pump.step()
    vec_copy.wait()
    pools[0:1, :] = vs[1, 12:13, :]
    pools[1:2, :] = vr[1, 12:13, :]
    vs[2] = vs[1] + vr[1]
    vec_copy = beside(vs.at[2], vr.at[2], "x")
    grad_qkv(2)
    pump.step()
    vec_copy.wait()
    vs[3] = vs[2] + vr[2]

    def along(src, into, base, j):
        return remote(
            src, into.at[p.z], z_sems.at[0, base, j], z_sems.at[1, base, j], p.along(j, nz)
        )

    def from_z(src, into, base, j):
        return remote(
            src,
            into.at[(p.z + nz - j) % nz],
            z_sems.at[0, base, j],
            z_sems.at[1, base, j],
            p.along(j, nz),
        )

    vz[p.z] = vs[3]
    each(1, nz, lambda j: along(vs.at[3], vz, 0, j).start())
    pump.step()
    each(1, nz, lambda j: from_z(vs.at[3], vz, 0, j).wait())
    vec_sum[...] = vz[0]

    def add_vec(z):
        vec_sum[...] += vz[z]

    each(1, nz, add_vec)
    swap_in.wait()
    pump.step()
    pump.step()

    tile8 = jnp.zeros(qs.shape[1:], f32)
    for c in range(len(order)):
        t = total[c]
        t = jnp.sum((t * t).reshape(-1, 8, 256), axis=0)
        tile8 = tile8 + t[:, :128] + t[:, 128:]
    qs[0] = tile8
    for i, axis in enumerate("kyx"):
        beside(qs.at[i], qr.at[i], axis).wait()
        qs[i + 1] = qs[i] + qr[i]
    qz[p.z] = qs[3]
    each(1, nz, lambda j: along(qs.at[3], qz, 1, j).start())
    each(1, nz, lambda j: from_z(qs.at[3], qz, 1, j).wait())
    squares[...] = qz[0]

    def add_square(z):
        squares[...] += qz[z]

    each(1, nz, add_square)
    keep_in.wait()


def backward(saved, r1, small, vec):
    w_all = saved[0]
    n_chunks, _, nz, _, rows, _ = w_all.shape
    length = saved[5].shape[1]
    blk = length // 4
    sd = jax.ShapeDtypeStruct
    V = pltpu.VMEM
    scratch = [
        V((8,) + w_all.shape[1:], bf16), V((8, length, 256), bf16), V((2, length, 256), f32),
        V((4, blk, D), bf16), V((D, length), bf16), V((8, length, 256), bf16),
        V((6, length, 256), bf16), V((D, length), bf16), V((4, blk, D), f32),
        V((2, blk, D), f32), V((2, blk, D), f32), V((2, length, 256), bf16),
        V((4, 128, length), bf16), V((8, 1, length), f32),
        V((2, 2, blk, D), bf16), V((2, 2, blk, D), bf16),
        V((length, 128), f32), V((length, 128), f32), V((8, 1, 256), f32),
        V((3, 2, nz, 2, rows, 256), bf16),
        V((5, nz, rows, 128), bf16), V((5, nz, rows, 128), bf16),
        V((4, nz, rows, 256), bf16), V((4, nz, rows, 256), bf16), V((4, nz, rows, 256), bf16),
        V((4, 16, D), f32), V((3, 16, D), f32), V((nz, 16, D), f32),
        V((4, 8, 128), f32), V((3, 8, 128), f32), V((nz, 8, 128), f32),
        DMA((7, 4, nz)), DMA((7, 4, nz)), DMA((2, 20)), DMA((32,)), DMA((12,)), DMA((2, 2, nz)),
    ]
    return pl.pallas_call(
        backward_kernel,
        out_shape=[
            sd((blk, D), f32), sd((blk, D), bf16),
            sd((n_chunks, rows, 256), f32), sd((16, D), f32), sd((2, D), f32), sd((8, 128), f32),
        ],
        in_specs=[ANY] * 15 + [VMEM] * 3,
        out_specs=[ANY] * 2 + [VMEM] * 4,
        scratch_shapes=scratch,
        compiler_params=pltpu.CompilerParams(
            collective_id=1, has_side_effects=True, vmem_limit_bytes=63 * 2**20
        ),
        name="backward",
    )(*saved, r1, small, vec)


def finish_kernel(count, tokens_all, *refs):
    (
        total, vec_sum, pools, squares, in_own, in_other,
        wq, wo, w1, w2, vec, mq, sq, mo, so, m1, s1, m2, s2, mv, sv,
        pooled, in_grad, norm,
        wq_n, mq_n, sq_n, wo_n, mo_n, so_n, w1_n, m1_n, s1_n, w2_n, m2_n, s2_n, v_n, mv_n, sv_n,
    ) = refs
    mp = lax.axis_index("mp")
    y = mp // 2
    g_vec = vec_sum[0 : vec.shape[0], :]
    grad_norm = jnp.sqrt(
        jnp.sum(squares[...], keepdims=True) + jnp.sum(g_vec * g_vec, keepdims=True)
    )
    norm[...] = grad_norm
    factor = jnp.minimum(1.0, clip_limit(count, tokens_all) / (grad_norm + 1e-06))
    rates = matrix_rates(D, FF, DOC_LEN)

    def update(old, new, part, g, rate, decay):
        results = adam_update(old[0][part], g * factor, old[1][part], old[2][part], rate, decay)
        for ref, result in zip(new, results):
            ref[part] = result

    for j in range(3):
        update((wq, mq, sq), (wq_n, mq_n, sq_n), (j,), total[j], rates[0], weight_decay)
    update((wo, mo, so), (wo_n, mo_n, so_n), (slice(None),), total[3], rates[1], weight_decay)
    for c in range(4):
        part = (slice(None), slice(c * 256, c * 256 + 256))
        update((w1, m1, s1), (w1_n, m1_n, s1_n), part, total[4 + c], rates[2], weight_decay)
        update((w2, m2, s2), (w2_n, m2_n, s2_n), part, total[8 + c], rates[3], weight_decay)
    in_grad[y] = in_own[...]
    in_grad[1 - y] = in_other[...].astype(f32)
    update((vec, mv, sv), (v_n, mv_n, sv_n), (slice(None),), g_vec, vector_rate, 0.0)
    columns = pl.ds(pl.multiple_of(mp * 256, 256), 256)
    pooled[pl.ds(y, 1), :] = pools[0:1, columns]
    pooled[pl.ds(1 - y, 1), :] = pools[1:2, columns]


def finish(tokens_all, count, results, weights, moments):
    in_own, in_other, total, vec_sum, pools, squares = results
    out_shape = [
        jax.ShapeDtypeStruct((2, 256), f32),
        jax.ShapeDtypeStruct((2,) + in_own.shape, f32),
        jax.ShapeDtypeStruct((1, 1), f32),
    ]
    for w in weights:
        out_shape += [jax.ShapeDtypeStruct(w.shape, f32)] * 3
    args = (total, vec_sum, pools, squares, in_own, in_other) + weights + moments
    rows = total.shape[1]
    steps = min(4, rows // 8)

    def cut(array):
        shape = array.shape
        lead = (0,) * (len(shape) - 2)
        block = shape[:-2] + (shape[-2] // steps, shape[-1])
        return pl.BlockSpec(block, lambda i: lead + (i, 0))

    def whole(array):
        zeros = (0,) * len(array.shape)
        return pl.BlockSpec(array.shape, lambda i: zeros)

    vectors = 4
    in_specs = [cut(total)] + [whole(a) for a in args[1:4]] + [cut(a) for a in args[4:6]]
    in_specs += [cut(w) for w in weights[:vectors]] + [whole(weights[vectors])]
    in_specs += [cut(m) for m in moments[: 2 * vectors]] + [whole(m) for m in moments[2 * vectors :]]
    out_specs = [whole(out_shape[0]), cut(out_shape[1]), whole(out_shape[2])]
    out_specs += [cut(o) for o in out_shape[3 : 3 + 3 * vectors]]
    out_specs += [whole(o) for o in out_shape[3 + 3 * vectors :]]
    return pl.pallas_call(
        partial(finish_kernel, count, tokens_all),
        grid=(steps,),
        out_shape=out_shape,
        in_specs=in_specs,
        out_specs=out_specs,
        compiler_params=pltpu.CompilerParams(vmem_limit_bytes=60 * 2**20),
        name="finish",
    )(*args)


def local(
    tokens, out_cot, cls_offset, w_qkv, w_out, w_one, w_two, vectors,
    m_qkv, v_qkv, m_out, v_out, m_one, v_one, m_two, v_two, m_vec, v_vec,
):
    length = tokens.shape[1] * lax.axis_size("mp")
    tokens_all = tokens.shape[0] * length * lax.axis_size("dp")
    weights = (w_qkv.swapaxes(0, 1), w_out, w_one, w_two, vectors)
    *saved, r1, small = forward(tokens, out_cot, cls_offset, *weights)
    results = backward(saved, r1, small, vectors)
    pooled, input_grad, grad_norm, *updated = finish(
        tokens_all,
        4 * D * D + 2 * D * FF,
        results,
        weights,
        (m_qkv.swapaxes(0, 1), v_qkv.swapaxes(0, 1), m_out, v_out, m_one, v_one, m_two, v_two, m_vec, v_vec),
    )
    updated[:3] = [u.swapaxes(0, 1) for u in updated[:3]]
    return (pooled, input_grad, grad_norm.reshape(()), *updated)


def solution(mesh):
    rows, wide, flat, whole = P("dp", "mp", None), P("dp", None, "mp"), P("dp", "mp"), P()
    return jax.shard_map(
        local,
        mesh=mesh,
        in_specs=(rows, rows, P("dp", None), wide, flat, flat, flat, whole)
        + (wide, wide)
        + (flat,) * 6
        + (whole, whole),
        out_specs=(flat, rows, whole) + (wide,) * 3 + (flat,) * 9 + (whole,) * 3,
        check_vma=False,
    )
```

```python
from functools import partial
import math

import jax
import jax.numpy as jnp
from jax import lax
from jax.experimental import pallas as pl
from jax.experimental.pallas import tpu as pltpu
from jax.sharding import PartitionSpec as P

D = 1024
HD = 64
FF = 4096
DOC_LEN = 1024
CLS_GAP = 256
STEP = 10

MESH = pl.DeviceIdType.MESH
ANY = pl.BlockSpec(memory_space=pl.ANY)
VMEM = pl.BlockSpec(memory_space=pltpu.VMEM)
DMA = pltpu.SemaphoreType.DMA
f32 = jnp.float32
bf16 = jnp.bfloat16

norm_eps = 1e-05
beta_one = 0.9
beta_two = 0.999
adam_eps = 1e-08
weight_decay = 0.01
vector_rate = 0.4
contract_last = (((1,), (1,)), ((), ()))


def clip_limit(params_all, tokens_all):
    return 0.005 * math.sqrt(params_all * tokens_all)


def matrix_rates(model_width, hidden, length):
    out_fan = max(1, 3 * model_width // length)
    return (
        1.5 / math.sqrt(model_width),
        1.5 / math.sqrt(out_fan),
        1.5 / math.sqrt(model_width),
        1.5 / math.sqrt(hidden),
    )


def adam_update(parameter, gradient, first_old, second_old, step_rate, decay_rate):
    first_new = beta_one * first_old + (1.0 - beta_one) * gradient
    second_new = beta_two * second_old + (1.0 - beta_two) * gradient * gradient
    first_hat = first_new / (1.0 - beta_one**STEP)
    second_hat = second_new / (1.0 - beta_two**STEP)
    updated = parameter - step_rate * (
        first_hat / (jnp.sqrt(second_hat) + adam_eps) + decay_rate * parameter
    )
    return (updated, first_new, second_new)


class Place:
    def __init__(self):
        dp, mp = lax.axis_index("dp"), lax.axis_index("mp")
        self.z, self.x = dp // 2, dp % 2
        self.y, self.k = mp // 2, mp % 2

    def near(self, axis):
        z, x, y, k = self.z, self.x, self.y, self.k
        if axis == "x":
            x = 1 - x
        elif axis == "y":
            y = 1 - y
        else:
            k = 1 - k
        return (z * 2 + x, y * 2 + k)

    def along(self, j, nz):
        return ((self.z + j) % nz * 2 + self.x, self.y * 2 + self.k)


def greet(place, nz, axes="xyk"):
    barrier = pltpu.get_barrier_semaphore()
    for axis in axes:
        pl.semaphore_signal(barrier, inc=1, device_id=place.near(axis), device_id_type=MESH)
    if nz > 1:

        def one(j, carry):
            pl.semaphore_signal(barrier, inc=1, device_id=place.along(j, nz), device_id_type=MESH)
            return carry

        lax.fori_loop(1, nz, one, 0)
    pl.semaphore_wait(barrier, len(axes) + nz - 1)


def remote(src, dst, send, recv, where):
    return pltpu.make_async_remote_copy(
        src_ref=src, dst_ref=dst, send_sem=send, recv_sem=recv, device_id=where, device_id_type=MESH
    )


def each(start, stop, body):
    def one(j, carry):
        body(j)
        return carry

    lax.fori_loop(start, stop, one, 0)


def dot(a, b, dims=(((1,), (0,)), ((), ()))):
    return lax.dot_general(a, b, dims, preferred_element_type=f32)


class Gather:
    def __init__(self, place, own, full, send, recv, far, by_x):
        self.p, self.own, self.full, self.send, self.recv = place, own, full, send, recv
        self.far, self.by_x = far, by_x
        self.nz = full.shape[2]

    def to(self, kind, c, j, src, dst, where):
        n = self.recv.shape[1]
        if c < n:
            send, recv = self.send.at[kind, c % 8, j], self.recv.at[kind, c, j]
        else:
            send, recv = self.far.at[0, c - n, kind], self.far.at[1, c - n, kind]
        return remote(src, dst, send, recv, where)

    def along_z(self, c, j):
        p = self.p
        return self.to(
            0, c, j, self.own.at[c], self.full.at[c, p.y, p.z, p.x], p.along(j, self.nz)
        )

    def pass_xy(self, kind, c, j):
        p = self.p
        there = self.full.at[c, p.y, (p.z + self.nz - j) % self.nz, p.x]
        src = self.own.at[c] if isinstance(j, int) and j == 0 else there
        return self.to(kind, c, j, src, there, p.near("x" if kind == 1 else "y"))

    def pass_half(self, kind, c, j):
        p = self.p
        z = (p.z + self.nz - j) % self.nz
        if kind == 3:
            ref = self.full.at[c, p.y, z, 1 - p.x, :, pl.ds(0, 128)]
            return self.to(3, c, j, ref, ref, p.near("y"))
        ref = self.full.at[c, 1 - p.y, z, p.x]
        if c not in self.by_x:
            ref = ref.at[:, pl.ds(128, 128)]
        return self.to(4, c, j, ref, ref, p.near("x"))

    def halves(self, c):
        return (4,) if c in self.by_x else (3, 4)

    def stage(self, s, c):
        nz = self.nz
        if s == 0:
            self.pass_xy(1, c, 0).start()
            self.pass_xy(2, c, 0).start()
            each(1, nz, lambda j: self.along_z(c, j).start())
        elif s == 1:

            def one(j):
                self.along_z(c, j).wait()
                self.pass_xy(1, c, j).start()
                self.pass_xy(2, c, j).start()

            each(1, nz, one)
        elif s == 2:
            def two(j):
                for kind in (2, 1):
                    self.pass_xy(kind, c, j).wait()
                    if kind + 2 in self.halves(c):
                        self.pass_half(kind + 2, c, j).start()

            two(0)

            each(1, nz, two)
        else:

            def three(j):
                for kind in self.halves(c):
                    self.pass_half(kind, c, j).wait()

            each(0, nz, three)


class Far:
    def __init__(self, gather, c, sends, recvs):
        self.g, self.c, self.sends, self.recvs = gather, c, sends, recvs

    def piece(self, i):
        p = self.g.p
        x = 1 - p.x if i in (1, 3) else p.x
        y = 1 - p.y if i in (2, 3) else p.y
        return self.g.full.at[self.c, y, p.z, x]

    def copy(self, i, j):
        g = self.g
        ref = self.piece(i)
        src = g.own.at[self.c] if i == 0 else ref
        return remote(src, ref, self.sends.at[i, j], self.recvs.at[i, j], g.p.along(j, g.nz))

    def step(self, s):
        g, c = self.g, self.c
        if s == 0:
            g.pass_xy(1, c, 0).start()
            g.pass_xy(2, c, 0).start()
        elif s == 1:
            for kind in (1, 2):
                g.pass_xy(kind, c, 0).wait()
                g.pass_half(kind + 2, c, 0).start()
        elif s == 2:
            for kind in (3, 4):
                g.pass_half(kind, c, 0).wait()
        elif s < 7:
            each(1, g.nz, lambda j: self.copy(s - 3, j).start())
        else:

            def last(j):
                for i in range(4):
                    self.copy(i, j).wait()

            each(1, g.nz, last)


class Pump:
    def __init__(self, mover, times, order):
        self.mover, self.times, self.order, self.t = mover, times, order, 0

    def step(self):
        for s in self.order:
            for c, when in enumerate(self.times):
                if when[s] == self.t:
                    self.mover.stage(s, c)
        self.t += 1


class Saver:
    def __init__(self, sems):
        self.sems, self.list = sems, []

    def start(self, src, dst):
        copy = pltpu.make_async_copy(src, dst, self.sems.at[len(self.list)])
        copy.start()
        self.list.append(copy)
        return copy

    def wait(self, *done):
        for copy in self.list:
            if all(copy is not other for other in done):
                copy.wait()


def turn(block):
    return block.astype(f32).T.astype(bf16)


def normalize(z):
    centered = z - jnp.mean(z, axis=-1, keepdims=True)
    r = lax.rsqrt(jnp.mean(centered * centered, axis=-1, keepdims=True) + norm_eps)
    return centered * r, r


def norm_backward(cot, xh, r, gain):
    e = cot * gain
    return r * (
        e - jnp.mean(e, axis=-1, keepdims=True) - xh * jnp.mean(e * xh, axis=-1, keepdims=True)
    )


def head_mask(h, dim, shape):
    lane = lax.broadcasted_iota(jnp.int32, shape, dim)
    return (lane // HD) == h


def keep_head(block, h, dim):
    return jnp.where(head_mask(h, dim, block.shape), block, jnp.zeros_like(block))


def col_sum(a):
    return jnp.sum(a, axis=0, keepdims=True)


FWD_SAVES = 40


def forward_kernel(
    x_ref, cot_ref, cls, wq, wo, w1, w2, vec,
    w_all, q_o, k_o, v_o, kt_o, xt_o, o_o, l_o, yt_o, g_o, gp_o, xh_o, df_o, dft_o, dz_o,
    r_o, small,
    shard, x_v, w_v, q_s, k_s, v_s, kt_s, vt_s, o_s, l_s, xt_s, y_s, yt_s, g_s, gp_s, acc, y1_s,
    xh_s, sb, rb, cot_v, cot_r,
    send, recv, far_xy, far_send, far_recv, side, save_sems, load_sems,
):
    p = Place()
    nz = w_all.shape[2]
    length = xt_s.shape[1]
    blk_rows = x_v.shape[1]
    saver = Saver(save_sems)
    keep_cot = saver.start(cot_ref.at[p.y], cot_v)
    load_cot = saver.start(cot_ref.at[1 - p.y], y1_s.at[0])
    for j in range(3):
        shard[j] = wq[j].astype(bf16)
    greet(p, nz)
    gather = Gather(p, shard, w_all, send, recv, far_xy, (0, 1, 5, 6))
    early = [(max(0, c - 1), c + 1, c + 2, c + 3) for c in range(3)]
    later = [(c - 2, c + 1, c + 3, c + 5) for c in range(3, w_all.shape[0] - 2)]
    pump = Pump(gather, early + later, (2, 0, 1, 3))
    far = [Far(gather, 10 + i, far_send.at[i], far_recv.at[i]) for i in range(2)]
    plan = {1:[(0,0),(1,0)],3:[(0,1),(1,1),(0,3)],4:[(1,3)],5:[(0,2),(1,2),(0,4)],6:[(1,4)],7:[(0,5)],8:[(1,5)],9:[(0,6)],10:[(1,6)]}

    def step():
        for i, s in plan.get(pump.t, ()):
            far[i].step(s)
        pump.step()

    n_side = [0]

    def beside(src, dst, axis):
        i = n_side[0]
        n_side[0] += 1
        copy = remote(src, dst, side.at[0, i], side.at[1, i], p.near(axis))
        copy.start()
        return copy

    def own(s):
        return (p.y if s == 0 else 1 - p.y) * 2 + p.k

    def other(s):
        return (p.y if s == 0 else 1 - p.y) * 2 + 1 - p.k

    loads = {}

    def load(c):
        loads[c] = pltpu.make_async_copy(w_all.at[c], w_v.at[c], load_sems.at[c])
        loads[c].start()

    def weight(c, b):
        return w_v[c, b].reshape(-1, 256)

    def rows_of(i, n):
        return pl.ds(pl.multiple_of(i * n, n), n)

    mine = x_v.at[own(0)]
    swap_x = beside(x_ref.at[1 - p.y], mine, "y")
    keep_x = saver.start(x_ref.at[p.y], mine)
    give_x = beside(x_ref.at[p.y], mine, "k")
    step()
    shard[3] = wo[...].astype(bf16)
    for c in range(4):
        shard[4 + c] = w1[:, c * 256 : c * 256 + 256].astype(bf16)
        shard[8 + c] = w2[:, c * 256 : c * 256 + 256].astype(bf16)
    keep_w = saver.start(shard, w_all.at[:, p.y, p.z, p.x])
    load_cot.wait()
    sb[1, 0] = y1_s[0].astype(bf16)
    step()
    swap_x.wait()
    pass_x = beside(x_v.at[own(1)], x_v.at[own(1)], "k")
    step()
    keep_x.wait()
    keep_w.wait()
    give_x.wait()
    pass_x.wait()
    half_rows = 2 * blk_rows

    def project(j):
        for b in range(2):
            w = weight(j, b)

            def tile(i):
                rows = rows_of(i, half_rows)
                x = x_v[pl.ds(2 * i, 2)].reshape(half_rows, -1)
                got = dot(x, w)
                if j != 1:
                    bias = pl.ds(pl.multiple_of((2 * b + p.k) * 256, 256), 256)
                    got = got + vec[j // 2 : j // 2 + 1, bias]
                got = got.astype(bf16)
                if j == 0:
                    got = got * bf16(0.125)
                dst = (q_s, k_s, v_s)[j]
                dst[2 * b, rows, :] = got[:, :128]
                dst[2 * b + 1, rows, :] = got[:, 128:]
                if j > 0:
                    turned = turn(got)
                    dst = (None, kt_s, vt_s)[j]
                    dst[2 * b, :, rows] = turned[:128]
                    dst[2 * b + 1, :, rows] = turned[128:]

            each(0, 2, tile)

    def flip(i):
        for s in range(4):
            cols = pl.ds(s * 256, 256)
            xt_s[cols, rows_of(i, blk_rows)] = turn(x_v[i, :, cols])

    each(0, 4, flip)
    save_xt = saver.start(xt_s, xt_o)
    step()
    load(0)
    step()
    load(1)
    loads[0].wait()
    project(0)
    step()
    load(2)
    loads[1].wait()
    project(1)
    swap_cot = beside(sb.at[1, 0], cot_r, "y")
    step()
    loads[2].wait()
    project(2)

    q_tile = 256

    def attend(pair):
        b, lanes = pair // 2, pl.ds(pair % 2 * 128, 128)

        def tile(i):
            rows = rows_of(i, q_tile)
            q2, k2, vt2 = q_s[pair, rows, :], k_s[pair], vt_s[pair]
            mixed = None
            for h in range(2):
                scores = dot(k2, keep_head(q2, h, 1), contract_last)
                top = jnp.max(scores, axis=0, keepdims=True)
                raised = jnp.exp(scores - top)
                total = col_sum(raised)
                shares = (raised * (1.0 / total)).astype(bf16)
                l_s[2 * pair + h, :, rows] = top + jnp.log(total)
                one = dot(keep_head(vt2, h, 0), shares)
                mixed = one if mixed is None else mixed + one
            o_s[b, rows, lanes] = mixed.T.astype(bf16)

        each(0, length // q_tile, tile)

    for pair in range(4):
        attend(pair)
        step()
        if pair > 0:
            load(2 + pair)
    for src, dst in ((q_s, q_o), (k_s, k_o), (v_s, v_o), (kt_s, kt_o), (o_s, o_o), (l_s, l_o)):
        saver.start(src, dst)

    loads[3].wait()

    def out_rows(blk):
        rows = rows_of(blk, blk_rows)
        acc[blk] = dot(o_s[0, rows, :], weight(3, 0), contract_last) + dot(
            o_s[1, rows, :], weight(3, 1), contract_last
        )

    def give_half(call, compute):
        sent = []
        for s in range(2):
            compute(other(s))
            sb[call, s] = acc[other(s)].astype(bf16)
            sent.append(beside(sb.at[call, s], rb.at[call, s], "k"))
        for s in range(2):
            compute(own(s))
        return sent

    sent = give_half(0, out_rows)
    shared = []
    for s in range(2):
        sent[s].wait()
        z = x_v[own(s)].astype(f32) + (acc[own(s)] + rb[0, s].astype(f32)) + vec[2:3, :]
        xh, r = normalize(z)
        xh_s[s] = xh
        r_o[s] = r
        y1 = xh * vec[3:4, :] + vec[4:5, :]
        y1_s[s] = y1
        y_s[own(s)] = y1.astype(bf16)
        shared.append(beside(y_s.at[own(s)], y_s.at[own(s)], "k"))
    saver.start(xh_s, xh_o)
    for copy in shared:
        copy.wait()

    def flip_y(i):
        for s in range(4):
            cols = pl.ds(s * 256, 256)
            yt_s[cols, rows_of(i, blk_rows)] = turn(y_s[i, :, cols])

    each(0, 4, flip_y)
    saver.start(yt_s, yt_o)

    def ffn_up(c):
        for b in range(2):
            w = weight(4 + c, b)
            bias = vec[pl.ds(8 + 2 * b + p.k, 1), c * 256 : c * 256 + 256]

            def tile(i):
                rows = rows_of(i, half_rows)
                u = dot(y_s[pl.ds(2 * i, 2)].reshape(half_rows, -1), w) + bias
                share = 0.5 * (1.0 + lax.erf(u * 0.7071067811865476))
                g_s[2 * c + b, rows, :] = (u * share).astype(bf16)
                gp_s[2 * c + b, rows, :] = share + u * (
                    jnp.exp(-0.5 * (u * u)) * 0.3989422804014327
                )

            each(0, 2, tile)
        saver.start(g_s.at[2 * c : 2 * c + 2], g_o.at[2 * c : 2 * c + 2])
        saver.start(gp_s.at[2 * c : 2 * c + 2], gp_o.at[2 * c : 2 * c + 2])

    def down_rows(c, blk):
        rows = rows_of(blk, blk_rows)
        got = dot(g_s[2 * c, rows, :], weight(8 + c, 0), contract_last) + dot(
            g_s[2 * c + 1, rows, :], weight(8 + c, 1), contract_last
        )
        acc[blk] = got if c == 0 else acc[blk] + got

    step()
    load(6)
    loads[4].wait()
    ffn_up(0)
    step()
    load(7)
    loads[5].wait()
    ffn_up(1)
    step()
    load(8)
    loads[6].wait()
    ffn_up(2)
    step()
    load(9)
    far[0].step(7)
    load(10)
    loads[7].wait()
    ffn_up(3)
    far[1].step(7)
    load(11)
    for c in range(3):
        loads[8 + c].wait()
        each(0, 4, partial(down_rows, c))
    loads[11].wait()
    keep_cot.wait()
    swap_cot.wait()
    save_xt.wait()
    sent = give_half(1, partial(down_rows, 3))
    shared = []
    totals = [0.0, 0.0, 0.0, 0.0]
    for s in range(2):
        sent[s].wait()
        z = y1_s[s] + (acc[own(s)] + rb[1, s].astype(f32)) + vec[5:6, :]
        xh, r = normalize(z)
        cot = cot_v[...] if s == 0 else cot_r[...].astype(f32)
        dz = norm_backward(cot, xh, r, vec[6:7, :])
        df = dz.astype(bf16)
        x_v[own(s)] = df
        shared.append(beside(x_v.at[own(s)], x_v.at[own(s)], "k"))
        xt_s[:, rows_of(own(s), blk_rows)] = turn(df)
        cols = xt_s.at[:, rows_of(own(s), blk_rows)]
        shared.append(beside(cols, cols, "k"))
        y1_s[s] = dz
        out = xh * vec[6:7, :] + vec[7:8, :]
        row = lax.broadcasted_iota(jnp.int32, (blk_rows, 1), 0) + own(s) * blk_rows
        hits = [row == cls[p.y, j] + j * CLS_GAP for j in range(cls.shape[1])]
        picks = sum(hit.astype(f32) for hit in hits) / len(hits)
        for i, term in enumerate((dz, cot * xh, cot, picks * out)):
            totals[i] = totals[i] + col_sum(term)
    for i in range(4):
        small[i : i + 1, :] = totals[i]
    saver.start(y1_s, dz_o)
    for copy in shared:
        copy.wait()
    saver.start(x_v, df_o)
    saver.start(xt_s, dft_o)
    saver.wait(keep_x, keep_w, keep_cot, load_cot, save_xt)


def forward(x_loc, cot, cls, w_qkv, w_out, w_one, w_two, vec):
    nz = lax.axis_size("dp") // 2
    n_chunks, rows = 12, w_out.shape[0]
    blk = x_loc.shape[1]
    length = 4 * blk
    full = (n_chunks, 2, nz, 2, rows, 256)
    sd = jax.ShapeDtypeStruct
    outs = [
        sd(full, bf16),
        sd((4, length, 128), bf16),
        sd((4, length, 128), bf16),
        sd((4, length, 128), bf16),
        sd((4, 128, length), bf16),
        sd((D, length), bf16),
        sd((2, length, 256), bf16),
        sd((8, 1, length), f32),
        sd((D, length), bf16),
        sd((8, length, 256), bf16),
        sd((8, length, 256), f32),
        sd((2, blk, D), f32),
        sd((4, blk, D), bf16),
        sd((D, length), bf16),
        sd((2, blk, D), f32),
        sd((2, blk, 1), f32),
        sd((8, D), f32),
    ]
    V = pltpu.VMEM
    scratch = [
        V((n_chunks, rows, 256), bf16), V((4, blk, D), bf16), V(full, bf16),
        V((4, length, 128), bf16), V((4, length, 128), bf16), V((4, length, 128), bf16),
        V((4, 128, length), bf16), V((4, 128, length), bf16),
        V((2, length, 256), bf16), V((8, 1, length), f32),
        V((D, length), bf16), V((4, blk, D), bf16), V((D, length), bf16),
        V((8, length, 256), bf16), V((8, length, 256), f32),
        V((4, blk, D), f32), V((2, blk, D), f32), V((2, blk, D), f32),
        V((2, 2, blk, D), bf16), V((2, 2, blk, D), bf16),
        V((blk, D), f32), V((blk, D), bf16),
        DMA((5, 8, nz)), DMA((5, n_chunks - 2, nz)), DMA((2, 2, 5)), DMA((2, 4, nz)), DMA((2, 4, nz)), DMA((2, 16)), DMA((FWD_SAVES,)), DMA((n_chunks,)),
    ]
    return pl.pallas_call(
        forward_kernel,
        out_shape=outs,
        in_specs=[ANY] * 2 + [pl.BlockSpec(memory_space=pltpu.SMEM)] + [VMEM] * 5,
        out_specs=[ANY] * 15 + [VMEM] * 2,
        scratch_shapes=scratch,
        compiler_params=pltpu.CompilerParams(
            collective_id=0, has_side_effects=True, vmem_limit_bytes=62 * 2**20
        ),
        name="forward",
    )(x_loc, cot, cls, w_qkv, w_out, w_one, w_two, vec)


class Reduce:
    def __init__(self, place, part, total, order, ra, rb, rx, ry, rz, send, recv):
        self.p, self.part, self.total, self.order = place, part, total, order
        self.ra, self.rb, self.rx, self.ry, self.rz = ra, rb, rx, ry, rz
        self.send, self.recv = send, recv
        self.nz = part.shape[2]

    def to(self, kind, r, j, src, dst, where):
        return remote(src, dst, self.send.at[kind, r % 4, j], self.recv.at[kind, r % 8, j], where)

    def copy(self, kind, r, z):
        p, a, b = self.p, pl.ds(0, 128), pl.ds(128, 128)
        part, slot = self.part.at[r % 5], r % 6
        if kind == 0:
            src, dst, axis = part.at[1 - p.y, z, 1 - p.x, :, a], self.ra.at[r % 8, z], "y"
        elif kind == 1:
            src, dst, axis = part.at[1 - p.y, z, 1 - p.x, :, b], self.rb.at[r % 8, z], "x"
        elif kind == 2:
            src, dst, axis = self.ra.at[r % 8, z], self.rx.at[slot, z, :, a], "x"
        elif kind == 3:
            src, dst, axis = self.rb.at[r % 8, z], self.ry.at[slot, z, :, b], "y"
        elif kind == 5:
            src, dst, axis = part.at[p.y, z, 1 - p.x, :, b], self.rx.at[slot, z, :, b], "x"
        else:
            src, dst, axis = part.at[1 - p.y, z, p.x, :, a], self.ry.at[slot, z, :, a], "y"
        return self.to(kind, r, z, src, dst, p.near(axis))

    def send_z(self, r, j):
        p = self.p
        z = (p.z + j) % self.nz
        return self.to(4, r, j, self.rx.at[r % 6, z], self.rz.at[r % 6, j], p.along(j, self.nz))

    def stage(self, s, r):
        p, nz, slot = self.p, self.nz, r % 6
        part, chunk = self.part.at[r % 5], self.order[r]
        if s == 0:

            def zero(z):
                self.copy(0, r, z).start()
                self.copy(1, r, z).start()

            each(0, nz, zero)
        elif s == 1:

            def one(z):
                self.copy(0, r, z).wait()
                self.copy(1, r, z).wait()
                self.ra[r % 8, z] = (
                    self.ra[r % 8, z].astype(f32) + part[p.y, z, 1 - p.x, :, 0:128].astype(f32)
                ).astype(bf16)
                self.rb[r % 8, z] = (
                    self.rb[r % 8, z].astype(f32) + part[1 - p.y, z, p.x, :, 128:256].astype(f32)
                ).astype(bf16)
                for kind in (2, 3, 5, 6):
                    self.copy(kind, r, z).start()

            each(0, nz, one)
        elif s == 2:

            def add(z):
                for kind in (2, 3, 5, 6):
                    self.copy(kind, r, z).wait()
                return (
                    part[p.y, z, p.x].astype(f32)
                    + self.rx[slot, z].astype(f32)
                    + self.ry[slot, z].astype(f32)
                )

            def two(j):
                z = (p.z + j) % nz
                self.rx[slot, z] = add(z).astype(bf16)
                self.send_z(r, j).start()

            each(1, nz, two)
            self.total[chunk] = add(p.z)
        else:

            def three(j):
                self.send_z(r, j).wait()
                self.total[chunk] += self.rz[slot, j].astype(f32)

            each(1, nz, three)


def backward_kernel(
    w_all, q_i, k_i, v_i, kt_i, xt_i, o_i, l_i, yt_i, g_i, gp_i, xh_i, df_i, dft_i, dz_i,
    r1, small, vec,
    in_own, in_other,
    total, vec_sum, pools, squares,
    w_v, g_s, gp_v, df_s, dft_s, du_s, dp_s, t_s, acc, xh_s, dz_s, o_s, kt_s, l_s,
    sb, rb, dk_s, dv_s, db_s, part, ra, rb_r, rx, ry, rz, vs, vr, vz, qs, qr, qz,
    send, recv, side, load_sems, w_sems, z_sems, q_sems,
):
    p = Place()
    nz = w_all.shape[2]
    length = dft_s.shape[1]
    blk_rows = df_s.shape[1]
    half_rows = 2 * blk_rows

    loader = Saver(load_sems)
    n_side = [0]

    def beside(src, dst, axis):
        i = n_side[0]
        n_side[0] += 1
        copy = remote(src, dst, side.at[0, i], side.at[1, i], p.near(axis))
        copy.start()
        return copy

    def own(s):
        return (p.y if s == 0 else 1 - p.y) * 2 + p.k

    def other(s):
        return (p.y if s == 0 else 1 - p.y) * 2 + 1 - p.k

    def rows_of(i, n):
        return pl.ds(pl.multiple_of(i * n, n), n)

    n_w = [0]

    def load_w(c, slot):
        copy = pltpu.make_async_copy(w_all.at[c], w_v.at[slot], w_sems.at[n_w[0]])
        n_w[0] += 1
        copy.start()
        return copy

    def weight(slot, b):
        return w_v[slot, b].reshape(-1, 256)

    got_dft = loader.start(dft_i, dft_s)
    got_g = [loader.start(g_i.at[2 * c : 2 * c + 2], g_s.at[2 * c : 2 * c + 2]) for c in range(4)]
    got_df = loader.start(df_i, df_s)
    got_w2 = [load_w(8 + c, c) for c in range(4)]
    got_gp = [loader.start(gp_i.at[i], gp_v.at[i]) for i in range(2)]
    got_w1 = [load_w(4 + c, 4 + c) for c in range(4)]
    got_yt = loader.start(yt_i, t_s)
    got_xh = loader.start(xh_i, xh_s)
    got_dz = loader.start(dz_i, dz_s)
    got_o = loader.start(o_i, o_s)
    got_kt = loader.start(kt_i, kt_s)
    got_l = loader.start(l_i, l_s)
    barrier = pltpu.get_barrier_semaphore()
    pl.semaphore_signal(barrier, inc=1, device_id=p.near("k"), device_id_type=MESH)

    def hello(j):
        there = ((p.z * 2 + p.x) * 2 + p.y + j) % (4 * nz)
        pl.semaphore_signal(
            barrier, inc=1, device_id=(there // 2, there % 2 * 2 + p.k), device_id_type=MESH
        )

    each(1, 4 * nz, hello)
    pl.semaphore_wait(barrier, 4 * nz)
    order = (8, 9, 10, 11, 4, 5, 6, 7, 3, 0, 1, 2)
    reduce = Reduce(p, part, total, order, ra, rb_r, rx, ry, rz, send, recv)
    pump = Pump(reduce, [(c, c + 1, c + 3, c + 4) if c < 11 else (c, c + 1, c + 2, c + 3) for c in range(len(order))], (0, 2, 1, 3))

    def into_part(r, left, right):
        for b in range(2):

            def tile(i):
                got = dot(left[rows_of(i, half_rows), :], right(b)).astype(bf16)
                part[r % 5, b, pl.ds(i * (nz // 2), nz // 2)] = got.reshape(
                    (nz // 2,) + part.shape[3:]
                )

            each(0, 2, tile)

    def grad_two(c):
        got_g[c].wait()
        into_part(c, dft_s, lambda b: g_s[2 * c + b])

    def grad_pre(c):
        got_w2[c].wait()
        for b in range(2):
            i = 2 * c + b
            got_gp[i].wait()
            w = weight(c, b)
            db_s[i] = jnp.zeros_like(db_s[i])

            def tile(t):
                rows = rows_of(t, half_rows)
                hidden = dot(df_s[pl.ds(2 * t, 2)].reshape(half_rows, -1), w)
                pre = (hidden * gp_v[i % 2, rows, :]).astype(bf16)
                du_s[i, rows, :] = pre
                db_s[i] += col_sum(pre.astype(f32))

            each(0, 2, tile)
            if i + 2 < 8:
                got_gp.append(loader.start(gp_i.at[i + 2], gp_v.at[i % 2]))

    def one_rows(blk):
        rows = rows_of(blk, blk_rows)
        got = None
        for c in range(4):
            for b in range(2):
                term = dot(du_s[2 * c + b, rows, :], weight(4 + c, b), contract_last)
                got = term if got is None else got + term
        acc[blk] = got

    def x_rows(blk):
        rows = rows_of(blk, blk_rows)
        got = None
        for j in range(3):
            for b in range(2):
                term = dot(dp_s[2 * j + b, rows, :], weight(j, b), contract_last)
                got = term if got is None else got + term
        acc[blk] = got

    def give_half(call, compute):
        sent = []
        for s in range(2):
            compute(other(s))
            sb[call, s] = acc[other(s)].astype(bf16)
            sent.append(beside(sb.at[call, s], rb.at[call, s], "k"))
        for s in range(2):
            compute(own(s))
        return sent

    got_dft.wait()
    grad_two(0)
    pump.step()
    grad_two(1)
    got_df.wait()
    grad_pre(0)
    grad_pre(1)
    grad_pre(2)
    pump.step()
    grad_two(2)
    grad_pre(3)
    got_w = [load_w(c, c) for c in range(4)]
    for copy in got_w1:
        copy.wait()
    pump.step()
    grad_two(3)
    lo, hi = pl.ds(0, 128), pl.ds(128, 128)
    got_q = loader.start(q_i, g_s.at[0:4, :, lo])
    got_k = loader.start(k_i, g_s.at[0:4, :, hi])
    got_v = loader.start(v_i, g_s.at[4:8, :, lo])
    sent = give_half(0, one_rows)
    got_xh.wait()
    got_dz.wait()
    shared = []
    sums = [0.0, 0.0, 0.0]
    for s in range(2):
        sent[s].wait()
        dy = dz_s[s] + (acc[own(s)] + rb[0, s].astype(f32))
        xh = xh_s[s]
        dz = norm_backward(dy, xh, r1[s], vec[3:4, :])
        da = dz.astype(bf16)
        df_s[own(s)] = da
        shared.append(beside(df_s.at[own(s)], df_s.at[own(s)], "k"))
        cols = dft_s.at[:, rows_of(own(s), blk_rows)]
        cols[...] = turn(da)
        shared.append(beside(cols, cols, "k"))
        dz_s[s] = dz
        for i, term in enumerate((dz, dy * xh, dy)):
            sums[i] = sums[i] + col_sum(term)
    pump.step()
    got_yt.wait()

    def grad_one(c):
        into_part(4 + c, t_s, lambda b: du_s[2 * c + b])

    grad_one(0)
    pump.step()
    for copy in shared:
        copy.wait()
    got_w[3].wait()
    for b in range(2):
        w = weight(3, b)

        def tile(t):
            rows = rows_of(t, half_rows)
            got = dot(df_s[pl.ds(2 * t, 2)].reshape(half_rows, -1), w).astype(bf16)
            g_s[4 + 2 * b, rows, 128:256] = got[:, :128]
            g_s[5 + 2 * b, rows, 128:256] = got[:, 128:]

        each(0, 2, tile)
    got_q.wait()
    got_k.wait()
    got_v.wait()
    got_kt.wait()
    got_l.wait()

    q_tile = 256
    vs[...] = jnp.zeros_like(vs)
    vs[0, 12:13, :] = small[3:4, :]
    for i in range(3):
        vs[0, 2 + i : 3 + i, :] = sums[i]
        vs[0, 5 + i : 6 + i, :] = small[i : i + 1, :]

    def attend(pair):
        b, lanes = pair // 2, slice(pair % 2 * 128, pair % 2 * 128 + 128)
        dk_s[...] = jnp.zeros_like(dk_s)
        dv_s[...] = jnp.zeros_like(dv_s)

        def tile(i):
            rows = rows_of(i, q_tile)
            q2, do2 = g_s[pair, rows, 0:128], g_s[4 + pair, rows, 128:256]
            k2, v2, kt2 = g_s[pair, :, 128:256], g_s[4 + pair, :, 0:128], kt_s[pair]
            dqt = None
            for h in range(2):
                qh, doh = keep_head(q2, h, 1), keep_head(do2, h, 1)
                scores = dot(k2, qh, contract_last)
                shares = jnp.exp(scores - l_s[2 * pair + h, :, rows])
                dshares = dot(v2, doh, contract_last)
                mean = col_sum(shares * dshares)
                dscores = (shares * (dshares - mean)).astype(bf16)
                dv_s[...] += dot(shares.astype(bf16), doh)
                dk_s[...] += dot(dscores, qh)
                one = dot(keep_head(kt2, h, 0), dscores)
                dqt = one if dqt is None else dqt + one
            dq = (dqt * 0.125).T.astype(bf16)
            dp_s[b, rows, lanes] = dq

        each(0, length // q_tile, tile)
        dp_s[2 + b, :, lanes] = dk_s[...].astype(bf16)
        dp_s[4 + b, :, lanes] = dv_s[...].astype(bf16)
        place = pl.ds(pl.multiple_of((2 * b + p.k) * 256 + pair % 2 * 128, 128), 128)
        vs[0, 0:1, place] = col_sum(dp_s[b, :, lanes].astype(f32))
        vs[0, 1:2, place] = col_sum(dp_s[4 + b, :, lanes].astype(f32))

    for pair in range(4):
        attend(pair)
        if pair < 3:
            grad_one(1 + pair)
        else:
            got_xt = loader.start(xt_i, t_s)
            got_o.wait()
            into_part(8, dft_s, lambda b: o_s[b])
        pump.step()
    for c in range(4):
        for b in range(2):
            vs[0, pl.ds(8 + 2 * b + p.k, 1), c * 256 : c * 256 + 256] = db_s[2 * c + b]
    vec_copy = beside(vs.at[0], vr.at[0], "k")
    got_xt.wait()

    def grad_qkv(j):
        into_part(9 + j, t_s, lambda b: dp_s[2 * j + b])

    for c in range(3):
        got_w[c].wait()
    sent = give_half(1, x_rows)
    grad_qkv(0)
    sent[1].wait()
    dz_s[1] += acc[own(1)] + rb[1, 1].astype(f32)
    sb[0, 0] = dz_s[1].astype(bf16)
    swap_in = beside(sb.at[0, 0], in_other, "y")
    pump.step()
    sent[0].wait()
    dz_s[0] += acc[own(0)] + rb[1, 0].astype(f32)
    keep_in = loader.start(dz_s.at[0], in_own)
    vec_copy.wait()
    vs[1] = vs[0] + vr[0]
    vec_copy = beside(vs.at[1], vr.at[1], "y")
    grad_qkv(1)
    pump.step()
    vec_copy.wait()
    pools[0:1, :] = vs[1, 12:13, :]
    pools[1:2, :] = vr[1, 12:13, :]
    vs[2] = vs[1] + vr[1]
    vec_copy = beside(vs.at[2], vr.at[2], "x")
    grad_qkv(2)
    pump.step()
    vec_copy.wait()
    vs[3] = vs[2] + vr[2]

    def along(src, into, j):
        return remote(
            src, into.at[p.z], z_sems.at[0, j], z_sems.at[1, j], p.along(j, nz)
        )

    def from_z(src, into, j):
        return remote(
            src,
            into.at[(p.z + nz - j) % nz],
            z_sems.at[0, j],
            z_sems.at[1, j],
            p.along(j, nz),
        )

    vz[p.z] = vs[3]
    each(1, nz, lambda j: along(vs.at[3], vz, j).start())
    pump.step()
    each(1, nz, lambda j: from_z(vs.at[3], vz, j).wait())
    vec_sum[...] = vz[0]

    def add_vec(z):
        vec_sum[...] += vz[z]

    each(1, nz, add_vec)
    swap_in.wait()
    while pump.t <= max(when[3] for when in pump.times):
        pump.step()

    tile8 = jnp.zeros(qs.shape[1:], f32)
    for c in range(len(order)):
        t = total[c]
        t = jnp.sum((t * t).reshape(-1, 8, 256), axis=0)
        tile8 = tile8 + t[:, :128] + t[:, 128:]
    qs[0] = tile8
    beside(qs.at[0], qr, "k").wait()
    qs[1] = qs[0] + qr[...]
    chips, me = 4 * nz, (p.z * 2 + p.x) * 2 + p.y

    def to_chip(j, into):
        there = (me + j) % chips
        return remote(
            qs.at[1], qz.at[into], q_sems.at[0, j], q_sems.at[1, j], (there // 2, there % 2 * 2 + p.k)
        )

    qz[me] = qs[1]
    each(1, chips, lambda j: to_chip(j, me).start())
    each(1, chips, lambda j: to_chip(j, (me + chips - j) % chips).wait())
    squares[...] = qz[0]

    def add_square(i):
        squares[...] += qz[i]

    each(1, chips, add_square)
    keep_in.wait()


def backward(saved, r1, small, vec):
    w_all = saved[0]
    n_chunks, _, nz, _, rows, _ = w_all.shape
    length = saved[5].shape[1]
    blk = length // 4
    sd = jax.ShapeDtypeStruct
    V = pltpu.VMEM
    scratch = [
        V((8,) + w_all.shape[1:], bf16), V((8, length, 256), bf16), V((2, length, 256), f32),
        V((4, blk, D), bf16), V((D, length), bf16), V((8, length, 256), bf16),
        V((6, length, 256), bf16), V((D, length), bf16), V((4, blk, D), f32),
        V((2, blk, D), f32), V((2, blk, D), f32), V((2, length, 256), bf16),
        V((4, 128, length), bf16), V((8, 1, length), f32),
        V((2, 2, blk, D), bf16), V((2, 2, blk, D), bf16),
        V((length, 128), f32), V((length, 128), f32), V((8, 1, 256), f32),
        V((5, 2, nz, 2, rows, 256), bf16),
        V((8, nz, rows, 128), bf16), V((8, nz, rows, 128), bf16),
        V((6, nz, rows, 256), bf16), V((6, nz, rows, 256), bf16), V((6, nz, rows, 256), bf16),
        V((4, 16, D), f32), V((3, 16, D), f32), V((nz, 16, D), f32),
        V((2, 8, 128), f32), V((8, 128), f32), V((4 * nz, 8, 128), f32),
        DMA((7, 4, nz)), DMA((7, 8, nz)), DMA((2, 20)), DMA((32,)), DMA((12,)), DMA((2, nz)), DMA((2, 4 * nz)),
    ]
    return pl.pallas_call(
        backward_kernel,
        out_shape=[
            sd((blk, D), f32), sd((blk, D), bf16),
            sd((n_chunks, rows, 256), f32), sd((16, D), f32), sd((2, D), f32), sd((8, 128), f32),
        ],
        in_specs=[ANY] * 15 + [VMEM] * 3,
        out_specs=[ANY] * 2 + [VMEM] * 4,
        scratch_shapes=scratch,
        compiler_params=pltpu.CompilerParams(
            collective_id=1, has_side_effects=True, vmem_limit_bytes=63 * 2**20
        ),
        name="backward",
    )(*saved, r1, small, vec)


def finish_kernel(count, tokens_all, *refs):
    (
        total, vec_sum, pools, squares, in_own, in_other,
        wq, wo, w1, w2, vec, mq, sq, mo, so, m1, s1, m2, s2, mv, sv,
        pooled, in_grad, norm,
        wq_n, mq_n, sq_n, wo_n, mo_n, so_n, w1_n, m1_n, s1_n, w2_n, m2_n, s2_n, v_n, mv_n, sv_n,
    ) = refs
    mp = lax.axis_index("mp")
    y = mp // 2
    g_vec = vec_sum[0 : vec.shape[0], :]
    grad_norm = jnp.sqrt(
        jnp.sum(squares[...], keepdims=True) + jnp.sum(g_vec * g_vec, keepdims=True)
    )
    norm[...] = grad_norm
    factor = jnp.minimum(1.0, clip_limit(count, tokens_all) / (grad_norm + 1e-06))
    rates = matrix_rates(D, FF, DOC_LEN)

    def update(old, new, part, g, rate, decay):
        results = adam_update(old[0][part], g * factor, old[1][part], old[2][part], rate, decay)
        for ref, result in zip(new, results):
            ref[part] = result

    for j in range(3):
        update((wq, mq, sq), (wq_n, mq_n, sq_n), (j,), total[j], rates[0], weight_decay)
    update((wo, mo, so), (wo_n, mo_n, so_n), (slice(None),), total[3], rates[1], weight_decay)
    for c in range(4):
        part = (slice(None), slice(c * 256, c * 256 + 256))
        update((w1, m1, s1), (w1_n, m1_n, s1_n), part, total[4 + c], rates[2], weight_decay)
        update((w2, m2, s2), (w2_n, m2_n, s2_n), part, total[8 + c], rates[3], weight_decay)
    in_grad[y] = in_own[...]
    in_grad[1 - y] = in_other[...].astype(f32)
    update((vec, mv, sv), (v_n, mv_n, sv_n), (slice(None),), g_vec, vector_rate, 0.0)
    columns = pl.ds(pl.multiple_of(mp * 256, 256), 256)
    pooled[pl.ds(y, 1), :] = pools[0:1, columns]
    pooled[pl.ds(1 - y, 1), :] = pools[1:2, columns]


def finish(tokens_all, count, results, weights, moments):
    in_own, in_other, total, vec_sum, pools, squares = results
    out_shape = [
        jax.ShapeDtypeStruct((2, 256), f32),
        jax.ShapeDtypeStruct((2,) + in_own.shape, f32),
        jax.ShapeDtypeStruct((1, 1), f32),
    ]
    for w in weights:
        out_shape += [jax.ShapeDtypeStruct(w.shape, f32)] * 3
    args = (total, vec_sum, pools, squares, in_own, in_other) + weights + moments
    rows = total.shape[1]
    steps = min(4, rows // 8)

    def cut(array):
        shape = array.shape
        lead = (0,) * (len(shape) - 2)
        block = shape[:-2] + (shape[-2] // steps, shape[-1])
        return pl.BlockSpec(block, lambda i: lead + (i, 0))

    def whole(array):
        zeros = (0,) * len(array.shape)
        return pl.BlockSpec(array.shape, lambda i: zeros)

    vectors = 4
    in_specs = [cut(total)] + [whole(a) for a in args[1:4]] + [cut(a) for a in args[4:6]]
    in_specs += [cut(w) for w in weights[:vectors]] + [whole(weights[vectors])]
    in_specs += [cut(m) for m in moments[: 2 * vectors]] + [whole(m) for m in moments[2 * vectors :]]
    out_specs = [whole(out_shape[0]), cut(out_shape[1]), whole(out_shape[2])]
    out_specs += [cut(o) for o in out_shape[3 : 3 + 3 * vectors]]
    out_specs += [whole(o) for o in out_shape[3 + 3 * vectors :]]
    return pl.pallas_call(
        partial(finish_kernel, count, tokens_all),
        grid=(steps,),
        out_shape=out_shape,
        in_specs=in_specs,
        out_specs=out_specs,
        compiler_params=pltpu.CompilerParams(vmem_limit_bytes=60 * 2**20),
        name="finish",
    )(*args)


def local(
    tokens, out_cot, cls_offset, w_qkv, w_out, w_one, w_two, vectors,
    m_qkv, v_qkv, m_out, v_out, m_one, v_one, m_two, v_two, m_vec, v_vec,
):
    length = tokens.shape[1] * lax.axis_size("mp")
    tokens_all = tokens.shape[0] * length * lax.axis_size("dp")
    weights = (w_qkv.swapaxes(0, 1), w_out, w_one, w_two, vectors)
    *saved, r1, small = forward(tokens, out_cot, cls_offset, *weights)
    results = backward(saved, r1, small, vectors)
    pooled, input_grad, grad_norm, *updated = finish(
        tokens_all,
        4 * D * D + 2 * D * FF,
        results,
        weights,
        (m_qkv.swapaxes(0, 1), v_qkv.swapaxes(0, 1), m_out, v_out, m_one, v_one, m_two, v_two, m_vec, v_vec),
    )
    updated[:3] = [u.swapaxes(0, 1) for u in updated[:3]]
    return (pooled, input_grad, grad_norm.reshape(()), *updated)


def solution(mesh):
    rows, wide, flat, whole = P("dp", "mp", None), P("dp", None, "mp"), P("dp", "mp"), P()
    return jax.shard_map(
        local,
        mesh=mesh,
        in_specs=(rows, rows, P("dp", None), wide, flat, flat, flat, whole)
        + (wide, wide)
        + (flat,) * 6
        + (whole, whole),
        out_specs=(flat, rows, whole) + (wide,) * 3 + (flat,) * 9 + (whole,) * 3,
        check_vma=False,
    )
```

```python
from functools import partial
import math

import jax
import jax.numpy as jnp
from jax import lax
from jax.experimental import pallas as pl
from jax.experimental.pallas import tpu as pltpu
from jax.sharding import PartitionSpec as P

D = 1024
HD = 64
FF = 4096
DOC_LEN = 1024
CLS_GAP = 256
STEP = 10

MESH = pl.DeviceIdType.MESH
ANY = pl.BlockSpec(memory_space=pl.ANY)
VMEM = pl.BlockSpec(memory_space=pltpu.VMEM)
DMA = pltpu.SemaphoreType.DMA
f32 = jnp.float32
bf16 = jnp.bfloat16

norm_eps = 1e-05
beta_one = 0.9
beta_two = 0.999
adam_eps = 1e-08
weight_decay = 0.01
vector_rate = 0.4
contract_last = (((1,), (1,)), ((), ()))


def clip_limit(params_all, tokens_all):
    return 0.005 * math.sqrt(params_all * tokens_all)


def matrix_rates(model_width, hidden, length):
    out_fan = max(1, 3 * model_width // length)
    return (
        1.5 / math.sqrt(model_width),
        1.5 / math.sqrt(out_fan),
        1.5 / math.sqrt(model_width),
        1.5 / math.sqrt(hidden),
    )


def adam_update(parameter, gradient, first_old, second_old, step_rate, decay_rate):
    first_new = beta_one * first_old + (1.0 - beta_one) * gradient
    second_new = beta_two * second_old + (1.0 - beta_two) * gradient * gradient
    first_hat = first_new / (1.0 - beta_one**STEP)
    second_hat = second_new / (1.0 - beta_two**STEP)
    updated = parameter - step_rate * (
        first_hat / (jnp.sqrt(second_hat) + adam_eps) + decay_rate * parameter
    )
    return (updated, first_new, second_new)


class Place:
    def __init__(self):
        dp, mp = lax.axis_index("dp"), lax.axis_index("mp")
        self.z, self.x = dp // 2, dp % 2
        self.y, self.k = mp // 2, mp % 2

    def near(self, axis):
        z, x, y, k = self.z, self.x, self.y, self.k
        if axis == "x":
            x = 1 - x
        elif axis == "y":
            y = 1 - y
        else:
            k = 1 - k
        return (z * 2 + x, y * 2 + k)

    def along(self, j, nz):
        return ((self.z + j) % nz * 2 + self.x, self.y * 2 + self.k)


def greet(place, nz, axes="xyk"):
    barrier = pltpu.get_barrier_semaphore()
    for axis in axes:
        pl.semaphore_signal(barrier, inc=1, device_id=place.near(axis), device_id_type=MESH)
    if nz > 1:

        def one(j, carry):
            pl.semaphore_signal(barrier, inc=1, device_id=place.along(j, nz), device_id_type=MESH)
            return carry

        lax.fori_loop(1, nz, one, 0)
    pl.semaphore_wait(barrier, len(axes) + nz - 1)


def remote(src, dst, send, recv, where):
    return pltpu.make_async_remote_copy(
        src_ref=src, dst_ref=dst, send_sem=send, recv_sem=recv, device_id=where, device_id_type=MESH
    )


def each(start, stop, body):
    def one(j, carry):
        body(j)
        return carry

    lax.fori_loop(start, stop, one, 0)


def dot(a, b, dims=(((1,), (0,)), ((), ()))):
    return lax.dot_general(a, b, dims, preferred_element_type=f32)


class Gather:
    def __init__(self, place, own, full, send, recv, far, by_x):
        self.p, self.own, self.full, self.send, self.recv = place, own, full, send, recv
        self.far, self.by_x = far, by_x
        self.nz = full.shape[2]

    def to(self, kind, c, j, src, dst, where):
        n = self.recv.shape[1]
        if c < n:
            send, recv = self.send.at[kind, c % 8, j], self.recv.at[kind, c, j]
        else:
            send, recv = self.far.at[0, c - n, kind], self.far.at[1, c - n, kind]
        return remote(src, dst, send, recv, where)

    def along_z(self, c, j):
        p = self.p
        return self.to(
            0, c, j, self.own.at[c], self.full.at[c, p.y, p.z, p.x], p.along(j, self.nz)
        )

    def pass_xy(self, kind, c, j):
        p = self.p
        there = self.full.at[c, p.y, (p.z + self.nz - j) % self.nz, p.x]
        src = self.own.at[c] if isinstance(j, int) and j == 0 else there
        return self.to(kind, c, j, src, there, p.near("x" if kind == 1 else "y"))

    def pass_half(self, kind, c, j):
        p = self.p
        z = (p.z + self.nz - j) % self.nz
        if kind == 3:
            ref = self.full.at[c, p.y, z, 1 - p.x, :, pl.ds(0, 128)]
            return self.to(3, c, j, ref, ref, p.near("y"))
        ref = self.full.at[c, 1 - p.y, z, p.x]
        if c not in self.by_x:
            ref = ref.at[:, pl.ds(128, 128)]
        return self.to(4, c, j, ref, ref, p.near("x"))

    def halves(self, c):
        return (4,) if c in self.by_x else (3, 4)

    def stage(self, s, c):
        nz = self.nz
        if s == 0:
            self.pass_xy(1, c, 0).start()
            self.pass_xy(2, c, 0).start()
            each(1, nz, lambda j: self.along_z(c, j).start())
        elif s == 1:

            def one(j):
                self.along_z(c, j).wait()
                self.pass_xy(1, c, j).start()
                self.pass_xy(2, c, j).start()

            each(1, nz, one)
        elif s == 2:
            def two(j):
                for kind in (2, 1):
                    self.pass_xy(kind, c, j).wait()
                    if kind + 2 in self.halves(c):
                        self.pass_half(kind + 2, c, j).start()

            two(0)

            each(1, nz, two)
        else:

            def three(j):
                for kind in self.halves(c):
                    self.pass_half(kind, c, j).wait()

            each(0, nz, three)


class Far:
    def __init__(self, gather, c, sends, recvs):
        self.g, self.c, self.sends, self.recvs = gather, c, sends, recvs

    def piece(self, i):
        p = self.g.p
        x = 1 - p.x if i in (1, 3) else p.x
        y = 1 - p.y if i in (2, 3) else p.y
        return self.g.full.at[self.c, y, p.z, x]

    def copy(self, i, j):
        g = self.g
        ref = self.piece(i)
        src = g.own.at[self.c] if i == 0 else ref
        return remote(src, ref, self.sends.at[i, j], self.recvs.at[i, j], g.p.along(j, g.nz))

    def step(self, s):
        g, c = self.g, self.c
        if s == 0:
            g.pass_xy(1, c, 0).start()
            g.pass_xy(2, c, 0).start()
        elif s == 1:
            for kind in (1, 2):
                g.pass_xy(kind, c, 0).wait()
                g.pass_half(kind + 2, c, 0).start()
        elif s == 2:
            for kind in (3, 4):
                g.pass_half(kind, c, 0).wait()
        elif s < 7:
            each(1, g.nz, lambda j: self.copy(s - 3, j).start())
        else:

            def last(j):
                for i in range(4):
                    self.copy(i, j).wait()

            each(1, g.nz, last)


class Pump:
    def __init__(self, mover, times, order):
        self.mover, self.times, self.order, self.t = mover, times, order, 0

    def step(self):
        for s in self.order:
            for c, when in enumerate(self.times):
                if when[s] == self.t:
                    self.mover.stage(s, c)
        self.t += 1


class Saver:
    def __init__(self, sems):
        self.sems, self.list = sems, []

    def start(self, src, dst):
        copy = pltpu.make_async_copy(src, dst, self.sems.at[len(self.list)])
        copy.start()
        self.list.append(copy)
        return copy

    def wait(self, *done):
        for copy in self.list:
            if all(copy is not other for other in done):
                copy.wait()


def turn(block):
    return block.astype(f32).T.astype(bf16)


def normalize(z):
    centered = z - jnp.mean(z, axis=-1, keepdims=True)
    r = lax.rsqrt(jnp.mean(centered * centered, axis=-1, keepdims=True) + norm_eps)
    return centered * r, r


def norm_backward(cot, xh, r, gain):
    e = cot * gain
    return r * (
        e - jnp.mean(e, axis=-1, keepdims=True) - xh * jnp.mean(e * xh, axis=-1, keepdims=True)
    )


def head_mask(h, dim, shape):
    lane = lax.broadcasted_iota(jnp.int32, shape, dim)
    return (lane // HD) == h


def keep_head(block, h, dim):
    return jnp.where(head_mask(h, dim, block.shape), block, jnp.zeros_like(block))


def col_sum(a):
    return jnp.sum(a, axis=0, keepdims=True)


FWD_SAVES = 40


def forward_kernel(
    x_ref, cot_ref, cls, wq, wo, w1, w2, vec,
    w_all, q_o, k_o, v_o, kt_o, xt_o, o_o, l_o, yt_o, g_o, gp_o, xh_o, df_o, dft_o, dz_o,
    r_o, small,
    shard, x_v, w_v, q_s, k_s, v_s, kt_s, vt_s, o_s, l_s, xt_s, y_s, yt_s, g_s, gp_s, acc, y1_s,
    xh_s, sb, rb, cot_v, cot_r,
    send, recv, far_xy, far_send, far_recv, side, save_sems, load_sems,
):
    p = Place()
    nz = w_all.shape[2]
    length = xt_s.shape[1]
    blk_rows = x_v.shape[1]
    saver = Saver(save_sems)
    keep_cot = saver.start(cot_ref.at[p.y], cot_v)
    load_cot = saver.start(cot_ref.at[1 - p.y], y1_s.at[0])
    for j in range(3):
        shard[j] = wq[j].astype(bf16)
    greet(p, nz)
    gather = Gather(p, shard, w_all, send, recv, far_xy, (0, 1, 5, 6))
    early = [(max(0, c - 1), c + 1, c + 2, c + 3) for c in range(3)]
    later = [(c - 2, c + 1, c + 3, c + 5) for c in range(3, w_all.shape[0] - 2)]
    pump = Pump(gather, early + later, (2, 0, 1, 3))
    far = [Far(gather, 10 + i, far_send.at[i], far_recv.at[i]) for i in range(2)]
    plan = {1:[(0,0),(1,0)],3:[(0,1),(1,1),(0,3)],4:[(1,3)],5:[(0,2),(1,2),(0,4)],6:[(1,4)],7:[(0,5)],8:[(1,5)],9:[(0,6)],10:[(1,6)]}

    def step():
        for i, s in plan.get(pump.t, ()):
            far[i].step(s)
        pump.step()

    n_side = [0]

    def beside(src, dst, axis):
        i = n_side[0]
        n_side[0] += 1
        copy = remote(src, dst, side.at[0, i], side.at[1, i], p.near(axis))
        copy.start()
        return copy

    def own(s):
        return (p.y if s == 0 else 1 - p.y) * 2 + p.k

    def other(s):
        return (p.y if s == 0 else 1 - p.y) * 2 + 1 - p.k

    loads = {}

    def load(c):
        loads[c] = pltpu.make_async_copy(w_all.at[c], w_v.at[c], load_sems.at[c])
        loads[c].start()

    def weight(c, b):
        return w_v[c, b].reshape(-1, 256)

    def rows_of(i, n):
        return pl.ds(pl.multiple_of(i * n, n), n)

    mine = x_v.at[own(0)]
    swap_x = beside(x_ref.at[1 - p.y], mine, "y")
    keep_x = saver.start(x_ref.at[p.y], mine)
    give_x = beside(x_ref.at[p.y], mine, "k")
    step()
    shard[3] = wo[...].astype(bf16)
    for c in range(4):
        shard[4 + c] = w1[:, c * 256 : c * 256 + 256].astype(bf16)
        shard[8 + c] = w2[:, c * 256 : c * 256 + 256].astype(bf16)
    keep_w = saver.start(shard, w_all.at[:, p.y, p.z, p.x])
    load_cot.wait()
    sb[1, 0] = y1_s[0].astype(bf16)
    step()
    swap_x.wait()
    pass_x = beside(x_v.at[own(1)], x_v.at[own(1)], "k")
    step()
    keep_x.wait()
    keep_w.wait()
    give_x.wait()
    pass_x.wait()
    half_rows = 2 * blk_rows

    def project(j):
        for b in range(2):
            w = weight(j, b)

            def tile(i):
                rows = rows_of(i, half_rows)
                x = x_v[pl.ds(2 * i, 2)].reshape(half_rows, -1)
                got = dot(x, w)
                if j != 1:
                    bias = pl.ds(pl.multiple_of((2 * b + p.k) * 256, 256), 256)
                    got = got + vec[j // 2 : j // 2 + 1, bias]
                got = got.astype(bf16)
                if j == 0:
                    got = got * bf16(0.125)
                dst = (q_s, k_s, v_s)[j]
                dst[2 * b, rows, :] = got[:, :128]
                dst[2 * b + 1, rows, :] = got[:, 128:]
                if j > 0:
                    turned = turn(got)
                    dst = (None, kt_s, vt_s)[j]
                    dst[2 * b, :, rows] = turned[:128]
                    dst[2 * b + 1, :, rows] = turned[128:]

            each(0, 2, tile)

    def flip(i):
        for s in range(4):
            cols = pl.ds(s * 256, 256)
            xt_s[cols, rows_of(i, blk_rows)] = turn(x_v[i, :, cols])

    each(0, 4, flip)
    save_xt = saver.start(xt_s, xt_o)
    step()
    load(0)
    step()
    load(1)
    loads[0].wait()
    project(0)
    step()
    load(2)
    loads[1].wait()
    project(1)
    swap_cot = beside(sb.at[1, 0], cot_r, "y")
    step()
    loads[2].wait()
    project(2)

    q_tile = 256

    def attend(pair):
        b, lanes = pair // 2, pl.ds(pair % 2 * 128, 128)

        def tile(i):
            rows = rows_of(i, q_tile)
            q2, k2, vt2 = q_s[pair, rows, :], k_s[pair], vt_s[pair]
            mixed = None
            for h in range(2):
                scores = dot(k2, keep_head(q2, h, 1), contract_last)
                top = jnp.max(scores, axis=0, keepdims=True)
                raised = jnp.exp(scores - top)
                total = col_sum(raised)
                shares = (raised * (1.0 / total)).astype(bf16)
                l_s[2 * pair + h, :, rows] = top + jnp.log(total)
                one = dot(keep_head(vt2, h, 0), shares)
                mixed = one if mixed is None else mixed + one
            o_s[b, rows, lanes] = mixed.T.astype(bf16)

        each(0, length // q_tile, tile)

    for pair in range(4):
        attend(pair)
        step()
        if pair > 0:
            load(2 + pair)
    for src, dst in ((q_s, q_o), (k_s, k_o), (v_s, v_o), (kt_s, kt_o), (o_s, o_o), (l_s, l_o)):
        saver.start(src, dst)

    loads[3].wait()

    def out_rows(blk):
        rows = rows_of(blk, blk_rows)
        acc[blk] = dot(o_s[0, rows, :], weight(3, 0), contract_last) + dot(
            o_s[1, rows, :], weight(3, 1), contract_last
        )

    def give_half(call, compute):
        sent = []
        for s in range(2):
            compute(other(s))
            sb[call, s] = acc[other(s)].astype(bf16)
            sent.append(beside(sb.at[call, s], rb.at[call, s], "k"))
        for s in range(2):
            compute(own(s))
        return sent

    sent = give_half(0, out_rows)
    shared = []
    for s in range(2):
        sent[s].wait()
        z = x_v[own(s)].astype(f32) + (acc[own(s)] + rb[0, s].astype(f32)) + vec[2:3, :]
        xh, r = normalize(z)
        xh_s[s] = xh
        r_o[s] = r
        y1 = xh * vec[3:4, :] + vec[4:5, :]
        y1_s[s] = y1
        y_s[own(s)] = y1.astype(bf16)
        shared.append(beside(y_s.at[own(s)], y_s.at[own(s)], "k"))
    saver.start(xh_s, xh_o)
    for copy in shared:
        copy.wait()

    def flip_y(i):
        for s in range(4):
            cols = pl.ds(s * 256, 256)
            yt_s[cols, rows_of(i, blk_rows)] = turn(y_s[i, :, cols])

    each(0, 4, flip_y)
    saver.start(yt_s, yt_o)

    def ffn_up(c):
        for b in range(2):
            w = weight(4 + c, b)
            bias = vec[pl.ds(8 + 2 * b + p.k, 1), c * 256 : c * 256 + 256]

            def tile(i):
                rows = rows_of(i, half_rows)
                u = dot(y_s[pl.ds(2 * i, 2)].reshape(half_rows, -1), w) + bias
                share = 0.5 * (1.0 + lax.erf(u * 0.7071067811865476))
                g_s[2 * c + b, rows, :] = (u * share).astype(bf16)
                gp_s[2 * c + b, rows, :] = share + u * (
                    jnp.exp(-0.5 * (u * u)) * 0.3989422804014327
                )

            each(0, 2, tile)
        saver.start(g_s.at[2 * c : 2 * c + 2], g_o.at[2 * c : 2 * c + 2])
        saver.start(gp_s.at[2 * c : 2 * c + 2], gp_o.at[2 * c : 2 * c + 2])

    def down_rows(c, blk):
        rows = rows_of(blk, blk_rows)
        got = dot(g_s[2 * c, rows, :], weight(8 + c, 0), contract_last) + dot(
            g_s[2 * c + 1, rows, :], weight(8 + c, 1), contract_last
        )
        acc[blk] = got if c == 0 else acc[blk] + got

    step()
    load(6)
    loads[4].wait()
    ffn_up(0)
    step()
    load(7)
    loads[5].wait()
    ffn_up(1)
    step()
    load(8)
    loads[6].wait()
    ffn_up(2)
    step()
    load(9)
    far[0].step(7)
    load(10)
    loads[7].wait()
    ffn_up(3)
    far[1].step(7)
    load(11)
    for c in range(3):
        loads[8 + c].wait()
        each(0, 4, partial(down_rows, c))
    loads[11].wait()
    keep_cot.wait()
    swap_cot.wait()
    save_xt.wait()
    sent = give_half(1, partial(down_rows, 3))
    shared = []
    totals = [0.0, 0.0, 0.0, 0.0]
    for s in range(2):
        sent[s].wait()
        z = y1_s[s] + (acc[own(s)] + rb[1, s].astype(f32)) + vec[5:6, :]
        xh, r = normalize(z)
        cot = cot_v[...] if s == 0 else cot_r[...].astype(f32)
        dz = norm_backward(cot, xh, r, vec[6:7, :])
        df = dz.astype(bf16)
        x_v[own(s)] = df
        shared.append(beside(x_v.at[own(s)], x_v.at[own(s)], "k"))
        xt_s[:, rows_of(own(s), blk_rows)] = turn(df)
        cols = xt_s.at[:, rows_of(own(s), blk_rows)]
        shared.append(beside(cols, cols, "k"))
        y1_s[s] = dz
        out = xh * vec[6:7, :] + vec[7:8, :]
        row = lax.broadcasted_iota(jnp.int32, (blk_rows, 1), 0) + own(s) * blk_rows
        hits = [row == cls[p.y, j] + j * CLS_GAP for j in range(cls.shape[1])]
        picks = sum(hit.astype(f32) for hit in hits) / len(hits)
        for i, term in enumerate((dz, cot * xh, cot, picks * out)):
            totals[i] = totals[i] + col_sum(term)
    for i in range(4):
        small[i : i + 1, :] = totals[i]
    saver.start(y1_s, dz_o)
    for copy in shared:
        copy.wait()
    saver.start(x_v, df_o)
    saver.start(xt_s, dft_o)
    saver.wait(keep_x, keep_w, keep_cot, load_cot, save_xt)


def forward(x_loc, cot, cls, w_qkv, w_out, w_one, w_two, vec):
    nz = lax.axis_size("dp") // 2
    n_chunks, rows = 12, w_out.shape[0]
    blk = x_loc.shape[1]
    length = 4 * blk
    full = (n_chunks, 2, nz, 2, rows, 256)
    sd = jax.ShapeDtypeStruct
    outs = [
        sd(full, bf16),
        sd((4, length, 128), bf16),
        sd((4, length, 128), bf16),
        sd((4, length, 128), bf16),
        sd((4, 128, length), bf16),
        sd((D, length), bf16),
        sd((2, length, 256), bf16),
        sd((8, 1, length), f32),
        sd((D, length), bf16),
        sd((8, length, 256), bf16),
        sd((8, length, 256), f32),
        sd((2, blk, D), f32),
        sd((4, blk, D), bf16),
        sd((D, length), bf16),
        sd((2, blk, D), f32),
        sd((2, blk, 1), f32),
        sd((8, D), f32),
    ]
    V = pltpu.VMEM
    scratch = [
        V((n_chunks, rows, 256), bf16), V((4, blk, D), bf16), V(full, bf16),
        V((4, length, 128), bf16), V((4, length, 128), bf16), V((4, length, 128), bf16),
        V((4, 128, length), bf16), V((4, 128, length), bf16),
        V((2, length, 256), bf16), V((8, 1, length), f32),
        V((D, length), bf16), V((4, blk, D), bf16), V((D, length), bf16),
        V((8, length, 256), bf16), V((8, length, 256), f32),
        V((4, blk, D), f32), V((2, blk, D), f32), V((2, blk, D), f32),
        V((2, 2, blk, D), bf16), V((2, 2, blk, D), bf16),
        V((blk, D), f32), V((blk, D), bf16),
        DMA((5, 8, nz)), DMA((5, n_chunks - 2, nz)), DMA((2, 2, 5)), DMA((2, 4, nz)), DMA((2, 4, nz)), DMA((2, 16)), DMA((FWD_SAVES,)), DMA((n_chunks,)),
    ]
    return pl.pallas_call(
        forward_kernel,
        out_shape=outs,
        in_specs=[ANY] * 2 + [pl.BlockSpec(memory_space=pltpu.SMEM)] + [VMEM] * 5,
        out_specs=[ANY] * 15 + [VMEM] * 2,
        scratch_shapes=scratch,
        compiler_params=pltpu.CompilerParams(
            collective_id=0, has_side_effects=True, vmem_limit_bytes=62 * 2**20
        ),
        name="forward",
    )(x_loc, cot, cls, w_qkv, w_out, w_one, w_two, vec)


class Reduce:
    def __init__(self, place, part, total, order, ra, rb, rx, ry, rz, send, recv):
        self.p, self.part, self.total, self.order = place, part, total, order
        self.ra, self.rb, self.rx, self.ry, self.rz = ra, rb, rx, ry, rz
        self.send, self.recv = send, recv
        self.nz = part.shape[2]

    def to(self, kind, r, j, src, dst, where):
        return remote(src, dst, self.send.at[kind, r % 4, j], self.recv.at[kind, r % 8, j], where)

    def copy(self, kind, r, z):
        p, a, b = self.p, pl.ds(0, 128), pl.ds(128, 128)
        part, slot = self.part.at[r % 5], r % 6
        if kind == 0:
            src, dst, axis = part.at[1 - p.y, z, 1 - p.x, :, a], self.ra.at[r % 8, z], "y"
        elif kind == 1:
            src, dst, axis = part.at[1 - p.y, z, 1 - p.x, :, b], self.rb.at[r % 8, z], "x"
        elif kind == 2:
            src, dst, axis = self.ra.at[r % 8, z], self.rx.at[slot, z, :, a], "x"
        elif kind == 3:
            src, dst, axis = self.rb.at[r % 8, z], self.ry.at[slot, z, :, b], "y"
        elif kind == 5:
            src, dst, axis = part.at[p.y, z, 1 - p.x, :, b], self.rx.at[slot, z, :, b], "x"
        else:
            src, dst, axis = part.at[1 - p.y, z, p.x, :, a], self.ry.at[slot, z, :, a], "y"
        return self.to(kind, r, z, src, dst, p.near(axis))

    def send_z(self, r, j):
        p = self.p
        z = (p.z + j) % self.nz
        return self.to(4, r, j, self.rx.at[r % 6, z], self.rz.at[r % 6, j], p.along(j, self.nz))

    def stage(self, s, r):
        p, nz, slot = self.p, self.nz, r % 6
        part, chunk = self.part.at[r % 5], self.order[r]
        if s == 0:

            def zero(z):
                self.copy(0, r, z).start()
                self.copy(1, r, z).start()

            each(0, nz, zero)
        elif s == 1:

            def one(z):
                self.copy(0, r, z).wait()
                self.copy(1, r, z).wait()
                self.ra[r % 8, z] = (
                    self.ra[r % 8, z].astype(f32) + part[p.y, z, 1 - p.x, :, 0:128].astype(f32)
                ).astype(bf16)
                self.rb[r % 8, z] = (
                    self.rb[r % 8, z].astype(f32) + part[1 - p.y, z, p.x, :, 128:256].astype(f32)
                ).astype(bf16)
                for kind in (2, 3, 5, 6):
                    self.copy(kind, r, z).start()

            each(0, nz, one)
        elif s == 2:

            def add(z):
                for kind in (2, 3, 5, 6):
                    self.copy(kind, r, z).wait()
                return (
                    part[p.y, z, p.x].astype(f32)
                    + self.rx[slot, z].astype(f32)
                    + self.ry[slot, z].astype(f32)
                )

            def two(j):
                z = (p.z + j) % nz
                self.rx[slot, z] = add(z).astype(bf16)
                self.send_z(r, j).start()

            each(1, nz, two)
            self.total[chunk] = add(p.z)
        else:

            def three(j):
                self.send_z(r, j).wait()
                self.total[chunk] += self.rz[slot, j].astype(f32)

            each(1, nz, three)


def backward_kernel(
    w_all, q_i, k_i, v_i, kt_i, xt_i, o_i, l_i, yt_i, g_i, gp_i, xh_i, df_i, dft_i, dz_i,
    r1, small, vec,
    in_own, in_other,
    total, vec_sum, pools, squares,
    w_v, g_s, gp_v, df_s, dft_s, du_s, dp_s, t_s, acc, xh_s, dz_s, o_s, kt_s, l_s,
    sb, rb, dk_s, dv_s, db_s, part, ra, rb_r, rx, ry, rz, vs, vr, vz, qs, qr, qz,
    send, recv, side, load_sems, w_sems, z_sems, q_sems,
):
    p = Place()
    nz = w_all.shape[2]
    length = dft_s.shape[1]
    blk_rows = df_s.shape[1]
    half_rows = 2 * blk_rows

    loader = Saver(load_sems)
    n_side = [0]

    def beside(src, dst, axis):
        i = n_side[0]
        n_side[0] += 1
        copy = remote(src, dst, side.at[0, i], side.at[1, i], p.near(axis))
        copy.start()
        return copy

    def own(s):
        return (p.y if s == 0 else 1 - p.y) * 2 + p.k

    def other(s):
        return (p.y if s == 0 else 1 - p.y) * 2 + 1 - p.k

    def rows_of(i, n):
        return pl.ds(pl.multiple_of(i * n, n), n)

    n_w = [0]

    def load_w(c, slot):
        copy = pltpu.make_async_copy(w_all.at[c], w_v.at[slot], w_sems.at[n_w[0]])
        n_w[0] += 1
        copy.start()
        return copy

    def weight(slot, b):
        return w_v[slot, b].reshape(-1, 256)

    got_dft = loader.start(dft_i, dft_s)
    got_g = [loader.start(g_i.at[2 * c : 2 * c + 2], g_s.at[2 * c : 2 * c + 2]) for c in range(4)]
    got_df = loader.start(df_i, df_s)
    got_w2 = [load_w(8 + c, c) for c in range(4)]
    got_gp = [loader.start(gp_i.at[i], gp_v.at[i]) for i in range(2)]
    got_w1 = [load_w(4 + c, 4 + c) for c in range(4)]
    got_yt = loader.start(yt_i, t_s)
    got_xh = loader.start(xh_i, xh_s)
    got_dz = loader.start(dz_i, dz_s)
    got_o = loader.start(o_i, o_s)
    got_kt = loader.start(kt_i, kt_s)
    got_l = loader.start(l_i, l_s)
    barrier = pltpu.get_barrier_semaphore()
    pl.semaphore_signal(barrier, inc=1, device_id=p.near("k"), device_id_type=MESH)

    def hello(j):
        there = ((p.z * 2 + p.x) * 2 + p.y + j) % (4 * nz)
        pl.semaphore_signal(
            barrier, inc=1, device_id=(there // 2, there % 2 * 2 + p.k), device_id_type=MESH
        )

    each(1, 4 * nz, hello)
    pl.semaphore_wait(barrier, 4 * nz)
    order = (8, 9, 10, 11, 4, 5, 6, 7, 3, 0, 1, 2)
    reduce = Reduce(p, part, total, order, ra, rb_r, rx, ry, rz, send, recv)
    pump = Pump(reduce, [(c, c + 2, c + 4, c + 5) for c in range(len(order))], (1, 2, 0, 3))

    def into_part(r, left, right):
        for b in range(2):

            def tile(i):
                got = dot(left[rows_of(i, half_rows), :], right(b)).astype(bf16)
                part[r % 5, b, pl.ds(i * (nz // 2), nz // 2)] = got.reshape(
                    (nz // 2,) + part.shape[3:]
                )

            each(0, 2, tile)

    def grad_two(c):
        got_g[c].wait()
        into_part(c, dft_s, lambda b: g_s[2 * c + b])

    def grad_pre(c):
        got_w2[c].wait()
        for b in range(2):
            i = 2 * c + b
            got_gp[i].wait()
            w = weight(c, b)
            db_s[i] = jnp.zeros_like(db_s[i])

            def tile(t):
                rows = rows_of(t, half_rows)
                hidden = dot(df_s[pl.ds(2 * t, 2)].reshape(half_rows, -1), w)
                pre = (hidden * gp_v[i % 2, rows, :]).astype(bf16)
                du_s[i, rows, :] = pre
                db_s[i] += col_sum(pre.astype(f32))

            each(0, 2, tile)
            if i + 2 < 8:
                got_gp.append(loader.start(gp_i.at[i + 2], gp_v.at[i % 2]))

    def one_rows(blk):
        rows = rows_of(blk, blk_rows)
        got = None
        for c in range(4):
            for b in range(2):
                term = dot(du_s[2 * c + b, rows, :], weight(4 + c, b), contract_last)
                got = term if got is None else got + term
        acc[blk] = got

    def x_rows(blk):
        rows = rows_of(blk, blk_rows)
        got = None
        for j in range(3):
            for b in range(2):
                term = dot(dp_s[2 * j + b, rows, :], weight(j, b), contract_last)
                got = term if got is None else got + term
        acc[blk] = got

    def give_half(call, compute):
        sent = []
        for s in range(2):
            compute(other(s))
            sb[call, s] = acc[other(s)].astype(bf16)
            sent.append(beside(sb.at[call, s], rb.at[call, s], "k"))
        for s in range(2):
            compute(own(s))
        return sent

    got_dft.wait()
    grad_two(0)
    pump.step()
    grad_two(1)
    got_df.wait()
    grad_pre(0)
    grad_pre(1)
    pump.step()
    grad_two(2)
    grad_pre(2)
    pump.step()
    grad_two(3)
    grad_pre(3)
    got_w = [load_w(c, c) for c in range(4)]
    pump.step()
    got_yt.wait()

    def grad_one(c):
        into_part(4 + c, t_s, lambda b: du_s[2 * c + b])

    grad_one(0)
    pump.step()
    for copy in got_w1:
        copy.wait()
    lo, hi = pl.ds(0, 128), pl.ds(128, 128)
    got_q = loader.start(q_i, g_s.at[0:4, :, lo])
    got_k = loader.start(k_i, g_s.at[0:4, :, hi])
    got_v = loader.start(v_i, g_s.at[4:8, :, lo])
    sent = give_half(0, one_rows)
    got_xh.wait()
    got_dz.wait()
    shared = []
    sums = [0.0, 0.0, 0.0]
    for s in range(2):
        sent[s].wait()
        dy = dz_s[s] + (acc[own(s)] + rb[0, s].astype(f32))
        xh = xh_s[s]
        dz = norm_backward(dy, xh, r1[s], vec[3:4, :])
        da = dz.astype(bf16)
        df_s[own(s)] = da
        shared.append(beside(df_s.at[own(s)], df_s.at[own(s)], "k"))
        cols = dft_s.at[:, rows_of(own(s), blk_rows)]
        cols[...] = turn(da)
        shared.append(beside(cols, cols, "k"))
        dz_s[s] = dz
        for i, term in enumerate((dz, dy * xh, dy)):
            sums[i] = sums[i] + col_sum(term)
    grad_one(1)
    pump.step()
    for copy in shared:
        copy.wait()
    got_w[3].wait()
    for b in range(2):
        w = weight(3, b)

        def tile(t):
            rows = rows_of(t, half_rows)
            got = dot(df_s[pl.ds(2 * t, 2)].reshape(half_rows, -1), w).astype(bf16)
            g_s[4 + 2 * b, rows, 128:256] = got[:, :128]
            g_s[5 + 2 * b, rows, 128:256] = got[:, 128:]

        each(0, 2, tile)
    got_q.wait()
    got_k.wait()
    got_v.wait()
    got_kt.wait()
    got_l.wait()

    q_tile = 256
    vs[...] = jnp.zeros_like(vs)
    vs[0, 12:13, :] = small[3:4, :]
    for i in range(3):
        vs[0, 2 + i : 3 + i, :] = sums[i]
        vs[0, 5 + i : 6 + i, :] = small[i : i + 1, :]

    def attend(pair):
        b, lanes = pair // 2, slice(pair % 2 * 128, pair % 2 * 128 + 128)
        dk_s[...] = jnp.zeros_like(dk_s)
        dv_s[...] = jnp.zeros_like(dv_s)

        def tile(i):
            rows = rows_of(i, q_tile)
            q2, do2 = g_s[pair, rows, 0:128], g_s[4 + pair, rows, 128:256]
            k2, v2, kt2 = g_s[pair, :, 128:256], g_s[4 + pair, :, 0:128], kt_s[pair]
            dqt = None
            for h in range(2):
                qh, doh = keep_head(q2, h, 1), keep_head(do2, h, 1)
                scores = dot(k2, qh, contract_last)
                shares = jnp.exp(scores - l_s[2 * pair + h, :, rows])
                dshares = dot(v2, doh, contract_last)
                mean = col_sum(shares * dshares)
                dscores = (shares * (dshares - mean)).astype(bf16)
                dv_s[...] += dot(shares.astype(bf16), doh)
                dk_s[...] += dot(dscores, qh)
                one = dot(keep_head(kt2, h, 0), dscores)
                dqt = one if dqt is None else dqt + one
            dq = (dqt * 0.125).T.astype(bf16)
            dp_s[b, rows, lanes] = dq

        each(0, length // q_tile, tile)
        dp_s[2 + b, :, lanes] = dk_s[...].astype(bf16)
        dp_s[4 + b, :, lanes] = dv_s[...].astype(bf16)
        place = pl.ds(pl.multiple_of((2 * b + p.k) * 256 + pair % 2 * 128, 128), 128)
        vs[0, 0:1, place] = col_sum(dp_s[b, :, lanes].astype(f32))
        vs[0, 1:2, place] = col_sum(dp_s[4 + b, :, lanes].astype(f32))

    for pair in range(4):
        attend(pair)
        if pair < 2:
            grad_one(2 + pair)
            pump.step()
        elif pair == 2:
            got_xt = loader.start(xt_i, t_s)
            got_o.wait()
            into_part(8, dft_s, lambda b: o_s[b])
            pump.step()
    for c in range(4):
        for b in range(2):
            vs[0, pl.ds(8 + 2 * b + p.k, 1), c * 256 : c * 256 + 256] = db_s[2 * c + b]
    vec_copy = beside(vs.at[0], vr.at[0], "k")
    got_xt.wait()

    def grad_qkv(j):
        into_part(9 + j, t_s, lambda b: dp_s[2 * j + b])

    for c in range(3):
        got_w[c].wait()
    grad_qkv(0)
    pump.step()
    sent = give_half(1, x_rows)
    sent[1].wait()
    dz_s[1] += acc[own(1)] + rb[1, 1].astype(f32)
    sb[0, 0] = dz_s[1].astype(bf16)
    swap_in = beside(sb.at[0, 0], in_other, "y")
    sent[0].wait()
    dz_s[0] += acc[own(0)] + rb[1, 0].astype(f32)
    keep_in = loader.start(dz_s.at[0], in_own)
    vec_copy.wait()
    vs[1] = vs[0] + vr[0]
    vec_copy = beside(vs.at[1], vr.at[1], "y")
    grad_qkv(1)
    pump.step()
    vec_copy.wait()
    pools[0:1, :] = vs[1, 12:13, :]
    pools[1:2, :] = vr[1, 12:13, :]
    vs[2] = vs[1] + vr[1]
    vec_copy = beside(vs.at[2], vr.at[2], "x")
    grad_qkv(2)
    pump.step()
    vec_copy.wait()
    vs[3] = vs[2] + vr[2]

    def along(src, into, j):
        return remote(
            src, into.at[p.z], z_sems.at[0, j], z_sems.at[1, j], p.along(j, nz)
        )

    def from_z(src, into, j):
        return remote(
            src,
            into.at[(p.z + nz - j) % nz],
            z_sems.at[0, j],
            z_sems.at[1, j],
            p.along(j, nz),
        )

    vz[p.z] = vs[3]
    each(1, nz, lambda j: along(vs.at[3], vz, j).start())
    pump.step()
    each(1, nz, lambda j: from_z(vs.at[3], vz, j).wait())
    vec_sum[...] = vz[0]

    def add_vec(z):
        vec_sum[...] += vz[z]

    each(1, nz, add_vec)
    swap_in.wait()
    while pump.t <= max(when[3] for when in pump.times):
        pump.step()

    tile8 = jnp.zeros(qs.shape[1:], f32)
    for c in range(len(order)):
        t = total[c]
        t = jnp.sum((t * t).reshape(-1, 8, 256), axis=0)
        tile8 = tile8 + t[:, :128] + t[:, 128:]
    qs[0] = tile8
    beside(qs.at[0], qr, "k").wait()
    qs[1] = qs[0] + qr[...]
    chips, me = 4 * nz, (p.z * 2 + p.x) * 2 + p.y

    def to_chip(j, into):
        there = (me + j) % chips
        return remote(
            qs.at[1], qz.at[into], q_sems.at[0, j], q_sems.at[1, j], (there // 2, there % 2 * 2 + p.k)
        )

    qz[me] = qs[1]
    each(1, chips, lambda j: to_chip(j, me).start())
    each(1, chips, lambda j: to_chip(j, (me + chips - j) % chips).wait())
    squares[...] = qz[0]

    def add_square(i):
        squares[...] += qz[i]

    each(1, chips, add_square)
    keep_in.wait()


def backward(saved, r1, small, vec):
    w_all = saved[0]
    n_chunks, _, nz, _, rows, _ = w_all.shape
    length = saved[5].shape[1]
    blk = length // 4
    sd = jax.ShapeDtypeStruct
    V = pltpu.VMEM
    scratch = [
        V((8,) + w_all.shape[1:], bf16), V((8, length, 256), bf16), V((2, length, 256), f32),
        V((4, blk, D), bf16), V((D, length), bf16), V((8, length, 256), bf16),
        V((6, length, 256), bf16), V((D, length), bf16), V((4, blk, D), f32),
        V((2, blk, D), f32), V((2, blk, D), f32), V((2, length, 256), bf16),
        V((4, 128, length), bf16), V((8, 1, length), f32),
        V((2, 2, blk, D), bf16), V((2, 2, blk, D), bf16),
        V((length, 128), f32), V((length, 128), f32), V((8, 1, 256), f32),
        V((5, 2, nz, 2, rows, 256), bf16),
        V((8, nz, rows, 128), bf16), V((8, nz, rows, 128), bf16),
        V((6, nz, rows, 256), bf16), V((6, nz, rows, 256), bf16), V((6, nz, rows, 256), bf16),
        V((4, 16, D), f32), V((3, 16, D), f32), V((nz, 16, D), f32),
        V((2, 8, 128), f32), V((8, 128), f32), V((4 * nz, 8, 128), f32),
        DMA((7, 4, nz)), DMA((7, 8, nz)), DMA((2, 20)), DMA((32,)), DMA((12,)), DMA((2, nz)), DMA((2, 4 * nz)),
    ]
    return pl.pallas_call(
        backward_kernel,
        out_shape=[
            sd((blk, D), f32), sd((blk, D), bf16),
            sd((n_chunks, rows, 256), f32), sd((16, D), f32), sd((2, D), f32), sd((8, 128), f32),
        ],
        in_specs=[ANY] * 15 + [VMEM] * 3,
        out_specs=[ANY] * 2 + [VMEM] * 4,
        scratch_shapes=scratch,
        compiler_params=pltpu.CompilerParams(
            collective_id=1, has_side_effects=True, vmem_limit_bytes=63 * 2**20
        ),
        name="backward",
    )(*saved, r1, small, vec)


def finish_kernel(count, tokens_all, *refs):
    (
        total, vec_sum, pools, squares, in_own, in_other,
        wq, wo, w1, w2, vec, mq, sq, mo, so, m1, s1, m2, s2, mv, sv,
        pooled, in_grad, norm,
        wq_n, mq_n, sq_n, wo_n, mo_n, so_n, w1_n, m1_n, s1_n, w2_n, m2_n, s2_n, v_n, mv_n, sv_n,
    ) = refs
    mp = lax.axis_index("mp")
    y = mp // 2
    g_vec = vec_sum[0 : vec.shape[0], :]
    grad_norm = jnp.sqrt(
        jnp.sum(squares[...], keepdims=True) + jnp.sum(g_vec * g_vec, keepdims=True)
    )
    norm[...] = grad_norm
    factor = jnp.minimum(1.0, clip_limit(count, tokens_all) / (grad_norm + 1e-06))
    rates = matrix_rates(D, FF, DOC_LEN)

    def update(old, new, part, g, rate, decay):
        results = adam_update(old[0][part], g * factor, old[1][part], old[2][part], rate, decay)
        for ref, result in zip(new, results):
            ref[part] = result

    for j in range(3):
        update((wq, mq, sq), (wq_n, mq_n, sq_n), (j,), total[j], rates[0], weight_decay)
    update((wo, mo, so), (wo_n, mo_n, so_n), (slice(None),), total[3], rates[1], weight_decay)
    for c in range(4):
        part = (slice(None), slice(c * 256, c * 256 + 256))
        update((w1, m1, s1), (w1_n, m1_n, s1_n), part, total[4 + c], rates[2], weight_decay)
        update((w2, m2, s2), (w2_n, m2_n, s2_n), part, total[8 + c], rates[3], weight_decay)
    in_grad[y] = in_own[...]
    in_grad[1 - y] = in_other[...].astype(f32)
    update((vec, mv, sv), (v_n, mv_n, sv_n), (slice(None),), g_vec, vector_rate, 0.0)
    columns = pl.ds(pl.multiple_of(mp * 256, 256), 256)
    pooled[pl.ds(y, 1), :] = pools[0:1, columns]
    pooled[pl.ds(1 - y, 1), :] = pools[1:2, columns]


def finish(tokens_all, count, results, weights, moments):
    in_own, in_other, total, vec_sum, pools, squares = results
    out_shape = [
        jax.ShapeDtypeStruct((2, 256), f32),
        jax.ShapeDtypeStruct((2,) + in_own.shape, f32),
        jax.ShapeDtypeStruct((1, 1), f32),
    ]
    for w in weights:
        out_shape += [jax.ShapeDtypeStruct(w.shape, f32)] * 3
    args = (total, vec_sum, pools, squares, in_own, in_other) + weights + moments
    rows = total.shape[1]
    steps = min(4, rows // 8)

    def cut(array):
        shape = array.shape
        lead = (0,) * (len(shape) - 2)
        block = shape[:-2] + (shape[-2] // steps, shape[-1])
        return pl.BlockSpec(block, lambda i: lead + (i, 0))

    def whole(array):
        zeros = (0,) * len(array.shape)
        return pl.BlockSpec(array.shape, lambda i: zeros)

    vectors = 4
    in_specs = [cut(total)] + [whole(a) for a in args[1:4]] + [cut(a) for a in args[4:6]]
    in_specs += [cut(w) for w in weights[:vectors]] + [whole(weights[vectors])]
    in_specs += [cut(m) for m in moments[: 2 * vectors]] + [whole(m) for m in moments[2 * vectors :]]
    out_specs = [whole(out_shape[0]), cut(out_shape[1]), whole(out_shape[2])]
    out_specs += [cut(o) for o in out_shape[3 : 3 + 3 * vectors]]
    out_specs += [whole(o) for o in out_shape[3 + 3 * vectors :]]
    return pl.pallas_call(
        partial(finish_kernel, count, tokens_all),
        grid=(steps,),
        out_shape=out_shape,
        in_specs=in_specs,
        out_specs=out_specs,
        compiler_params=pltpu.CompilerParams(vmem_limit_bytes=60 * 2**20),
        name="finish",
    )(*args)


def local(
    tokens, out_cot, cls_offset, w_qkv, w_out, w_one, w_two, vectors,
    m_qkv, v_qkv, m_out, v_out, m_one, v_one, m_two, v_two, m_vec, v_vec,
):
    length = tokens.shape[1] * lax.axis_size("mp")
    tokens_all = tokens.shape[0] * length * lax.axis_size("dp")
    weights = (w_qkv.swapaxes(0, 1), w_out, w_one, w_two, vectors)
    *saved, r1, small = forward(tokens, out_cot, cls_offset, *weights)
    results = backward(saved, r1, small, vectors)
    pooled, input_grad, grad_norm, *updated = finish(
        tokens_all,
        4 * D * D + 2 * D * FF,
        results,
        weights,
        (m_qkv.swapaxes(0, 1), v_qkv.swapaxes(0, 1), m_out, v_out, m_one, v_one, m_two, v_two, m_vec, v_vec),
    )
    updated[:3] = [u.swapaxes(0, 1) for u in updated[:3]]
    return (pooled, input_grad, grad_norm.reshape(()), *updated)


def solution(mesh):
    rows, wide, flat, whole = P("dp", "mp", None), P("dp", None, "mp"), P("dp", "mp"), P()
    return jax.shard_map(
        local,
        mesh=mesh,
        in_specs=(rows, rows, P("dp", None), wide, flat, flat, flat, whole)
        + (wide, wide)
        + (flat,) * 6
        + (whole, whole),
        out_specs=(flat, rows, whole) + (wide,) * 3 + (flat,) * 9 + (whole,) * 3,
        check_vma=False,
    )
```
